256 devices in a mesh: batch: 128 (over z, x, y_hi, core), mp: 2 (over y_lo).
Axes of the slice: x: 4, y: 4 (y_hi: 2, y_lo: 2; y = y_hi * 2 + y_lo), z: 8, core: 2. Of those that a mesh axis runs over, the one named last changes fastest.
Arguments:
- patches: bfloat16 [256, 729, 1152], P('batch', None, 'mp'), may hold values from -6 to 6
- image_qkv: bfloat16 [1152, 3, 1152], P('batch', None, 'mp'), may hold values from -6 to 6
- image_out: bfloat16 [1152, 1152], P('mp', 'batch'), may hold values from -0.1875 to 0.1875
- captions: bfloat16 [256, 64, 1152], P('batch', None, 'mp'), may hold values from -6 to 6
- text_qkv: bfloat16 [1152, 3, 1152], P(None, None, 'mp'), may hold values from -6 to 6
- text_out: bfloat16 [1152, 1152], P('mp'), may hold values from -0.1875 to 0.1875
Outputs:
- image_hidden: bfloat16 [256, 729, 1152], P('batch', None, 'mp')
- image_grad: float32 [256, 1152], P('batch', 'mp')
- text_grad: float32 [256, 1152], P('batch', 'mp')
The draws below stay inside these ranges and needn't reach their ends.
All inputs are finite; a program needn't handle non-finite values.
Results may differ from the reference program's by a relative error of at most 0.013.
Values may be sent and summed in bfloat16 or wider, within the bound.
No kernel may reach another device: no remote copies, remote signals or barrier semaphores. Data moves between devices by JAX's collectives and lax.ppermute only.
A program may use at most 128 MiB of HBM per device.

```python
import math
import jax
import jax.numpy as jnp
from jax import lax

D = 1152
HEADS = 16
PATCHES = 729
TEXT_LEN = 64
HEAD_DIM = 72
IMAGES = 256


def draw_patches(key, part):
    key = jax.random.fold_in(key, 11)
    return jax.random.truncated_normal(key, -5.0, 5.0, (IMAGES, PATCHES, D), jnp.float32).astype(jnp.bfloat16)


def draw_captions(key, part):
    key = jax.random.fold_in(key, 13)
    return jax.random.truncated_normal(key, -5.0, 5.0, (IMAGES, TEXT_LEN, D), jnp.float32).astype(jnp.bfloat16)


def draw_image_qkv(key, part):
    key = jax.random.fold_in(key, 21)
    matrix = jax.random.truncated_normal(key, -5.0, 5.0, (D, 3, D), jnp.float32) / math.sqrt(D)
    return matrix.astype(jnp.bfloat16)


def draw_text_qkv(key, part):
    key = jax.random.fold_in(key, 23)
    matrix = jax.random.truncated_normal(key, -5.0, 5.0, (D, 3, D), jnp.float32) / math.sqrt(D)
    return matrix.astype(jnp.bfloat16)


def block_scale(key, shape, pieces, least, high):
    loudness = 1.0
    for dim, parts in pieces:
        steps = jax.random.uniform(jax.random.fold_in(jax.random.fold_in(key, 6), dim), (parts,), jnp.float32, least / len(pieces), high / len(pieces))
        loudness = loudness * jnp.repeat(jnp.exp(steps), shape[dim] // parts).reshape((-1,) + (1,) * (len(shape) - 1 - dim))
    return loudness


def bell_draw(key, extent, width, bound, cuts=(), kind=jnp.bfloat16):
    drawn = jax.random.normal(key, extent, jnp.float32) * width
    if len(cuts) > 0:
        drawn = block_scale(key, extent, cuts, -0.22, 0.18) * drawn
    return jnp.clip(drawn, min=-bound, max=bound).astype(kind)


def setup_inputs(seed: int = 0) -> dict:
    seeds = jax.random.split(jax.random.key(seed), 7)
    return {
        "patches": draw_patches(jax.random.fold_in(seeds[6], 71), 0),
        "image_qkv": draw_image_qkv(jax.random.fold_in(seeds[6], 71), 0),
        "image_out": bell_draw(seeds[2], (D, D), D ** -0.5, 0.1875, ((0, 2), (1, 128))),
        "captions": draw_captions(jax.random.fold_in(seeds[6], 71), 0),
        "text_qkv": draw_text_qkv(jax.random.fold_in(seeds[6], 71), 0),
        "text_out": bell_draw(seeds[5], (D, D), D ** -0.5, 0.1875, ((0, 2),)),
    }


logit_scale = 10.0
logit_shift = -1.0

def norm_rows(values):
    center = lax.optimization_barrier(jnp.mean(values, axis=-1, keepdims=True))
    centred = values - center
    spread = lax.optimization_barrier(jnp.mean(centred * centred, axis=-1, keepdims=True))
    return centred * lax.rsqrt(spread + 1e-06)

def tower_layer(inputs, w_qkv, w_out):
    count = inputs.shape[0]
    normed = norm_rows(inputs.astype(jnp.float32)).astype(jnp.bfloat16)
    projected = jnp.dot(normed, w_qkv.reshape(D, 3 * D), preferred_element_type=jnp.float32)
    projected = projected.astype(jnp.bfloat16).reshape(count, 3, HEADS, HEAD_DIM)
    query_vectors = projected[:, 0].astype(jnp.float32)
    key_vectors = projected[:, 1].astype(jnp.float32)
    value_vectors = projected[:, 2].astype(jnp.float32)
    logits = jnp.einsum('qhd,khd->hqk', query_vectors, key_vectors) * HEAD_DIM ** (-0.5)
    attention_weight = jax.nn.softmax(logits, axis=-1).astype(jnp.bfloat16)
    attended = jnp.einsum('hqk,khd->qhd', attention_weight.astype(jnp.float32), value_vectors)
    attended = attended.astype(jnp.bfloat16).reshape(count, D)
    return inputs.astype(jnp.float32) + jnp.dot(attended, w_out, preferred_element_type=jnp.float32)

def embed_rows(features):
    total = lax.optimization_barrier(jnp.sum(features * features, axis=-1, keepdims=True))
    return (features * lax.rsqrt(total + 1e-06)).astype(jnp.bfloat16)

def reference(patches, image_qkv, image_out, captions, text_qkv, text_out):

    def image_step(single):
        layer_out = tower_layer(single, image_qkv, image_out)
        return (layer_out.astype(jnp.bfloat16), lax.optimization_barrier(jnp.mean(layer_out, axis=0)))

    def text_step(single):
        return tower_layer(single, text_qkv, text_out)[-1]
    image_hidden, pooled = lax.map(image_step, patches)
    text_last = lax.map(text_step, captions)
    image_embed = embed_rows(pooled)
    text_embed = embed_rows(text_last)
    logits = logit_scale * jnp.dot(image_embed, text_embed.T, preferred_element_type=jnp.float32) + logit_shift
    labels = jnp.where(jnp.eye(IMAGES, dtype=bool), 1.0, -1.0).astype(jnp.float32)
    pair_grad = (logit_scale * labels * (jax.nn.sigmoid(labels * logits) - 1.0)).astype(jnp.bfloat16)
    image_grad = jnp.dot(pair_grad, text_embed, preferred_element_type=jnp.float32)
    text_grad = jnp.dot(pair_grad.T, image_embed, preferred_element_type=jnp.float32)
    return (image_hidden, image_grad, text_grad)
```

```python
import functools
import math

import jax
import jax.numpy as jnp
import numpy as np
from jax import lax
from jax.experimental import pallas as pl
from jax.experimental.pallas import tpu as pltpu
from jax.sharding import Mesh, PartitionSpec as P

D = 1152
HALF = 576
HEAD_DIM = 72
SEQ = 729
ROWS = 768
QROWS = 736
QBLOCK = 368
TEXT = 64
COLS = 2304
QKV = 1792
WO_AT = 1664
WIN = 640
SPLIT = (80, 64)
PIECE = 144

f32 = jnp.float32
bf16 = jnp.bfloat16
NT = (((1,), (1,)), ((), ()))
TN = (((0,), (0,)), ((), ()))
VMEM_LIMIT = 48 * 1024 * 1024


def dot(a, b, dims=(((1,), (0,)), ((), ()))):
    return lax.dot_general(a, b, dims, preferred_element_type=f32)


def call(body, outs, args, specs=None, out_specs=None, scratch=(), flops=0, bytes_accessed=0, name=None, aliases=None):
    whole = pl.BlockSpec(memory_space=pltpu.VMEM)
    return pl.pallas_call(
        body,
        out_shape=outs,
        in_specs=specs if specs is not None else [whole] * len(args),
        out_specs=out_specs if out_specs is not None else jax.tree.map(lambda _: whole, outs),
        scratch_shapes=list(scratch),
        compiler_params=pltpu.CompilerParams(vmem_limit_bytes=VMEM_LIMIT),
        cost_estimate=pl.CostEstimate(flops=int(flops), bytes_accessed=int(bytes_accessed), transcendentals=0),
        input_output_aliases=aliases or {},
        name=name,
    )(*args)


def shape(dims, kind):
    return jax.ShapeDtypeStruct(dims, kind)


VM = pl.BlockSpec(memory_space=pltpu.VMEM)
SM = pl.BlockSpec(memory_space=pltpu.SMEM)
ANY = pl.BlockSpec(memory_space=pl.ANY)


def shift(value, axis, size, step):
    return lax.ppermute(value, axis, [((i + step) % size, i) for i in range(size)])


def norm_kernel(idx_ref, xo_ref, xr_ref, out_ref, mean_ref, pad_ref):
    xo = xo_ref[0].astype(f32)
    xr = xr_ref[0].astype(f32)
    center = (jnp.sum(xo, axis=0, keepdims=True) + jnp.sum(xr, axis=0, keepdims=True)) * (1.0 / D)
    co = xo - center
    cr = xr - center
    spread = (jnp.sum(co * co, axis=0, keepdims=True) + jnp.sum(cr * cr, axis=0, keepdims=True)) * (1.0 / D)
    scale = lax.rsqrt(spread + 1e-06)
    pad_ref[:, pl.ds(640, 128)] = jnp.zeros((D, 128), bf16)
    pad_ref[pl.ds(0, HALF), pl.ds(0, SEQ)] = (co * scale).astype(bf16)
    pad_ref[pl.ds(HALF, HALF), pl.ds(0, SEQ)] = (cr * scale).astype(bf16)
    rows = lax.broadcasted_iota(jnp.int32, (D, D), 0)
    pick = (rows == idx_ref[...]).astype(f32).astype(bf16)
    for block in range(ROWS // 128):
        part = pad_ref[:, pl.ds(128 * block, 128)]
        out_ref[pl.ds(128 * block, 128), :] = dot(part, pick, TN).astype(bf16)
    ones = jnp.ones((8, SEQ), bf16)
    mean_ref[:, pl.ds(0, HALF)] = dot(ones, xo_ref[0], NT) * (1.0 / SEQ)
    mean_ref[:, pl.ds(HALF + 64, HALF)] = dot(ones, xr_ref[0], NT) * (1.0 / SEQ)


def norm_patches(idx, own, other, sample):
    sample_spec = pl.BlockSpec((1, HALF, SEQ), lambda i: (sample, 0, 0))
    other_spec = pl.BlockSpec((1, HALF, SEQ), lambda i: (0, 0, 0))
    return pl.pallas_call(
        norm_kernel,
        grid=(1,),
        out_shape=(shape((ROWS, D), bf16), shape((8, 1280), f32)),
        in_specs=[pl.BlockSpec((1, D), lambda i: (0, 0)), sample_spec, other_spec],
        out_specs=(pl.BlockSpec((ROWS, D), lambda i: (0, 0)), pl.BlockSpec((8, 1280), lambda i: (0, 0))),
        scratch_shapes=[pltpu.VMEM((D, ROWS), bf16)],
        compiler_params=pltpu.CompilerParams(vmem_limit_bytes=VMEM_LIMIT),
        cost_estimate=pl.CostEstimate(flops=2 * ROWS * D * D, bytes_accessed=4 * ROWS * D, transcendentals=0),
        name="norm_patches",
    )(idx, own, other)


def order_kernel(idx_ref, *refs):
    pieces, (out_ref, mixed_ref, sems) = refs[:8], refs[8:]
    copies = []
    row = 0
    for n, piece in enumerate(pieces):
        count = piece.shape[0]
        copies.append(
            pltpu.make_async_copy(
                piece.at[:, pl.ds(WO_AT, WIN)], mixed_ref.at[pl.ds(row, count), :], sems.at[n]
            )
        )
        row += count
    for copy in copies:
        copy.start()
    for copy in copies:
        copy.wait()
    for block in range(4):
        rows = 288 * block + lax.broadcasted_iota(jnp.int32, (288, D), 0)
        pick = (rows == idx_ref[...]).astype(f32).astype(bf16)
        out_ref[pl.ds(288 * block, 288), :] = dot(pick, mixed_ref[...]).astype(bf16)


def order_out(idx, pieces):
    return call(
        order_kernel,
        shape((D, WIN), bf16),
        [idx] + pieces,
        specs=[VM] + [ANY] * 8,
        scratch=[pltpu.VMEM((D, WIN), bf16), pltpu.SemaphoreType.DMA((8,))],
        flops=2 * D * D * WIN,
        bytes_accessed=4 * D * WIN,
        name="order_out",
    )


def attend_kernel(x_ref, *refs):
    pieces, (att_ref, sum_ref, w_ref, qkv_ref, sems) = refs[:8], refs[8:]
    copies = []
    row = 0
    for n, piece in enumerate(pieces):
        count = piece.shape[0]
        copies.append(
            pltpu.make_async_copy(piece.at[:, pl.ds(0, QKV)], w_ref.at[pl.ds(row, count), :], sems.at[n])
        )
        row += count
    for copy in copies:
        copy.start()
    att_ref[...] = jnp.zeros_like(att_ref)
    for copy in copies:
        copy.wait()

    q_scale = math.log2(math.e) * HEAD_DIM ** (-0.5)

    def project(n, carry):
        at = pl.multiple_of(n * 256, 256)
        lane = at + lax.broadcasted_iota(jnp.int32, (1, 256), 1)
        scale = jnp.where(lane < HALF, q_scale, 1.0).astype(f32)
        qkv_ref[:, pl.ds(at, 256)] = (dot(x_ref[...], w_ref[:, pl.ds(at, 256)]) * scale).astype(bf16)
        return carry

    lax.fori_loop(0, QKV // 256, project, 0)

    lane = lax.broadcasted_iota(jnp.int32, (1, 256), 1)

    def between(low, high):
        return ((lane >= low) & (lane < high)).astype(f32)

    last = (lane == 255).astype(f32)
    key_row = lax.broadcasted_iota(jnp.int32, (ROWS, 1), 0)
    key_bias = jnp.where(key_row >= SEQ, -1e30, 0.0).astype(f32) * last

    def pair(step, carry):
        p = step // 2
        at = pl.multiple_of(p * 128, 128)
        row = pl.multiple_of((step % 2) * QBLOCK, 16)
        q_at = 16 * p
        v_at = 64 + 16 * p
        q_win = qkv_ref[pl.ds(row, QBLOCK), pl.ds(at, 256)]
        v_win = qkv_ref[:, pl.ds(512 + at, 256)]
        k_win = qkv_ref[:, pl.ds(D + at, 256)] * (1.0 - last).astype(bf16) + key_bias.astype(bf16)
        total = None
        for h in range(2):
            low = q_at + HEAD_DIM * h
            q = q_win * between(low, low + HEAD_DIM).astype(bf16) + last.astype(bf16)
            s = dot(q, k_win, NT)
            weight = jnp.exp2(s - jnp.max(s, axis=1, keepdims=True)).astype(bf16)
            low = v_at + HEAD_DIM * h
            v = v_win * between(low, low + HEAD_DIM).astype(bf16) + (lane == h).astype(f32).astype(bf16)
            o = dot(weight, v)
            total = o if total is None else total + o
        inverse = jnp.where(lane < v_at + HEAD_DIM, 1.0 / total[:, 0:1], 1.0 / total[:, 1:2])
        mixed = (total * inverse * between(v_at, v_at + 2 * HEAD_DIM)).astype(bf16)
        att_ref[pl.ds(row, QBLOCK), pl.ds(at, 256)] = att_ref[pl.ds(row, QBLOCK), pl.ds(at, 256)] + mixed
        return carry

    lax.fori_loop(0, 8, pair, 0)
    valid = (lax.broadcasted_iota(jnp.int32, (8, QROWS), 1) < SEQ).astype(f32).astype(bf16)
    sum_ref[...] = dot(valid, att_ref[...])


def attend(x, pieces):
    return call(
        attend_kernel,
        (shape((QROWS, WIN), bf16), shape((8, WIN), f32)),
        [x] + pieces,
        specs=[VM] + [ANY] * 8,
        scratch=[
            pltpu.VMEM((D, QKV), bf16),
            pltpu.VMEM((ROWS, QKV), bf16),
            pltpu.SemaphoreType.DMA((8,)),
        ],
        flops=2 * ROWS * D * QKV + 8 * 4 * ROWS * ROWS * 256,
        bytes_accessed=2 * (D * QKV + ROWS * D + QROWS * WIN),
        name="attend",
    )


def project_kernel(m_ref, att_ref, w_ref, x_ref, own_ref, send_ref):
    m = m_ref[0]
    mine = w_ref[pl.ds(pl.multiple_of(m * HALF, HALF), HALF), :]
    theirs = w_ref[pl.ds(pl.multiple_of((1 - m) * HALF, HALF), HALF), :]
    send_ref[...] = dot(theirs, att_ref[...], NT)[:, :SEQ].astype(bf16)
    own_ref[...] = dot(mine, att_ref[...], NT)[:, :SEQ] + x_ref[0].astype(f32)


def project(m, att, w, x, sample):
    full = lambda *dims: pl.BlockSpec(dims, lambda i: (0,) * len(dims))
    return pl.pallas_call(
        project_kernel,
        grid=(1,),
        out_shape=(shape((HALF, SEQ), f32), shape((HALF, SEQ), bf16)),
        in_specs=[SM, full(QROWS, WIN), full(D, WIN), pl.BlockSpec((1, HALF, SEQ), lambda i: (sample, 0, 0))],
        out_specs=(full(HALF, SEQ), full(HALF, SEQ)),
        compiler_params=pltpu.CompilerParams(vmem_limit_bytes=VMEM_LIMIT),
        cost_estimate=pl.CostEstimate(
            flops=2 * D * WIN * QROWS, bytes_accessed=2 * (QROWS * WIN + D * WIN) + 8 * HALF * SEQ, transcendentals=0
        ),
        name="project",
    )(m, att, w, x)


def finish_kernel(own_ref, other_ref, *refs):
    out_ref = refs[-1]
    out_ref[0] = (own_ref[...] + other_ref[...].astype(f32)).astype(bf16)


def finish(own, other, sample, before=None):
    rows = 288
    spec = pl.BlockSpec((rows, SEQ), lambda i: (i, 0))
    args = [own, other] + ([before] if before is not None else [])
    return pl.pallas_call(
        finish_kernel,
        grid=(HALF // rows,),
        out_shape=shape((2, HALF, SEQ), bf16),
        in_specs=[spec, spec] + ([ANY] if before is not None else []),
        out_specs=pl.BlockSpec((1, rows, SEQ), lambda i: (sample, i, 0)),
        input_output_aliases={2: 0} if before is not None else {},
        compiler_params=pltpu.CompilerParams(vmem_limit_bytes=VMEM_LIMIT),
        cost_estimate=pl.CostEstimate(flops=HALF * SEQ, bytes_accessed=8 * HALF * SEQ, transcendentals=0),
        name="finish",
    )(*args)


def text_kernel(m_ref, co_ref, cr_ref, w_ref, wo_ref, part_ref, last_ref, x_ref):
    m = m_ref[0]
    own = co_ref[...].astype(f32)
    other = cr_ref[...].astype(f32)
    first = jnp.where(m == 0, own, other)
    second = jnp.where(m == 0, other, own)
    x_ref[:, pl.ds(0, HALF)] = first
    x_ref[:, pl.ds(HALF, HALF)] = second
    x = x_ref[...]
    center = jnp.sum(x, axis=1, keepdims=True) * (1.0 / D)
    centred = x - center
    spread = jnp.sum(centred * centred, axis=1, keepdims=True) * (1.0 / D)
    normed = (centred * lax.rsqrt(spread + 1e-06)).astype(bf16)
    q = dot(normed, w_ref[0], NT).astype(bf16).astype(f32)
    k = dot(normed, w_ref[1], NT).astype(bf16)
    v = dot(normed, w_ref[2], NT).astype(bf16)
    row = lax.broadcasted_iota(jnp.int32, (16, HALF), 0)
    lane = lax.broadcasted_iota(jnp.int32, (16, HALF), 1)
    low = (row % 8) * HEAD_DIM
    of_head = (lane >= low) & (lane < low + HEAD_DIM)
    q_last = jnp.where(row < 8, q[TEXT - 1 : TEXT], q[2 * TEXT - 1 : 2 * TEXT])
    q_head = jnp.where(of_head, q_last, 0.0).astype(bf16)
    s = dot(q_head, k, NT) * HEAD_DIM ** (-0.5)
    key = lax.broadcasted_iota(jnp.int32, (16, 2 * TEXT), 1)
    of = lax.broadcasted_iota(jnp.int32, (16, 2 * TEXT), 0)
    s = jnp.where((key < TEXT) == (of < 8), s, -1e30)
    e = jnp.exp(s - jnp.max(s, axis=1, keepdims=True))
    weight = (e / jnp.sum(e, axis=1, keepdims=True)).astype(bf16)
    o = jnp.where(of_head, dot(weight, v), 0.0)
    a = jnp.sum(jnp.where(row < 8, o, 0.0), axis=0, keepdims=True)
    b = jnp.sum(jnp.where(row < 8, 0.0, o), axis=0, keepdims=True)
    att = jnp.where(lax.broadcasted_iota(jnp.int32, (8, HALF), 0) == 0, a, b).astype(bf16)
    part_ref[...] = dot(att, wo_ref[...])
    at = lax.broadcasted_iota(jnp.int32, (8, D), 0)
    last_ref[...] = jnp.where(at == 0, x[TEXT - 1 : TEXT], x[2 * TEXT - 1 : 2 * TEXT])


def text_tower(m, own, other, w, wo):
    return call(
        text_kernel,
        (shape((8, D), f32), shape((8, D), f32)),
        [m, own, other, w, wo],
        specs=[SM, VM, VM, VM, VM],
        scratch=[pltpu.VMEM((2 * TEXT, D), f32)],
        flops=2 * 128 * D * 3 * HALF,
        bytes_accessed=2 * (3 * HALF * D + HALF * D),
        name="text_tower",
    )


def embed_rows(features, out_ref):
    total = jnp.sum(features * features, axis=1, keepdims=True)
    embedded = (features * lax.rsqrt(total + 1e-06)).astype(bf16)
    out_ref[:, pl.ds(0, D)] = embedded[0:1]
    out_ref[:, pl.ds(D, D)] = embedded[1:2]


def embed_kernel(base_ref, mine_ref, other_ref, out_ref):
    embed_rows(base_ref[...] + (mine_ref[...] + other_ref[...]), out_ref)


def embed(base, mine, other):
    return call(embed_kernel, shape((1, COLS), bf16), [base, mine, other], bytes_accessed=100000, name="embed")


def pool_kernel(m_ref, a_ref, b_ref, ma_ref, mb_ref, w_ref, part_ref, mean_ref):
    row = lax.broadcasted_iota(jnp.int32, (8, WIN), 0)
    sums = jnp.where(row == 0, a_ref[...], b_ref[...]) * (1.0 / SEQ)
    high = sums.astype(bf16)
    rest = sums - high.astype(f32)
    mid = rest.astype(bf16)
    low = (rest - mid.astype(f32)).astype(bf16)
    w = w_ref[...]
    part_ref[...] = dot(high, w, NT) + (dot(mid, w, NT) + dot(low, w, NT))
    m = m_ref[0]
    at = lax.broadcasted_iota(jnp.int32, (8, HALF), 0)
    own = jnp.where(at == 0, ma_ref[:, pl.ds(0, HALF)], mb_ref[:, pl.ds(0, HALF)])
    other = jnp.where(at == 0, ma_ref[:, pl.ds(HALF + 64, HALF)], mb_ref[:, pl.ds(HALF + 64, HALF)])
    mean_ref[:, pl.ds(0, HALF)] = jnp.where(m == 0, own, other)
    mean_ref[:, pl.ds(HALF, HALF)] = jnp.where(m == 0, other, own)


def pool(m, sum_a, sum_b, mean_a, mean_b, w):
    return call(
        pool_kernel,
        (shape((8, D), f32), shape((8, D), f32)),
        [m, sum_a, sum_b, mean_a, mean_b, w],
        specs=[SM] + [VM] * 5,
        flops=3 * 2 * 8 * WIN * D,
        bytes_accessed=2 * D * WIN,
        name="pool",
    )


def pair_kernel(m_ref, own_ref, near_ref, far_ref, out_ref):
    row = lax.broadcasted_iota(jnp.int32, (8, D), 0)
    own = own_ref[...].astype(f32)
    own = jnp.where(row == 0, own[:, 0:D], own[:, D:]).astype(bf16)
    count = near_ref.shape[0]
    at_row = lax.broadcasted_iota(jnp.int32, (8, count), 0)
    at_col = lax.broadcasted_iota(jnp.int32, (8, count), 1)
    grad = None
    for ref in (near_ref, far_ref):
        for which in range(2):
            each = ref[:, pl.ds(D * which, D)]
            logit = 10.0 * dot(own, each, NT) - 1.0
            same = (at_row == which) & (at_col == 0) if ref is near_ref else (at_row < 0)
            label = jnp.where(same, 1.0, -1.0)
            weight = (-10.0 * label / (1.0 + jnp.exp(label * logit))).astype(bf16)
            term = dot(weight, each)
            grad = term if grad is None else grad + term
    out_ref[...] = jnp.where(m_ref[0] == 0, grad[0:2, 0:HALF], grad[0:2, HALF:])


def pair_grad(m, own, near, far):
    return call(
        pair_kernel,
        shape((2, HALF), f32),
        [m, own, near, far],
        specs=[SM, VM, VM, VM],
        flops=2 * 2 * 8 * 256 * D,
        bytes_accessed=2 * 256 * D,
        name="pair_grad",
    )


def gather_embeds(embedded):
    both = jnp.concatenate([embedded, shift(embedded, "w", 2, 1)], axis=0)
    along_z = jnp.concatenate([both] + [shift(both, "z", 8, k) for k in range(1, 8)], axis=0)
    along_x = jnp.concatenate([along_z] + [shift(along_z, "x", 4, k) for k in range(1, 4)], axis=0)
    return along_x, shift(along_x, "c", 2, 1)


def gather_weights(image_qkv, image_out):
    slab = jnp.concatenate(
        [image_qkv[:, 0:1], image_qkv[:, 2:3], image_qkv[:, 1:2], jnp.transpose(image_out)[:, None, :]], axis=1
    )
    both = jnp.concatenate([slab, shift(slab, "w", 2, 1)], axis=0)
    parts = [both] + [shift(both, "z", 8, k) for k in range(1, 8)]
    piece = jnp.concatenate(parts, axis=0).reshape(PIECE, COLS)
    cut = SPLIT[0]
    a0, b0 = piece[:cut], piece[cut:]
    a1, b1 = shift(a0, "x", 4, 1), shift(b0, "x", 4, 1)
    a3, b3 = shift(a0, "x", 4, 3), shift(b0, "x", 4, 3)
    a2 = shift(a3, "x", 4, 3)
    b2 = shift(b1, "x", 4, 1)
    near = [a0, b0, a1, b1, a2, b2, a3, b3]
    near_rows = [jnp.concatenate([near[i], near[i + 1]], axis=0) for i in (0, 2, 4, 6)]
    far_rows = [shift(block, "c", 2, 1) for block in near_rows]
    return near_rows + far_rows


def row_order(z, x, w, c):
    at = np.arange(D)
    r, rest = at % 9, at // 9
    wr, rest = rest % 2, rest // 2
    zr, rest = rest % 8, rest // 8
    xr, cr = rest % 4, rest // 4
    device = (((z + zr) % 8 * 4 + (x + xr) % 4) * 2 + (w + wr) % 2) * 2 + (c + cr) % 2
    return (device * 9 + r).astype(jnp.int32).reshape(1, D)


def on_device(patches, image_qkv, image_out, captions, text_qkv, text_out):
    z, x, w, c, m = (lax.axis_index(a) for a in ("z", "x", "w", "c", "m"))
    m_arr = jnp.reshape(m, (1,)).astype(jnp.int32)
    order = row_order(z, x, w, c)
    norm_order = (order + HALF * m) % D

    own = jnp.transpose(patches, (0, 2, 1))
    pieces = gather_weights(image_qkv, image_out)
    captions2 = captions.reshape(2 * TEXT, HALF)
    captions_other = shift(captions2, "m", 2, 1)
    other = [shift(own[s : s + 1], "m", 2, 1) for s in range(2)]

    part, last = text_tower(m_arr, captions2, captions_other, jnp.transpose(text_qkv, (1, 2, 0)), text_out)
    text_embed = embed(last, part, shift(part, "m", 2, 1))
    text_near, text_far = gather_embeds(text_embed)

    normed, means = zip(*[norm_patches(norm_order, own, other[s], s) for s in range(2)])
    wo = order_out(order, pieces)

    att0, sum0 = attend(normed[0], pieces)
    own0, send0 = project(m_arr, att0, wo, own, 0)
    other0 = shift(send0, "m", 2, 1)
    att1, sum1 = attend(normed[1], pieces)
    pool_part, pool_mean = pool(m_arr, sum0, sum1, means[0], means[1], wo)
    image_embed = embed(pool_mean, pool_part, shift(pool_part, "m", 2, 1))
    own1, send1 = project(m_arr, att1, wo, own, 1)
    other1 = shift(send1, "m", 2, 1)
    image_near, image_far = gather_embeds(image_embed)

    image_grad = pair_grad(m_arr, image_embed, text_near, text_far)
    hidden = finish(own0, other0, 0)
    hidden = finish(own1, other1, 1, hidden)
    text_grad = pair_grad(m_arr, text_embed, image_near, image_far)
    return jnp.transpose(hidden, (0, 2, 1)), image_grad, text_grad


def solution(mesh):
    split = Mesh(mesh.devices.reshape(8, 4, 2, 2, 2), ("z", "x", "w", "c", "m"))
    batch = ("z", "x", "w", "c")
    return jax.shard_map(
        on_device,
        mesh=split,
        in_specs=(
            P(batch, None, "m"),
            P(batch, None, "m"),
            P("m", batch),
            P(batch, None, "m"),
            P(None, None, "m"),
            P("m", None),
        ),
        out_specs=(P(batch, None, "m"), P(batch, "m"), P(batch, "m")),
        check_vma=False,
    )
```

```python
import functools
import math

import jax
import jax.numpy as jnp
import numpy as np
from jax import lax
from jax.experimental import pallas as pl
from jax.experimental.pallas import tpu as pltpu
from jax.sharding import Mesh, PartitionSpec as P

D = 1152
HALF = 576
HEAD_DIM = 72
SEQ = 729
ROWS = 768
QROWS = 736
QBLOCK = 368
TEXT = 64
COLS = 2304
QKV = 1792
WO_AT = 1664
WIN = 640
SPLIT = (80, 64)
PIECE = 144
MESSAGE = 4 * D

f32 = jnp.float32
bf16 = jnp.bfloat16
NT = (((1,), (1,)), ((), ()))
TN = (((0,), (0,)), ((), ()))
VMEM_LIMIT = 32 * 1024 * 1024


def dot(a, b, dims=(((1,), (0,)), ((), ()))):
    return lax.dot_general(a, b, dims, preferred_element_type=f32)


def call(body, outs, args, specs=None, out_specs=None, scratch=(), flops=0, bytes_accessed=0, name=None, aliases=None):
    whole = pl.BlockSpec(memory_space=pltpu.VMEM)
    return pl.pallas_call(
        body,
        out_shape=outs,
        in_specs=specs if specs is not None else [whole] * len(args),
        out_specs=out_specs if out_specs is not None else jax.tree.map(lambda _: whole, outs),
        scratch_shapes=list(scratch),
        compiler_params=pltpu.CompilerParams(vmem_limit_bytes=VMEM_LIMIT),
        cost_estimate=pl.CostEstimate(flops=int(flops), bytes_accessed=int(bytes_accessed), transcendentals=0),
        input_output_aliases=aliases or {},
        name=name,
    )(*args)


def shape(dims, kind):
    return jax.ShapeDtypeStruct(dims, kind)


VM = pl.BlockSpec(memory_space=pltpu.VMEM)
SM = pl.BlockSpec(memory_space=pltpu.SMEM)
ANY = pl.BlockSpec(memory_space=pl.ANY)


def shift(value, axis, size, step):
    return lax.ppermute(value, axis, [((i + step) % size, i) for i in range(size)])


def spread(value, axes, size):
    return lax.all_to_all(jnp.broadcast_to(value[None], (size,) + value.shape), axes, 0, 0)


def after(value, *others):
    return lax.optimization_barrier((value,) + others)[0]


def norm_kernel(idx_ref, xo_ref, xr_ref, out_ref, mean_ref, pad_ref, turned_ref):
    xo = xo_ref[0].astype(f32)
    xr = xr_ref[0].astype(f32)
    center = (jnp.sum(xo, axis=0, keepdims=True) + jnp.sum(xr, axis=0, keepdims=True)) * (1.0 / D)
    co = xo - center
    cr = xr - center
    spread = (jnp.sum(co * co, axis=0, keepdims=True) + jnp.sum(cr * cr, axis=0, keepdims=True)) * (1.0 / D)
    scale = lax.rsqrt(spread + 1e-06)
    pad_ref[:, pl.ds(640, 128)] = jnp.zeros((D, 128), bf16)
    pad_ref[pl.ds(0, HALF), pl.ds(0, SEQ)] = (co * scale).astype(bf16)
    pad_ref[pl.ds(HALF, HALF), pl.ds(0, SEQ)] = (cr * scale).astype(bf16)
    turned_ref[...] = jnp.transpose(pad_ref[...])
    for at in range(0, D, 256):
        size = min(256, D - at)
        rows = lax.broadcasted_iota(jnp.int32, (D, size), 0)
        pick = (rows == idx_ref[:, pl.ds(at, size)]).astype(f32).astype(bf16)
        out_ref[:, pl.ds(at, size)] = dot(turned_ref[...], pick).astype(bf16)
    ones = jnp.ones((8, SEQ), bf16)
    mean_ref[:, pl.ds(0, HALF)] = dot(ones, xo_ref[0], NT) * (1.0 / SEQ)
    mean_ref[:, pl.ds(HALF + 64, HALF)] = dot(ones, xr_ref[0], NT) * (1.0 / SEQ)


def norm_patches(idx, own, other, sample):
    sample_spec = pl.BlockSpec((1, HALF, SEQ), lambda i: (sample, 0, 0))
    other_spec = pl.BlockSpec((1, HALF, SEQ), lambda i: (0, 0, 0))
    return pl.pallas_call(
        norm_kernel,
        grid=(1,),
        out_shape=(shape((ROWS, D), bf16), shape((8, 1280), f32)),
        in_specs=[pl.BlockSpec((1, D), lambda i: (0, 0)), sample_spec, other_spec],
        out_specs=(pl.BlockSpec((ROWS, D), lambda i: (0, 0)), pl.BlockSpec((8, 1280), lambda i: (0, 0))),
        scratch_shapes=[pltpu.VMEM((D, ROWS), bf16), pltpu.VMEM((ROWS, D), bf16)],
        compiler_params=pltpu.CompilerParams(vmem_limit_bytes=VMEM_LIMIT),
        cost_estimate=pl.CostEstimate(flops=2 * ROWS * D * D, bytes_accessed=4 * ROWS * D, transcendentals=0),
        name="norm_patches",
    )(idx, own, other)


def order_kernel(idx_ref, *refs):
    pieces, (out_ref, mixed_ref, pick_ref, sems) = refs[:16], refs[16:]
    copies = []
    row = 0
    for n, piece in enumerate(pieces):
        count = piece.shape[0]
        copies.append(
            pltpu.make_async_copy(
                piece.at[:, pl.ds(WO_AT, WIN)], mixed_ref.at[pl.ds(row, count), :], sems.at[n]
            )
        )
        row += count
    for copy in copies:
        copy.start()
    for copy in copies:
        copy.wait()
    rows = lax.broadcasted_iota(jnp.int32, (D, D), 0)
    pick_ref[...] = (rows == idx_ref[...]).astype(f32).astype(bf16)
    for at in range(0, WIN, 256):
        size = min(256, WIN - at)
        out_ref[:, pl.ds(at, size)] = dot(pick_ref[...], mixed_ref[:, pl.ds(at, size)]).astype(bf16)


def order_out(idx, pieces):
    return call(
        order_kernel,
        shape((D, WIN), bf16),
        [idx] + pieces,
        specs=[VM] + [ANY] * 16,
        scratch=[pltpu.VMEM((D, WIN), bf16), pltpu.VMEM((D, D), bf16), pltpu.SemaphoreType.DMA((16,))],
        flops=2 * D * D * WIN,
        bytes_accessed=4 * D * WIN,
        name="order_out",
    )


def attend_kernel(x_ref, *refs):
    pieces, (att_ref, sum_ref, w_ref, qkv_ref, sems) = refs[:16], refs[16:]
    copies = []
    row = 0
    for n, piece in enumerate(pieces):
        count = piece.shape[0]
        copies.append(
            pltpu.make_async_copy(piece.at[:, pl.ds(0, QKV)], w_ref.at[pl.ds(row, count), :], sems.at[n])
        )
        row += count
    for copy in copies:
        copy.start()
    att_ref[...] = jnp.zeros_like(att_ref)
    for copy in copies:
        copy.wait()

    q_scale = math.log2(math.e) * HEAD_DIM ** (-0.5)

    def project(n, carry):
        at = pl.multiple_of(n * 256, 256)
        lane = at + lax.broadcasted_iota(jnp.int32, (1, 256), 1)
        scale = jnp.where(lane < HALF, q_scale, 1.0).astype(f32)
        qkv_ref[:, pl.ds(at, 256)] = (dot(x_ref[...], w_ref[:, pl.ds(at, 256)]) * scale).astype(bf16)
        return carry

    lax.fori_loop(0, QKV // 256, project, 0)

    lane = lax.broadcasted_iota(jnp.int32, (1, 256), 1)

    def between(low, high):
        return ((lane >= low) & (lane < high)).astype(f32)

    last = (lane == 255).astype(f32)
    key_row = lax.broadcasted_iota(jnp.int32, (ROWS, 1), 0)
    key_bias = jnp.where(key_row >= SEQ, -1e30, 0.0).astype(f32) * last

    def pair(p, carry):
        at = pl.multiple_of(p * 128, 128)
        q_at = 16 * p
        v_at = 64 + 16 * p
        k_win = qkv_ref[:, pl.ds(D + at, 256)] * (1.0 - last).astype(bf16) + key_bias.astype(bf16)
        v_win = qkv_ref[:, pl.ds(512 + at, 256)]
        values = []
        for h in range(2):
            low = v_at + HEAD_DIM * h
            ones = (lane == h).astype(f32).astype(bf16)
            values.append(v_win * between(low, low + HEAD_DIM).astype(bf16) + ones)
        units = [(row, h) for row in range(0, QROWS, QBLOCK) for h in range(2)]
        scores, weights, totals = {}, {}, {}

        def score(u):
            row, h = units[u]
            low = q_at + HEAD_DIM * h
            q_win = qkv_ref[pl.ds(row, QBLOCK), pl.ds(at, 256)]
            q = q_win * between(low, low + HEAD_DIM).astype(bf16) + last.astype(bf16)
            scores[u] = dot(q, k_win, NT)

        def weigh(u):
            s = scores.pop(u)
            weights[u] = jnp.exp2((s - jnp.max(s, axis=1, keepdims=True)).astype(bf16))

        def mix(u):
            row, h = units[u]
            totals[u] = dot(weights.pop(u), values[h])

        def store(u):
            row = units[u][0]
            total = totals.pop(u) + totals.pop(u + 1)
            inverse = jnp.where(lane < v_at + HEAD_DIM, 1.0 / total[:, 0:1], 1.0 / total[:, 1:2])
            mixed = (total * inverse * between(v_at, v_at + 2 * HEAD_DIM)).astype(bf16)
            att_ref[pl.ds(row, QBLOCK), pl.ds(at, 256)] = att_ref[pl.ds(row, QBLOCK), pl.ds(at, 256)] + mixed

        score(0)
        for u in range(len(units)):
            if u + 1 < len(units):
                score(u + 1)
            weigh(u)
            mix(u)
            if u % 2 == 1:
                store(u - 1)
        return carry

    lax.fori_loop(0, 4, pair, 0)
    valid = (lax.broadcasted_iota(jnp.int32, (8, QROWS), 1) < SEQ).astype(f32).astype(bf16)
    sum_ref[...] = dot(valid, att_ref[...])


def attend(x, pieces):
    return call(
        attend_kernel,
        (shape((QROWS, WIN), bf16), shape((8, WIN), f32)),
        [x] + pieces,
        specs=[VM] + [ANY] * 16,
        scratch=[
            pltpu.VMEM((D, QKV), bf16),
            pltpu.VMEM((ROWS, QKV), bf16),
            pltpu.SemaphoreType.DMA((16,)),
        ],
        flops=2 * ROWS * D * QKV + 8 * 4 * ROWS * ROWS * 256,
        bytes_accessed=2 * (D * QKV + ROWS * D + QROWS * WIN),
        name="attend",
    )


def project_kernel(m_ref, att_ref, w_ref, x_ref, own_ref, send_ref):
    m = m_ref[0]
    mine = w_ref[pl.ds(pl.multiple_of(m * HALF, HALF), HALF), :]
    theirs = w_ref[pl.ds(pl.multiple_of((1 - m) * HALF, HALF), HALF), :]
    send_ref[...] = dot(theirs, att_ref[...], NT)[:, :SEQ].astype(bf16)
    own_ref[...] = dot(mine, att_ref[...], NT)[:, :SEQ] + x_ref[0].astype(f32)


def project(m, att, w, x, sample):
    full = lambda *dims: pl.BlockSpec(dims, lambda i: (0,) * len(dims))
    return pl.pallas_call(
        project_kernel,
        grid=(1,),
        out_shape=(shape((HALF, SEQ), f32), shape((HALF, SEQ), bf16)),
        in_specs=[SM, full(QROWS, WIN), full(D, WIN), pl.BlockSpec((1, HALF, SEQ), lambda i: (sample, 0, 0))],
        out_specs=(full(HALF, SEQ), full(HALF, SEQ)),
        compiler_params=pltpu.CompilerParams(vmem_limit_bytes=VMEM_LIMIT),
        cost_estimate=pl.CostEstimate(
            flops=2 * D * WIN * QROWS, bytes_accessed=2 * (QROWS * WIN + D * WIN) + 8 * HALF * SEQ, transcendentals=0
        ),
        name="project",
    )(m, att, w, x)


def finish_kernel(own_ref, other_ref, *refs):
    out_ref = refs[-1]
    out_ref[0] = (own_ref[...] + other_ref[...].astype(f32)).astype(bf16)


def finish(own, other, sample, before=None):
    rows = 288
    spec = pl.BlockSpec((rows, SEQ), lambda i: (i, 0))
    args = [own, other] + ([before] if before is not None else [])
    return pl.pallas_call(
        finish_kernel,
        grid=(HALF // rows,),
        out_shape=shape((2, HALF, SEQ), bf16),
        in_specs=[spec, spec] + ([ANY] if before is not None else []),
        out_specs=pl.BlockSpec((1, rows, SEQ), lambda i: (sample, i, 0)),
        input_output_aliases={2: 0} if before is not None else {},
        compiler_params=pltpu.CompilerParams(vmem_limit_bytes=VMEM_LIMIT),
        cost_estimate=pl.CostEstimate(flops=HALF * SEQ, bytes_accessed=8 * HALF * SEQ, transcendentals=0),
        name="finish",
    )(*args)


def text_kernel(m_ref, co_ref, cr_ref, w_ref, wo_ref, part_ref, last_ref, x_ref):
    m = m_ref[0]
    own = co_ref[...].astype(f32)
    other = cr_ref[...].astype(f32)
    first = jnp.where(m == 0, own, other)
    second = jnp.where(m == 0, other, own)
    x_ref[:, pl.ds(0, HALF)] = first
    x_ref[:, pl.ds(HALF, HALF)] = second
    x = x_ref[...]
    center = jnp.sum(x, axis=1, keepdims=True) * (1.0 / D)
    centred = x - center
    spread = jnp.sum(centred * centred, axis=1, keepdims=True) * (1.0 / D)
    normed = (centred * lax.rsqrt(spread + 1e-06)).astype(bf16)
    q = dot(normed, w_ref[0], NT).astype(bf16).astype(f32)
    k = dot(normed, w_ref[1], NT).astype(bf16)
    v = dot(normed, w_ref[2], NT).astype(bf16)
    row = lax.broadcasted_iota(jnp.int32, (16, HALF), 0)
    lane = lax.broadcasted_iota(jnp.int32, (16, HALF), 1)
    low = (row % 8) * HEAD_DIM
    of_head = (lane >= low) & (lane < low + HEAD_DIM)
    q_last = jnp.where(row < 8, q[TEXT - 1 : TEXT], q[2 * TEXT - 1 : 2 * TEXT])
    q_head = jnp.where(of_head, q_last, 0.0).astype(bf16)
    s = dot(q_head, k, NT) * HEAD_DIM ** (-0.5)
    key = lax.broadcasted_iota(jnp.int32, (16, 2 * TEXT), 1)
    of = lax.broadcasted_iota(jnp.int32, (16, 2 * TEXT), 0)
    s = jnp.where((key < TEXT) == (of < 8), s, -1e30)
    e = jnp.exp(s - jnp.max(s, axis=1, keepdims=True))
    weight = (e / jnp.sum(e, axis=1, keepdims=True)).astype(bf16)
    o = jnp.where(of_head, dot(weight, v), 0.0)
    a = jnp.sum(jnp.where(row < 8, o, 0.0), axis=0, keepdims=True)
    b = jnp.sum(jnp.where(row < 8, 0.0, o), axis=0, keepdims=True)
    att = jnp.where(lax.broadcasted_iota(jnp.int32, (8, HALF), 0) == 2, a, b).astype(bf16)
    part_ref[...] = dot(att, wo_ref[...])
    at = lax.broadcasted_iota(jnp.int32, (8, D), 0)
    last_ref[...] = jnp.where(at == 2, x[TEXT - 1 : TEXT], x[2 * TEXT - 1 : 2 * TEXT])


def text_tower(m, own, other, w, wo):
    return call(
        text_kernel,
        (shape((8, D), f32), shape((8, D), f32)),
        [m, own, other, w, wo],
        specs=[SM, VM, VM, VM, VM],
        scratch=[pltpu.VMEM((2 * TEXT, D), f32)],
        flops=2 * 128 * D * 3 * HALF,
        bytes_accessed=2 * (3 * HALF * D + HALF * D),
        name="text_tower",
    )


def embed_rows(features, out_ref):
    total = jnp.sum(features * features, axis=1, keepdims=True)
    embedded = (features * lax.rsqrt(total + 1e-06)).astype(bf16)
    for which in range(4):
        out_ref[:, pl.ds(D * which, D)] = embedded[which : which + 1]


def embed_kernel(base_ref, mine_ref, other_ref, out_ref):
    embed_rows(base_ref[...] + (mine_ref[...] + other_ref[...]), out_ref)


def embed(base, mine, other):
    return call(embed_kernel, shape((1, MESSAGE), bf16), [base, mine, other], bytes_accessed=100000, name="embed")


def pool_kernel(m_ref, a_ref, b_ref, ma_ref, mb_ref, w_ref, text_ref, last_ref, part_ref, base_ref):
    row = lax.broadcasted_iota(jnp.int32, (8, WIN), 0)
    sums = jnp.where(row == 0, a_ref[...], b_ref[...]) * (1.0 / SEQ)
    high = sums.astype(bf16)
    rest = sums - high.astype(f32)
    mid = rest.astype(bf16)
    low = (rest - mid.astype(f32)).astype(bf16)
    w = w_ref[...]
    pooled = dot(high, w, NT) + (dot(mid, w, NT) + dot(low, w, NT))
    image_row = lax.broadcasted_iota(jnp.int32, (8, D), 0) < 2
    part_ref[...] = jnp.where(image_row, pooled, text_ref[...])
    m = m_ref[0]
    at = lax.broadcasted_iota(jnp.int32, (8, HALF), 0)
    own = jnp.where(at == 0, ma_ref[:, pl.ds(0, HALF)], mb_ref[:, pl.ds(0, HALF)])
    other = jnp.where(at == 0, ma_ref[:, pl.ds(HALF + 64, HALF)], mb_ref[:, pl.ds(HALF + 64, HALF)])
    image_row = at < 2
    base_ref[:, pl.ds(0, HALF)] = jnp.where(image_row, jnp.where(m == 0, own, other), last_ref[:, pl.ds(0, HALF)])
    base_ref[:, pl.ds(HALF, HALF)] = jnp.where(image_row, jnp.where(m == 0, other, own), last_ref[:, pl.ds(HALF, HALF)])


def pool(m, sum_a, sum_b, mean_a, mean_b, w, text_part, text_last):
    return call(
        pool_kernel,
        (shape((8, D), f32), shape((8, D), f32)),
        [m, sum_a, sum_b, mean_a, mean_b, w, text_part, text_last],
        specs=[SM] + [VM] * 7,
        flops=3 * 2 * 8 * WIN * D,
        bytes_accessed=2 * D * WIN,
        name="pool",
    )


def pair_kernel(m_ref, at_ref, own_ref, all_ref, image_ref, text_ref):
    own = own_ref[...].astype(f32)
    row = lax.broadcasted_iota(jnp.int32, (8, D), 0)
    at_row = lax.broadcasted_iota(jnp.int32, (8, 128), 0)
    at_col = lax.broadcasted_iota(jnp.int32, (8, 128), 1)
    for mine, others, out_ref in ((0, 2, image_ref), (2, 0, text_ref)):
        rows = jnp.where(row == 0, own[:, D * mine : D * mine + D], own[:, D * mine + D : D * mine + 2 * D]).astype(bf16)
        grad = None
        for which in range(2):
            each = all_ref[:, pl.ds(D * (others + which), D)]
            logit = 10.0 * dot(rows, each, NT) - 1.0
            label = jnp.where((at_row == which) & (at_col == at_ref[0]), 1.0, -1.0)
            weight = (-10.0 * label / (1.0 + jnp.exp(label * logit))).astype(bf16)
            term = dot(weight, each)
            grad = term if grad is None else grad + term
        out_ref[...] = jnp.where(m_ref[0] == 0, grad[0:2, 0:HALF], grad[0:2, HALF:])


def pair_grads(m, at, own, every):
    return call(
        pair_kernel,
        (shape((2, HALF), f32), shape((2, HALF), f32)),
        [m, at, own, every],
        specs=[SM, SM, VM, VM],
        flops=4 * 2 * 8 * 256 * D,
        bytes_accessed=2 * 128 * MESSAGE,
        name="pair_grads",
    )


def weight_slabs(image_qkv, image_out):
    return jnp.concatenate(
        [image_qkv[:, 0:1], image_qkv[:, 2:3], image_qkv[:, 1:2], jnp.transpose(image_out)[:, None, :]], axis=1
    )


def gather_weights(slab, over_w):
    pair = jnp.concatenate([slab, over_w], axis=0)
    return lax.all_gather(pair, "z", axis=0, tiled=True).reshape(PIECE, COLS)


def row_order(x, w, c):
    at = np.arange(D)
    r, rest = at % 9, at // 9
    wr, rest = rest % 2, rest // 2
    z, rest = rest % 8, rest // 8
    xr, cr = rest % 4, rest // 4
    device = ((z * 4 + (x + xr) % 4) * 2 + (w + wr) % 2) * 2 + (c + cr) % 2
    return (device * 9 + r).astype(jnp.int32).reshape(1, D)


def on_device(patches, image_qkv, image_out, captions, text_qkv, text_out):
    z, x, w, c, m = (lax.axis_index(a) for a in ("z", "x", "w", "c", "m"))
    m_arr = jnp.reshape(m, (1,)).astype(jnp.int32)
    order = row_order(x, w, c)
    norm_order = (order + HALF * m) % D

    own = jnp.transpose(patches, (0, 2, 1))
    captions2 = captions.reshape(2 * TEXT, HALF)
    captions_other = shift(captions2, "m", 2, 1)
    slab = weight_slabs(image_qkv, image_out)
    over_w = shift(slab, "w", 2, 1)
    other0 = shift(after(own[0:1], over_w, captions_other), "m", 2, 1)
    piece = gather_weights(slab, over_w)

    a0, b0 = piece[: SPLIT[0]], piece[SPLIT[0] :]
    a1, b1 = shift(a0, "x", 4, 1), shift(b0, "x", 4, 1)
    a3, b3 = shift(a0, "x", 4, 3), shift(b0, "x", 4, 3)
    other1 = shift(after(own[1:2], other0), "m", 2, 1)
    normed0, mean0 = norm_patches(norm_order, own, other0, 0)
    text_part, text_last = text_tower(
        m_arr, captions2, captions_other, jnp.transpose(text_qkv, (1, 2, 0)), text_out
    )
    a2 = shift(after(a3, normed0), "x", 4, 3)
    b2 = shift(after(b1, text_part), "x", 4, 1)
    near = [a0, b0, a1, b1, a2, b2, a3, b3]
    normed1, mean1 = norm_patches(norm_order, own, other1, 1)
    pieces = near + [shift(block if n != 4 else after(block, normed1), "c", 2, 1) for n, block in enumerate(near)]

    att0, sum0 = attend(normed0, pieces)
    wo = order_out(after(order, sum0), pieces)
    own0, send0 = project(m_arr, att0, wo, own, 0)
    got0 = shift(send0, "m", 2, 1)
    att1, sum1 = attend(after(normed1, send0), pieces)
    part, base = pool(m_arr, sum0, after(sum1, got0), mean0, mean1, wo, text_part, text_last)
    embedded = embed(base, part, shift(part, "m", 2, 1))
    hidden = finish(own0, after(got0, part), 0)
    own1, send1 = project(m_arr, after(att1, hidden), wo, own, 1)
    both = jnp.concatenate([embedded, shift(embedded, "w", 2, 1)], axis=0)
    got1 = shift(after(send1, both), "m", 2, 1)
    along_z = spread(both, "z", 8).reshape(16, MESSAGE)
    every = spread(along_z, ("x", "c"), 8).reshape(128, MESSAGE)

    at = jnp.reshape(((x * 2 + c) * 8 + z) * 2, (1,)).astype(jnp.int32)
    image_grad, text_grad = pair_grads(m_arr, at, embedded, every)
    hidden = finish(own1, got1, 1, hidden)
    return jnp.transpose(hidden, (0, 2, 1)), image_grad, text_grad


def solution(mesh):
    split = Mesh(mesh.devices.reshape(8, 4, 2, 2, 2), ("z", "x", "w", "c", "m"))
    batch = ("z", "x", "w", "c")
    return jax.shard_map(
        on_device,
        mesh=split,
        in_specs=(
            P(batch, None, "m"),
            P(batch, None, "m"),
            P("m", batch),
            P(batch, None, "m"),
            P(None, None, "m"),
            P("m", None),
        ),
        out_specs=(P(batch, None, "m"), P(batch, "m"), P(batch, "m")),
        check_vma=False,
    )
```

```python
import functools
import math

import jax
import jax.numpy as jnp
import numpy as np
from jax import lax
from jax.experimental import pallas as pl
from jax.experimental.pallas import tpu as pltpu
from jax.sharding import Mesh, PartitionSpec as P

D = 1152
HALF = 576
HEAD_DIM = 72
SEQ = 729
ROWS = 768
QROWS = 736
QBLOCK = 368
TEXT = 64
COLS = 2304
QKV = 1792
WO_AT = 1664
WIN = 640
SPLIT = (80, 64)
PIECE = 144
Z_STEPS = (0, 1, 2, 7)
MESSAGE = 4 * D

f32 = jnp.float32
bf16 = jnp.bfloat16
NT = (((1,), (1,)), ((), ()))
TN = (((0,), (0,)), ((), ()))
VMEM_LIMIT = 24 * 1024 * 1024


def dot(a, b, dims=(((1,), (0,)), ((), ()))):
    return lax.dot_general(a, b, dims, preferred_element_type=f32)


def call(body, outs, args, specs=None, out_specs=None, scratch=(), flops=0, bytes_accessed=0, name=None, aliases=None):
    whole = pl.BlockSpec(memory_space=pltpu.VMEM)
    return pl.pallas_call(
        body,
        out_shape=outs,
        in_specs=specs if specs is not None else [whole] * len(args),
        out_specs=out_specs if out_specs is not None else jax.tree.map(lambda _: whole, outs),
        scratch_shapes=list(scratch),
        compiler_params=pltpu.CompilerParams(vmem_limit_bytes=VMEM_LIMIT),
        cost_estimate=pl.CostEstimate(flops=int(flops), bytes_accessed=int(bytes_accessed), transcendentals=0),
        input_output_aliases=aliases or {},
        name=name,
    )(*args)


def shape(dims, kind):
    return jax.ShapeDtypeStruct(dims, kind)


VM = pl.BlockSpec(memory_space=pltpu.VMEM)
SM = pl.BlockSpec(memory_space=pltpu.SMEM)
ANY = pl.BlockSpec(memory_space=pl.ANY)


def shift(value, axis, size, step):
    return lax.ppermute(value, axis, [((i + step) % size, i) for i in range(size)])


def shift_zw(value, dz, dw):
    pairs = [((z + dz) % 8 * 2 + (w + dw) % 2, z * 2 + w) for z in range(8) for w in range(2)]
    return lax.ppermute(value, ("z", "w"), pairs)


def after(value, *others):
    return lax.optimization_barrier((value,) + others)[0]


def norm_kernel(idx_ref, xo_ref, xr_ref, out_ref, mean_ref, pad_ref, turned_ref):
    xo = xo_ref[0].astype(f32)
    xr = xr_ref[0].astype(f32)
    center = (jnp.sum(xo, axis=0, keepdims=True) + jnp.sum(xr, axis=0, keepdims=True)) * (1.0 / D)
    co = xo - center
    cr = xr - center
    spread = (jnp.sum(co * co, axis=0, keepdims=True) + jnp.sum(cr * cr, axis=0, keepdims=True)) * (1.0 / D)
    scale = lax.rsqrt(spread + 1e-06)
    pad_ref[:, pl.ds(640, 128)] = jnp.zeros((D, 128), bf16)
    pad_ref[pl.ds(0, HALF), pl.ds(0, SEQ)] = (co * scale).astype(bf16)
    pad_ref[pl.ds(HALF, HALF), pl.ds(0, SEQ)] = (cr * scale).astype(bf16)
    turned_ref[...] = jnp.transpose(pad_ref[...])
    for at in range(0, D, 256):
        size = min(256, D - at)
        rows = lax.broadcasted_iota(jnp.int32, (D, size), 0)
        pick = (rows == idx_ref[:, pl.ds(at, size)]).astype(f32).astype(bf16)
        out_ref[:, pl.ds(at, size)] = dot(turned_ref[...], pick).astype(bf16)
    ones = jnp.ones((8, SEQ), bf16)
    mean_ref[:, pl.ds(0, HALF)] = dot(ones, xo_ref[0], NT) * (1.0 / SEQ)
    mean_ref[:, pl.ds(HALF + 64, HALF)] = dot(ones, xr_ref[0], NT) * (1.0 / SEQ)


def norm_patches(idx, own, other, sample):
    sample_spec = pl.BlockSpec((1, HALF, SEQ), lambda i: (sample, 0, 0))
    other_spec = pl.BlockSpec((1, HALF, SEQ), lambda i: (0, 0, 0))
    return pl.pallas_call(
        norm_kernel,
        grid=(1,),
        out_shape=(shape((ROWS, D), bf16), shape((8, 1280), f32)),
        in_specs=[pl.BlockSpec((1, D), lambda i: (0, 0)), sample_spec, other_spec],
        out_specs=(pl.BlockSpec((ROWS, D), lambda i: (0, 0)), pl.BlockSpec((8, 1280), lambda i: (0, 0))),
        scratch_shapes=[pltpu.VMEM((D, ROWS), bf16), pltpu.VMEM((ROWS, D), bf16)],
        compiler_params=pltpu.CompilerParams(vmem_limit_bytes=VMEM_LIMIT),
        cost_estimate=pl.CostEstimate(flops=2 * ROWS * D * D, bytes_accessed=4 * ROWS * D, transcendentals=0),
        name="norm_patches",
    )(idx, own, other)


def order_kernel(idx_ref, *refs):
    pieces, (out_ref, mixed_ref, pick_ref, sems) = refs[:10], refs[10:]
    copies = []
    row = 0
    for n, piece in enumerate(pieces):
        count = piece.shape[0]
        copies.append(
            pltpu.make_async_copy(
                piece.at[:, pl.ds(WO_AT, WIN)], mixed_ref.at[pl.ds(row, count), :], sems.at[n]
            )
        )
        row += count
    for copy in copies:
        copy.start()
    for copy in copies:
        copy.wait()
    rows = lax.broadcasted_iota(jnp.int32, (D, D), 0)
    pick_ref[...] = (rows == idx_ref[...]).astype(f32).astype(bf16)
    for at in range(0, WIN, 256):
        size = min(256, WIN - at)
        out_ref[:, pl.ds(at, size)] = dot(pick_ref[...], mixed_ref[:, pl.ds(at, size)]).astype(bf16)


def order_out(idx, pieces):
    return call(
        order_kernel,
        shape((D, WIN), bf16),
        [idx] + pieces,
        specs=[VM] + [ANY] * 10,
        scratch=[pltpu.VMEM((D, WIN), bf16), pltpu.VMEM((D, D), bf16), pltpu.SemaphoreType.DMA((10,))],
        flops=2 * D * D * WIN,
        bytes_accessed=4 * D * WIN,
        name="order_out",
    )


def attend_kernel(x_ref, *refs):
    pieces, (att_ref, sum_ref, w_ref, qkv_ref, sems) = refs[:10], refs[10:]
    copies = []
    row = 0
    for n, piece in enumerate(pieces):
        count = piece.shape[0]
        copies.append(
            pltpu.make_async_copy(piece.at[:, pl.ds(0, QKV)], w_ref.at[pl.ds(row, count), :], sems.at[n])
        )
        row += count
    for copy in copies:
        copy.start()
    att_ref[...] = jnp.zeros_like(att_ref)
    for copy in copies:
        copy.wait()

    q_scale = math.log2(math.e) * HEAD_DIM ** (-0.5)

    def project(n, carry):
        at = pl.multiple_of(n * 256, 256)
        lane = at + lax.broadcasted_iota(jnp.int32, (1, 256), 1)
        scale = jnp.where(lane < HALF, q_scale, 1.0).astype(f32)
        qkv_ref[:, pl.ds(at, 256)] = (dot(x_ref[...], w_ref[:, pl.ds(at, 256)]) * scale).astype(bf16)
        return carry

    lax.fori_loop(0, QKV // 256, project, 0)

    lane = lax.broadcasted_iota(jnp.int32, (1, 256), 1)

    def between(low, high):
        return ((lane >= low) & (lane < high)).astype(f32)

    last = (lane == 255).astype(f32)
    key_row = lax.broadcasted_iota(jnp.int32, (ROWS, 1), 0)
    key_bias = jnp.where(key_row >= SEQ, -1e30, 0.0).astype(f32) * last

    def pair(p, carry):
        at = pl.multiple_of(p * 128, 128)
        q_at = 16 * p
        v_at = 64 + 16 * p
        k_win = qkv_ref[:, pl.ds(D + at, 256)] * (1.0 - last).astype(bf16) + key_bias.astype(bf16)
        v_win = qkv_ref[:, pl.ds(512 + at, 256)]
        values = []
        for h in range(2):
            low = v_at + HEAD_DIM * h
            ones = (lane == h).astype(f32).astype(bf16)
            values.append(v_win * between(low, low + HEAD_DIM).astype(bf16) + ones)
        units = [(row, h) for row in range(0, QROWS, QBLOCK) for h in range(2)]
        scores, weights, totals = {}, {}, {}

        def score(u):
            row, h = units[u]
            low = q_at + HEAD_DIM * h
            q_win = qkv_ref[pl.ds(row, QBLOCK), pl.ds(at, 256)]
            q = q_win * between(low, low + HEAD_DIM).astype(bf16) + last.astype(bf16)
            scores[u] = dot(q, k_win, NT)

        def weigh(u):
            s = scores.pop(u)
            weights[u] = jnp.exp2((s - jnp.max(s, axis=1, keepdims=True)).astype(bf16))

        def mix(u):
            row, h = units[u]
            totals[u] = dot(weights.pop(u), values[h])

        def store(u):
            row = units[u][0]
            total = totals.pop(u) + totals.pop(u + 1)
            inverse = jnp.where(lane < v_at + HEAD_DIM, 1.0 / total[:, 0:1], 1.0 / total[:, 1:2])
            mixed = (total * inverse * between(v_at, v_at + 2 * HEAD_DIM)).astype(bf16)
            att_ref[pl.ds(row, QBLOCK), pl.ds(at, 256)] = att_ref[pl.ds(row, QBLOCK), pl.ds(at, 256)] + mixed

        score(0)
        for u in range(len(units)):
            if u + 1 < len(units):
                score(u + 1)
            weigh(u)
            mix(u)
            if u % 2 == 1:
                store(u - 1)
        return carry

    lax.fori_loop(0, 4, pair, 0)
    valid = (lax.broadcasted_iota(jnp.int32, (8, QROWS), 1) < SEQ).astype(f32).astype(bf16)
    sum_ref[...] = dot(valid, att_ref[...])


def attend(x, pieces):
    return call(
        attend_kernel,
        (shape((QROWS, WIN), bf16), shape((8, WIN), f32)),
        [x] + pieces,
        specs=[VM] + [ANY] * 10,
        scratch=[
            pltpu.VMEM((D, QKV), bf16),
            pltpu.VMEM((ROWS, QKV), bf16),
            pltpu.SemaphoreType.DMA((10,)),
        ],
        flops=2 * ROWS * D * QKV + 8 * 4 * ROWS * ROWS * 256,
        bytes_accessed=2 * (D * QKV + ROWS * D + QROWS * WIN),
        name="attend",
    )


def project_kernel(m_ref, att_ref, w_ref, x_ref, own_ref, send_ref):
    m = m_ref[0]
    mine = w_ref[pl.ds(pl.multiple_of(m * HALF, HALF), HALF), :]
    theirs = w_ref[pl.ds(pl.multiple_of((1 - m) * HALF, HALF), HALF), :]
    send_ref[...] = dot(theirs, att_ref[...], NT)[:, :SEQ].astype(bf16)
    own_ref[...] = dot(mine, att_ref[...], NT)[:, :SEQ] + x_ref[0].astype(f32)


def project(m, att, w, x, sample):
    full = lambda *dims: pl.BlockSpec(dims, lambda i: (0,) * len(dims))
    return pl.pallas_call(
        project_kernel,
        grid=(1,),
        out_shape=(shape((HALF, SEQ), f32), shape((HALF, SEQ), bf16)),
        in_specs=[SM, full(QROWS, WIN), full(D, WIN), pl.BlockSpec((1, HALF, SEQ), lambda i: (sample, 0, 0))],
        out_specs=(full(HALF, SEQ), full(HALF, SEQ)),
        compiler_params=pltpu.CompilerParams(vmem_limit_bytes=VMEM_LIMIT),
        cost_estimate=pl.CostEstimate(
            flops=2 * D * WIN * QROWS, bytes_accessed=2 * (QROWS * WIN + D * WIN) + 8 * HALF * SEQ, transcendentals=0
        ),
        name="project",
    )(m, att, w, x)


def finish_kernel(own_ref, other_ref, *refs):
    out_ref = refs[-1]
    out_ref[0] = (own_ref[...] + other_ref[...].astype(f32)).astype(bf16)


def finish(own, other, sample, before=None):
    rows = 288
    spec = pl.BlockSpec((rows, SEQ), lambda i: (i, 0))
    args = [own, other] + ([before] if before is not None else [])
    return pl.pallas_call(
        finish_kernel,
        grid=(HALF // rows,),
        out_shape=shape((2, HALF, SEQ), bf16),
        in_specs=[spec, spec] + ([ANY] if before is not None else []),
        out_specs=pl.BlockSpec((1, rows, SEQ), lambda i: (sample, i, 0)),
        input_output_aliases={2: 0} if before is not None else {},
        compiler_params=pltpu.CompilerParams(vmem_limit_bytes=VMEM_LIMIT),
        cost_estimate=pl.CostEstimate(flops=HALF * SEQ, bytes_accessed=8 * HALF * SEQ, transcendentals=0),
        name="finish",
    )(*args)


def text_kernel(m_ref, co_ref, cr_ref, w_ref, wo_ref, part_ref, last_ref, x_ref):
    m = m_ref[0]
    own = co_ref[...].astype(f32)
    other = cr_ref[...].astype(f32)
    first = jnp.where(m == 0, own, other)
    second = jnp.where(m == 0, other, own)
    x_ref[:, pl.ds(0, HALF)] = first
    x_ref[:, pl.ds(HALF, HALF)] = second
    x = x_ref[...]
    center = jnp.sum(x, axis=1, keepdims=True) * (1.0 / D)
    centred = x - center
    spread = jnp.sum(centred * centred, axis=1, keepdims=True) * (1.0 / D)
    normed = (centred * lax.rsqrt(spread + 1e-06)).astype(bf16)
    q = dot(normed, w_ref[0], NT).astype(bf16).astype(f32)
    k = dot(normed, w_ref[1], NT).astype(bf16)
    v = dot(normed, w_ref[2], NT).astype(bf16)
    row = lax.broadcasted_iota(jnp.int32, (16, HALF), 0)
    lane = lax.broadcasted_iota(jnp.int32, (16, HALF), 1)
    low = (row % 8) * HEAD_DIM
    of_head = (lane >= low) & (lane < low + HEAD_DIM)
    q_last = jnp.where(row < 8, q[TEXT - 1 : TEXT], q[2 * TEXT - 1 : 2 * TEXT])
    q_head = jnp.where(of_head, q_last, 0.0).astype(bf16)
    s = dot(q_head, k, NT) * HEAD_DIM ** (-0.5)
    key = lax.broadcasted_iota(jnp.int32, (16, 2 * TEXT), 1)
    of = lax.broadcasted_iota(jnp.int32, (16, 2 * TEXT), 0)
    s = jnp.where((key < TEXT) == (of < 8), s, -1e30)
    e = jnp.exp(s - jnp.max(s, axis=1, keepdims=True))
    weight = (e / jnp.sum(e, axis=1, keepdims=True)).astype(bf16)
    o = jnp.where(of_head, dot(weight, v), 0.0)
    a = jnp.sum(jnp.where(row < 8, o, 0.0), axis=0, keepdims=True)
    b = jnp.sum(jnp.where(row < 8, 0.0, o), axis=0, keepdims=True)
    att = jnp.where(lax.broadcasted_iota(jnp.int32, (8, HALF), 0) == 2, a, b).astype(bf16)
    part_ref[...] = dot(att, wo_ref[...])
    at = lax.broadcasted_iota(jnp.int32, (8, D), 0)
    last_ref[...] = jnp.where(at == 2, x[TEXT - 1 : TEXT], x[2 * TEXT - 1 : 2 * TEXT])


def text_tower(m, own, other, w, wo):
    return call(
        text_kernel,
        (shape((8, D), f32), shape((8, D), f32)),
        [m, own, other, w, wo],
        specs=[SM, VM, VM, VM, VM],
        scratch=[pltpu.VMEM((2 * TEXT, D), f32)],
        flops=2 * 128 * D * 3 * HALF,
        bytes_accessed=2 * (3 * HALF * D + HALF * D),
        name="text_tower",
    )


def embed_rows(features, out_ref):
    total = jnp.sum(features * features, axis=1, keepdims=True)
    embedded = (features * lax.rsqrt(total + 1e-06)).astype(bf16)
    for which in range(4):
        out_ref[:, pl.ds(D * which, D)] = embedded[which : which + 1]


def embed_kernel(base_ref, mine_ref, other_ref, out_ref):
    embed_rows(base_ref[...] + (mine_ref[...] + other_ref[...]), out_ref)


def embed(base, mine, other):
    return call(embed_kernel, shape((1, MESSAGE), bf16), [base, mine, other], bytes_accessed=100000, name="embed")


def pool_kernel(m_ref, a_ref, b_ref, ma_ref, mb_ref, w_ref, text_ref, last_ref, part_ref, base_ref):
    row = lax.broadcasted_iota(jnp.int32, (8, WIN), 0)
    sums = jnp.where(row == 0, a_ref[...], b_ref[...]) * (1.0 / SEQ)
    high = sums.astype(bf16)
    rest = sums - high.astype(f32)
    mid = rest.astype(bf16)
    low = (rest - mid.astype(f32)).astype(bf16)
    w = w_ref[...]
    pooled = dot(high, w, NT) + (dot(mid, w, NT) + dot(low, w, NT))
    image_row = lax.broadcasted_iota(jnp.int32, (8, D), 0) < 2
    part_ref[...] = jnp.where(image_row, pooled, text_ref[...])
    m = m_ref[0]
    at = lax.broadcasted_iota(jnp.int32, (8, HALF), 0)
    own = jnp.where(at == 0, ma_ref[:, pl.ds(0, HALF)], mb_ref[:, pl.ds(0, HALF)])
    other = jnp.where(at == 0, ma_ref[:, pl.ds(HALF + 64, HALF)], mb_ref[:, pl.ds(HALF + 64, HALF)])
    image_row = at < 2
    base_ref[:, pl.ds(0, HALF)] = jnp.where(image_row, jnp.where(m == 0, own, other), last_ref[:, pl.ds(0, HALF)])
    base_ref[:, pl.ds(HALF, HALF)] = jnp.where(image_row, jnp.where(m == 0, other, own), last_ref[:, pl.ds(HALF, HALF)])


def pool(m, sum_a, sum_b, mean_a, mean_b, w, text_part, text_last):
    return call(
        pool_kernel,
        (shape((8, D), f32), shape((8, D), f32)),
        [m, sum_a, sum_b, mean_a, mean_b, w, text_part, text_last],
        specs=[SM] + [VM] * 7,
        flops=3 * 2 * 8 * WIN * D,
        bytes_accessed=2 * D * WIN,
        name="pool",
    )


def pair_kernel(m_ref, own_ref, *refs):
    pieces, (image_ref, text_ref, all_ref) = refs[:8], refs[8:]
    for n, piece in enumerate(pieces):
        all_ref[pl.ds(16 * n, 16), :] = piece[...]
    own = own_ref[...].astype(f32)
    row = lax.broadcasted_iota(jnp.int32, (8, D), 0)
    at_row = lax.broadcasted_iota(jnp.int32, (8, 128), 0)
    at_col = lax.broadcasted_iota(jnp.int32, (8, 128), 1)
    for mine, others, out_ref in ((0, 2, image_ref), (2, 0, text_ref)):
        rows = jnp.where(row == 0, own[:, D * mine : D * mine + D], own[:, D * mine + D : D * mine + 2 * D]).astype(bf16)
        grad = None
        for which in range(2):
            each = all_ref[:, pl.ds(D * (others + which), D)]
            logit = 10.0 * dot(rows, each, NT) - 1.0
            label = jnp.where((at_row == which) & (at_col == 0), 1.0, -1.0)
            weight = (-10.0 * label / (1.0 + jnp.exp(label * logit))).astype(bf16)
            term = dot(weight, each)
            grad = term if grad is None else grad + term
        out_ref[...] = jnp.where(m_ref[0] == 0, grad[0:2, 0:HALF], grad[0:2, HALF:])


def pair_grads(m, own, pieces):
    return call(
        pair_kernel,
        (shape((2, HALF), f32), shape((2, HALF), f32)),
        [m, own] + pieces,
        specs=[SM] + [VM] * 9,
        scratch=[pltpu.VMEM((128, MESSAGE), bf16)],
        flops=4 * 2 * 8 * 256 * D,
        bytes_accessed=2 * 128 * MESSAGE,
        name="pair_grads",
    )


def gather_quad(embedded):
    others = [shift(embedded, "w", 2, 1), shift(embedded, "z", 8, 4), shift_zw(embedded, 4, 1)]
    return jnp.concatenate([embedded] + others, axis=0)


def gather_rest(quad):
    along_z = jnp.concatenate([quad] + [shift(quad, "z", 8, k) for k in Z_STEPS[1:]], axis=0)
    near = [along_z] + [shift(along_z, "x", 4, k) for k in (1, 3, 2)]
    return near + [shift(piece, "c", 2, 1) for piece in near]


def weight_slabs(image_qkv, image_out):
    return jnp.concatenate(
        [image_qkv[:, 0:1], image_qkv[:, 2:3], image_qkv[:, 1:2], jnp.transpose(image_out)[:, None, :]], axis=1
    )


def gather_weights(slab, over_w, over_z, over_zw):
    pair = after(jnp.concatenate([slab, over_w], axis=0))
    quad = after(jnp.concatenate([slab, over_w, over_z, over_zw], axis=0))
    quads = [quad, shift(quad, "z", 8, 1), shift(pair, "z", 8, 2), shift(pair, "z", 8, 6), shift(quad, "z", 8, 7)]
    return jnp.concatenate(quads, axis=0).reshape(PIECE, COLS)


def row_order(z, x, w, c):
    at = np.arange(D)
    r, rest = at % 9, at // 9
    wr, rest = rest % 2, rest // 2
    z4, rest = rest % 2, rest // 2
    zr, rest = np.array(Z_STEPS)[rest % 4] + 4 * z4, rest // 4
    xr, cr = rest % 4, rest // 4
    device = (((z + zr) % 8 * 4 + (x + xr) % 4) * 2 + (w + wr) % 2) * 2 + (c + cr) % 2
    return (device * 9 + r).astype(jnp.int32).reshape(1, D)


def on_device(patches, image_qkv, image_out, captions, text_qkv, text_out):
    z, x, w, c, m = (lax.axis_index(a) for a in ("z", "x", "w", "c", "m"))
    m_arr = jnp.reshape(m, (1,)).astype(jnp.int32)
    order = row_order(z, x, w, c)
    norm_order = (order + HALF * m) % D

    own = jnp.transpose(patches, (0, 2, 1))
    captions2 = captions.reshape(2 * TEXT, HALF)
    captions_other = shift(captions2, "m", 2, 1)
    slab = weight_slabs(image_qkv, image_out)
    first = [shift(slab, "w", 2, 1), shift(slab, "z", 8, 4), shift_zw(slab, 4, 1)]
    other0 = shift(after(own[0:1], captions_other, *first), "m", 2, 1)
    piece = gather_weights(slab, *first)
    text_part, text_last = text_tower(
        m_arr, captions2, after(captions_other, *first), jnp.transpose(text_qkv, (1, 2, 0)), text_out
    )

    piece = after(piece, text_part)
    next_piece, last_piece = shift(piece, "x", 4, 1), shift(piece, "x", 4, 3)
    other1 = shift(after(own[1:2], other0, piece), "m", 2, 1)
    normed0, mean0 = norm_patches(norm_order, own, after(other0, piece), 0)
    far_a = shift(last_piece[: SPLIT[0]], "x", 4, 3)
    far_b = shift(next_piece[SPLIT[0] :], "x", 4, 1)
    near = [piece, next_piece, far_a, far_b, last_piece]
    pieces = near + [shift(after(block, normed0), "c", 2, 1) for block in near]
    normed1, mean1 = norm_patches(norm_order, own, other1, 1)

    att0, sum0 = attend(after(normed0, normed1), pieces)
    wo = order_out(after(order, sum0), pieces)
    own0, send0 = project(m_arr, att0, wo, own, 0)
    got0 = shift(send0, "m", 2, 1)
    att1, sum1 = attend(after(normed1, send0), pieces)
    part, base = pool(m_arr, sum0, after(sum1, got0), mean0, mean1, wo, text_part, text_last)
    hidden = finish(own0, after(got0, part), 0)
    own1, send1 = project(m_arr, after(att1, hidden), wo, own, 1)
    embedded = embed(base, part, after(shift(part, "m", 2, 1), send1))
    quad = gather_quad(embedded)
    got1 = shift(after(send1, quad), "m", 2, 1)
    every = gather_rest(quad)

    image_grad, text_grad = pair_grads(m_arr, embedded, every)
    hidden = finish(own1, got1, 1, hidden)
    return jnp.transpose(hidden, (0, 2, 1)), image_grad, text_grad


def solution(mesh):
    split = Mesh(mesh.devices.reshape(8, 4, 2, 2, 2), ("z", "x", "w", "c", "m"))
    batch = ("z", "x", "w", "c")
    return jax.shard_map(
        on_device,
        mesh=split,
        in_specs=(
            P(batch, None, "m"),
            P(batch, None, "m"),
            P("m", batch),
            P(batch, None, "m"),
            P(None, None, "m"),
            P("m", None),
        ),
        out_specs=(P(batch, None, "m"), P(batch, "m"), P(batch, "m")),
        check_vma=False,
    )
```

```python
import functools
import math

import jax
import jax.numpy as jnp
import numpy as np
from jax import lax
from jax.experimental import pallas as pl
from jax.experimental.pallas import tpu as pltpu
from jax.sharding import Mesh, PartitionSpec as P

D = 1152
HALF = 576
HEAD_DIM = 72
SEQ = 729
ROWS = 768
QROWS = 736
QBLOCK = 368
TEXT = 64
COLS = 2304
QKV = 1792
WO_AT = 1664
WIN = 640
SPLIT = (80, 64)
PIECE = 144
Z_STEPS = (0, 1, 2, 7)
MESSAGE = 4 * D

f32 = jnp.float32
bf16 = jnp.bfloat16
NT = (((1,), (1,)), ((), ()))
TN = (((0,), (0,)), ((), ()))
VMEM_LIMIT = 24 * 1024 * 1024


def dot(a, b, dims=(((1,), (0,)), ((), ()))):
    return lax.dot_general(a, b, dims, preferred_element_type=f32)


def call(body, outs, args, specs=None, out_specs=None, scratch=(), flops=0, bytes_accessed=0, name=None, aliases=None):
    whole = pl.BlockSpec(memory_space=pltpu.VMEM)
    return pl.pallas_call(
        body,
        out_shape=outs,
        in_specs=specs if specs is not None else [whole] * len(args),
        out_specs=out_specs if out_specs is not None else jax.tree.map(lambda _: whole, outs),
        scratch_shapes=list(scratch),
        compiler_params=pltpu.CompilerParams(vmem_limit_bytes=VMEM_LIMIT),
        cost_estimate=pl.CostEstimate(flops=int(flops), bytes_accessed=int(bytes_accessed), transcendentals=0),
        input_output_aliases=aliases or {},
        name=name,
    )(*args)


def shape(dims, kind):
    return jax.ShapeDtypeStruct(dims, kind)


VM = pl.BlockSpec(memory_space=pltpu.VMEM)
SM = pl.BlockSpec(memory_space=pltpu.SMEM)
ANY = pl.BlockSpec(memory_space=pl.ANY)


def shift(value, axis, size, step):
    return lax.ppermute(value, axis, [((i + step) % size, i) for i in range(size)])


def after(value, *others):
    return lax.optimization_barrier((value,) + others)[0]


def norm_kernel(idx_ref, xo_ref, xr_ref, out_ref, mean_ref, pad_ref, turned_ref):
    xo = xo_ref[0].astype(f32)
    xr = xr_ref[0].astype(f32)
    center = (jnp.sum(xo, axis=0, keepdims=True) + jnp.sum(xr, axis=0, keepdims=True)) * (1.0 / D)
    co = xo - center
    cr = xr - center
    spread = (jnp.sum(co * co, axis=0, keepdims=True) + jnp.sum(cr * cr, axis=0, keepdims=True)) * (1.0 / D)
    scale = lax.rsqrt(spread + 1e-06)
    pad_ref[:, pl.ds(640, 128)] = jnp.zeros((D, 128), bf16)
    pad_ref[pl.ds(0, HALF), pl.ds(0, SEQ)] = (co * scale).astype(bf16)
    pad_ref[pl.ds(HALF, HALF), pl.ds(0, SEQ)] = (cr * scale).astype(bf16)
    turned_ref[...] = jnp.transpose(pad_ref[...])
    for at in range(0, D, 256):
        size = min(256, D - at)
        rows = lax.broadcasted_iota(jnp.int32, (D, size), 0)
        pick = (rows == idx_ref[:, pl.ds(at, size)]).astype(f32).astype(bf16)
        out_ref[:, pl.ds(at, size)] = dot(turned_ref[...], pick).astype(bf16)
    ones = jnp.ones((8, SEQ), bf16)
    mean_ref[:, pl.ds(0, HALF)] = dot(ones, xo_ref[0], NT) * (1.0 / SEQ)
    mean_ref[:, pl.ds(HALF + 64, HALF)] = dot(ones, xr_ref[0], NT) * (1.0 / SEQ)


def norm_patches(idx, own, other, sample):
    sample_spec = pl.BlockSpec((1, HALF, SEQ), lambda i: (sample, 0, 0))
    other_spec = pl.BlockSpec((1, HALF, SEQ), lambda i: (0, 0, 0))
    return pl.pallas_call(
        norm_kernel,
        grid=(1,),
        out_shape=(shape((ROWS, D), bf16), shape((8, 1280), f32)),
        in_specs=[pl.BlockSpec((1, D), lambda i: (0, 0)), sample_spec, other_spec],
        out_specs=(pl.BlockSpec((ROWS, D), lambda i: (0, 0)), pl.BlockSpec((8, 1280), lambda i: (0, 0))),
        scratch_shapes=[pltpu.VMEM((D, ROWS), bf16), pltpu.VMEM((ROWS, D), bf16)],
        compiler_params=pltpu.CompilerParams(vmem_limit_bytes=VMEM_LIMIT),
        cost_estimate=pl.CostEstimate(flops=2 * ROWS * D * D, bytes_accessed=4 * ROWS * D, transcendentals=0),
        name="norm_patches",
    )(idx, own, other)


def order_kernel(idx_ref, *refs):
    pieces, (out_ref, mixed_ref, pick_ref, sems) = refs[:10], refs[10:]
    copies = []
    row = 0
    for n, piece in enumerate(pieces):
        count = piece.shape[0]
        copies.append(
            pltpu.make_async_copy(
                piece.at[:, pl.ds(WO_AT, WIN)], mixed_ref.at[pl.ds(row, count), :], sems.at[n]
            )
        )
        row += count
    for copy in copies:
        copy.start()
    for copy in copies:
        copy.wait()
    rows = lax.broadcasted_iota(jnp.int32, (D, D), 0)
    pick_ref[...] = (rows == idx_ref[...]).astype(f32).astype(bf16)
    for at in range(0, WIN, 256):
        size = min(256, WIN - at)
        out_ref[:, pl.ds(at, size)] = dot(pick_ref[...], mixed_ref[:, pl.ds(at, size)]).astype(bf16)


def order_out(idx, pieces):
    return call(
        order_kernel,
        shape((D, WIN), bf16),
        [idx] + pieces,
        specs=[VM] + [ANY] * 10,
        scratch=[pltpu.VMEM((D, WIN), bf16), pltpu.VMEM((D, D), bf16), pltpu.SemaphoreType.DMA((10,))],
        flops=2 * D * D * WIN,
        bytes_accessed=4 * D * WIN,
        name="order_out",
    )


def attend_kernel(x_ref, *refs):
    pieces, (att_ref, sum_ref, w_ref, qkv_ref, sems) = refs[:10], refs[10:]
    copies = []
    row = 0
    for n, piece in enumerate(pieces):
        count = piece.shape[0]
        copies.append(
            pltpu.make_async_copy(piece.at[:, pl.ds(0, QKV)], w_ref.at[pl.ds(row, count), :], sems.at[n])
        )
        row += count
    for copy in copies:
        copy.start()
    att_ref[...] = jnp.zeros_like(att_ref)
    for copy in copies:
        copy.wait()

    q_scale = math.log2(math.e) * HEAD_DIM ** (-0.5)

    def project(n, carry):
        at = pl.multiple_of(n * 256, 256)
        lane = at + lax.broadcasted_iota(jnp.int32, (1, 256), 1)
        scale = jnp.where(lane < HALF, q_scale, 1.0).astype(f32)
        qkv_ref[:, pl.ds(at, 256)] = (dot(x_ref[...], w_ref[:, pl.ds(at, 256)]) * scale).astype(bf16)
        return carry

    lax.fori_loop(0, QKV // 256, project, 0)

    lane = lax.broadcasted_iota(jnp.int32, (1, 256), 1)

    def between(low, high):
        return ((lane >= low) & (lane < high)).astype(f32)

    last = (lane == 255).astype(f32)
    key_row = lax.broadcasted_iota(jnp.int32, (ROWS, 1), 0)
    key_bias = jnp.where(key_row >= SEQ, -1e30, 0.0).astype(f32) * last

    def pair(p, carry):
        at = pl.multiple_of(p * 128, 128)
        q_at = 16 * p
        v_at = 64 + 16 * p
        k_win = qkv_ref[:, pl.ds(D + at, 256)] * (1.0 - last).astype(bf16) + key_bias.astype(bf16)
        v_win = qkv_ref[:, pl.ds(512 + at, 256)]
        values = []
        for h in range(2):
            low = v_at + HEAD_DIM * h
            ones = (lane == h).astype(f32).astype(bf16)
            values.append(v_win * between(low, low + HEAD_DIM).astype(bf16) + ones)
        units = [(row, h) for row in range(0, QROWS, QBLOCK) for h in range(2)]
        scores, weights, totals = {}, {}, {}

        def score(u):
            row, h = units[u]
            low = q_at + HEAD_DIM * h
            q_win = qkv_ref[pl.ds(row, QBLOCK), pl.ds(at, 256)]
            q = q_win * between(low, low + HEAD_DIM).astype(bf16) + last.astype(bf16)
            scores[u] = dot(q, k_win, NT)

        def weigh(u):
            s = scores.pop(u)
            weights[u] = jnp.exp2((s - jnp.max(s, axis=1, keepdims=True)).astype(bf16))

        def mix(u):
            row, h = units[u]
            totals[u] = dot(weights.pop(u), values[h])

        def store(u):
            row = units[u][0]
            total = totals.pop(u) + totals.pop(u + 1)
            inverse = jnp.where(lane < v_at + HEAD_DIM, 1.0 / total[:, 0:1], 1.0 / total[:, 1:2])
            mixed = (total * inverse * between(v_at, v_at + 2 * HEAD_DIM)).astype(bf16)
            att_ref[pl.ds(row, QBLOCK), pl.ds(at, 256)] = att_ref[pl.ds(row, QBLOCK), pl.ds(at, 256)] + mixed

        score(0)
        for u in range(len(units)):
            if u + 1 < len(units):
                score(u + 1)
            weigh(u)
            mix(u)
            if u % 2 == 1:
                store(u - 1)
        return carry

    lax.fori_loop(0, 4, pair, 0)
    valid = (lax.broadcasted_iota(jnp.int32, (8, QROWS), 1) < SEQ).astype(f32).astype(bf16)
    sum_ref[...] = dot(valid, att_ref[...])


def attend(x, pieces):
    return call(
        attend_kernel,
        (shape((QROWS, WIN), bf16), shape((8, WIN), f32)),
        [x] + pieces,
        specs=[VM] + [ANY] * 10,
        scratch=[
            pltpu.VMEM((D, QKV), bf16),
            pltpu.VMEM((ROWS, QKV), bf16),
            pltpu.SemaphoreType.DMA((10,)),
        ],
        flops=2 * ROWS * D * QKV + 8 * 4 * ROWS * ROWS * 256,
        bytes_accessed=2 * (D * QKV + ROWS * D + QROWS * WIN),
        name="attend",
    )


def project_kernel(m_ref, att_ref, w_ref, x_ref, own_ref, send_ref):
    m = m_ref[0]
    mine = w_ref[pl.ds(pl.multiple_of(m * HALF, HALF), HALF), :]
    theirs = w_ref[pl.ds(pl.multiple_of((1 - m) * HALF, HALF), HALF), :]
    send_ref[...] = dot(theirs, att_ref[...], NT)[:, :SEQ].astype(bf16)
    own_ref[...] = dot(mine, att_ref[...], NT)[:, :SEQ] + x_ref[0].astype(f32)


def project(m, att, w, x, sample):
    full = lambda *dims: pl.BlockSpec(dims, lambda i: (0,) * len(dims))
    return pl.pallas_call(
        project_kernel,
        grid=(1,),
        out_shape=(shape((HALF, SEQ), f32), shape((HALF, SEQ), bf16)),
        in_specs=[SM, full(QROWS, WIN), full(D, WIN), pl.BlockSpec((1, HALF, SEQ), lambda i: (sample, 0, 0))],
        out_specs=(full(HALF, SEQ), full(HALF, SEQ)),
        compiler_params=pltpu.CompilerParams(vmem_limit_bytes=VMEM_LIMIT),
        cost_estimate=pl.CostEstimate(
            flops=2 * D * WIN * QROWS, bytes_accessed=2 * (QROWS * WIN + D * WIN) + 8 * HALF * SEQ, transcendentals=0
        ),
        name="project",
    )(m, att, w, x)


def finish_kernel(own_ref, other_ref, *refs):
    out_ref = refs[-1]
    out_ref[0] = (own_ref[...] + other_ref[...].astype(f32)).astype(bf16)


def finish(own, other, sample, before=None):
    rows = 288
    spec = pl.BlockSpec((rows, SEQ), lambda i: (i, 0))
    args = [own, other] + ([before] if before is not None else [])
    return pl.pallas_call(
        finish_kernel,
        grid=(HALF // rows,),
        out_shape=shape((2, HALF, SEQ), bf16),
        in_specs=[spec, spec] + ([ANY] if before is not None else []),
        out_specs=pl.BlockSpec((1, rows, SEQ), lambda i: (sample, i, 0)),
        input_output_aliases={2: 0} if before is not None else {},
        compiler_params=pltpu.CompilerParams(vmem_limit_bytes=VMEM_LIMIT),
        cost_estimate=pl.CostEstimate(flops=HALF * SEQ, bytes_accessed=8 * HALF * SEQ, transcendentals=0),
        name="finish",
    )(*args)


def text_kernel(m_ref, co_ref, cr_ref, w_ref, wo_ref, part_ref, last_ref, x_ref):
    m = m_ref[0]
    own = co_ref[...].astype(f32)
    other = cr_ref[...].astype(f32)
    first = jnp.where(m == 0, own, other)
    second = jnp.where(m == 0, other, own)
    x_ref[:, pl.ds(0, HALF)] = first
    x_ref[:, pl.ds(HALF, HALF)] = second
    x = x_ref[...]
    center = jnp.sum(x, axis=1, keepdims=True) * (1.0 / D)
    centred = x - center
    spread = jnp.sum(centred * centred, axis=1, keepdims=True) * (1.0 / D)
    normed = (centred * lax.rsqrt(spread + 1e-06)).astype(bf16)
    q = dot(normed, w_ref[0], NT).astype(bf16).astype(f32)
    k = dot(normed, w_ref[1], NT).astype(bf16)
    v = dot(normed, w_ref[2], NT).astype(bf16)
    row = lax.broadcasted_iota(jnp.int32, (16, HALF), 0)
    lane = lax.broadcasted_iota(jnp.int32, (16, HALF), 1)
    low = (row % 8) * HEAD_DIM
    of_head = (lane >= low) & (lane < low + HEAD_DIM)
    q_last = jnp.where(row < 8, q[TEXT - 1 : TEXT], q[2 * TEXT - 1 : 2 * TEXT])
    q_head = jnp.where(of_head, q_last, 0.0).astype(bf16)
    s = dot(q_head, k, NT) * HEAD_DIM ** (-0.5)
    key = lax.broadcasted_iota(jnp.int32, (16, 2 * TEXT), 1)
    of = lax.broadcasted_iota(jnp.int32, (16, 2 * TEXT), 0)
    s = jnp.where((key < TEXT) == (of < 8), s, -1e30)
    e = jnp.exp(s - jnp.max(s, axis=1, keepdims=True))
    weight = (e / jnp.sum(e, axis=1, keepdims=True)).astype(bf16)
    o = jnp.where(of_head, dot(weight, v), 0.0)
    a = jnp.sum(jnp.where(row < 8, o, 0.0), axis=0, keepdims=True)
    b = jnp.sum(jnp.where(row < 8, 0.0, o), axis=0, keepdims=True)
    att = jnp.where(lax.broadcasted_iota(jnp.int32, (8, HALF), 0) == 2, a, b).astype(bf16)
    part_ref[...] = dot(att, wo_ref[...])
    at = lax.broadcasted_iota(jnp.int32, (8, D), 0)
    last_ref[...] = jnp.where(at == 2, x[TEXT - 1 : TEXT], x[2 * TEXT - 1 : 2 * TEXT])


def text_tower(m, own, other, w, wo):
    return call(
        text_kernel,
        (shape((8, D), f32), shape((8, D), f32)),
        [m, own, other, w, wo],
        specs=[SM, VM, VM, VM, VM],
        scratch=[pltpu.VMEM((2 * TEXT, D), f32)],
        flops=0,
        bytes_accessed=0,
        name="text_tower",
    )


def embed_rows(features, out_ref):
    total = jnp.sum(features * features, axis=1, keepdims=True)
    embedded = (features * lax.rsqrt(total + 1e-06)).astype(bf16)
    for which in range(4):
        out_ref[:, pl.ds(D * which, D)] = embedded[which : which + 1]


def embed_kernel(base_ref, mine_ref, other_ref, out_ref):
    embed_rows(base_ref[...] + (mine_ref[...] + other_ref[...]), out_ref)


def embed(base, mine, other):
    return call(embed_kernel, shape((1, MESSAGE), bf16), [base, mine, other], bytes_accessed=100000, name="embed")


def pool_kernel(m_ref, a_ref, b_ref, ma_ref, mb_ref, w_ref, text_ref, last_ref, part_ref, base_ref):
    row = lax.broadcasted_iota(jnp.int32, (8, WIN), 0)
    sums = jnp.where(row == 0, a_ref[...], b_ref[...]) * (1.0 / SEQ)
    high = sums.astype(bf16)
    rest = sums - high.astype(f32)
    mid = rest.astype(bf16)
    low = (rest - mid.astype(f32)).astype(bf16)
    w = w_ref[...]
    pooled = dot(high, w, NT) + (dot(mid, w, NT) + dot(low, w, NT))
    image_row = lax.broadcasted_iota(jnp.int32, (8, D), 0) < 2
    part_ref[...] = jnp.where(image_row, pooled, text_ref[...])
    m = m_ref[0]
    at = lax.broadcasted_iota(jnp.int32, (8, HALF), 0)
    own = jnp.where(at == 0, ma_ref[:, pl.ds(0, HALF)], mb_ref[:, pl.ds(0, HALF)])
    other = jnp.where(at == 0, ma_ref[:, pl.ds(HALF + 64, HALF)], mb_ref[:, pl.ds(HALF + 64, HALF)])
    image_row = at < 2
    base_ref[:, pl.ds(0, HALF)] = jnp.where(image_row, jnp.where(m == 0, own, other), last_ref[:, pl.ds(0, HALF)])
    base_ref[:, pl.ds(HALF, HALF)] = jnp.where(image_row, jnp.where(m == 0, other, own), last_ref[:, pl.ds(HALF, HALF)])


def pool(m, sum_a, sum_b, mean_a, mean_b, w, text_part, text_last):
    return call(
        pool_kernel,
        (shape((8, D), f32), shape((8, D), f32)),
        [m, sum_a, sum_b, mean_a, mean_b, w, text_part, text_last],
        specs=[SM] + [VM] * 7,
        flops=3 * 2 * 8 * WIN * D,
        bytes_accessed=2 * D * WIN,
        name="pool",
    )


def pair_kernel(m_ref, own_ref, *refs):
    pieces, (image_ref, text_ref, all_ref) = refs[:8], refs[8:]
    for n, piece in enumerate(pieces):
        all_ref[pl.ds(16 * n, 16), :] = piece[...]
    own = own_ref[...].astype(f32)
    row = lax.broadcasted_iota(jnp.int32, (8, D), 0)
    at_row = lax.broadcasted_iota(jnp.int32, (8, 128), 0)
    at_col = lax.broadcasted_iota(jnp.int32, (8, 128), 1)
    for mine, others, out_ref in ((0, 2, image_ref), (2, 0, text_ref)):
        rows = jnp.where(row == 0, own[:, D * mine : D * mine + D], own[:, D * mine + D : D * mine + 2 * D]).astype(bf16)
        grad = None
        for which in range(2):
            each = all_ref[:, pl.ds(D * (others + which), D)]
            logit = 10.0 * dot(rows, each, NT) - 1.0
            label = jnp.where((at_row == which) & (at_col == 0), 1.0, -1.0)
            weight = (-10.0 * label / (1.0 + jnp.exp(label * logit))).astype(bf16)
            term = dot(weight, each)
            grad = term if grad is None else grad + term
        out_ref[...] = jnp.where(m_ref[0] == 0, grad[0:2, 0:HALF], grad[0:2, HALF:])


def pair_grads(m, own, pieces):
    return call(
        pair_kernel,
        (shape((2, HALF), f32), shape((2, HALF), f32)),
        [m, own] + pieces,
        specs=[SM] + [VM] * 9,
        scratch=[pltpu.VMEM((128, MESSAGE), bf16)],
        flops=4 * 2 * 8 * 256 * D,
        bytes_accessed=2 * 128 * MESSAGE,
        name="pair_grads",
    )


def gather_rest(pair):
    quad = jnp.concatenate([pair, shift(pair, "z", 8, 4)], axis=0)
    along_z = jnp.concatenate([quad] + [shift(quad, "z", 8, k) for k in (1, 2, 7)], axis=0)
    near = [along_z] + [shift(along_z, "x", 4, k) for k in (1, 3, 2)]
    return near + [shift(piece, "c", 2, 1) for piece in near]


def weight_slab(image_qkv, image_out):
    turned = jnp.transpose(image_out)
    return jnp.concatenate(
        [
            jnp.concatenate([image_qkv[:, 0], image_qkv[:, 2]], axis=1),
            jnp.concatenate([image_qkv[:, 1], turned], axis=1),
        ],
        axis=0,
    )


def gather_weights(slab, over_w, behind):
    pair = after(jnp.concatenate([slab[:9], over_w[:9], slab[9:], over_w[9:]], axis=0), behind)
    over_z = shift(pair, "z", 8, 4)
    quad = after(jnp.concatenate([pair[:18], over_z[:18], pair[18:], over_z[18:]], axis=0))
    others = [shift(quad, "z", 8, 1), shift(pair, "z", 8, 2), shift(pair, "z", 8, 6), shift(quad, "z", 8, 7)]
    halves = []
    for half in range(2):
        parts = [part[part.shape[0] // 2 * half : part.shape[0] // 2 * (half + 1)] for part in [quad] + others]
        halves.append(jnp.concatenate(parts, axis=0))
    return jnp.concatenate(halves, axis=1)


def row_order(z, x, w, c):
    at = np.arange(D)
    r, rest = at % 9, at // 9
    wr, rest = rest % 2, rest // 2
    z4, rest = rest % 2, rest // 2
    zr, rest = np.array(Z_STEPS)[rest % 4] + 4 * z4, rest // 4
    xr, cr = rest % 4, rest // 4
    device = (((z + zr) % 8 * 4 + (x + xr) % 4) * 2 + (w + wr) % 2) * 2 + (c + cr) % 2
    return (device * 9 + r).astype(jnp.int32).reshape(1, D)


def on_device(patches, image_qkv, image_out, captions, text_qkv, text_out):
    z, x, w, c, m = (lax.axis_index(a) for a in ("z", "x", "w", "c", "m"))
    m_arr = jnp.reshape(m, (1,)).astype(jnp.int32)
    order = row_order(z, x, w, c)
    norm_order = (order + HALF * m) % D

    own = jnp.transpose(patches, (0, 2, 1))
    captions2 = captions.reshape(2 * TEXT, HALF)
    captions_other = shift(captions2, "m", 2, 1)
    slab = weight_slab(image_qkv, image_out)
    over_w = shift(slab, "w", 2, 1)
    other0 = shift(after(own[0:1], captions_other, over_w), "m", 2, 1)
    piece = gather_weights(slab, over_w, captions_other)
    text_part, text_last = text_tower(
        m_arr, captions2, after(captions_other, over_w), jnp.transpose(text_qkv, (1, 2, 0)), text_out
    )

    piece = after(piece, text_part)
    next_piece, last_piece = shift(piece, "x", 4, 1), shift(piece, "x", 4, 3)
    other1 = shift(after(own[1:2], other0), "m", 2, 1)
    normed0, mean0 = norm_patches(norm_order, own, other0, 0)
    far_a = shift(last_piece[: SPLIT[0]], "x", 4, 3)
    far_b = shift(next_piece[SPLIT[0] :], "x", 4, 1)
    near = [piece, next_piece, far_a, far_b, last_piece]
    pieces = near + [shift(after(block, normed0), "c", 2, 1) for block in near]
    normed1, mean1 = norm_patches(norm_order, own, other1, 1)

    att0, sum0 = attend(after(normed0, normed1), pieces)
    wo = order_out(after(order, sum0), pieces)
    own0, send0 = project(m_arr, att0, wo, own, 0)
    got0 = shift(send0, "m", 2, 1)
    att1, sum1 = attend(after(normed1, send0), pieces)
    part, base = pool(m_arr, sum0, sum1, mean0, mean1, wo, text_part, text_last)
    own1, send1 = project(m_arr, after(att1, part), wo, own, 1)
    hidden = finish(own0, after(got0, part, send1), 0)
    embedded = embed(base, part, after(shift(part, "m", 2, 1), hidden))
    embedded_w = shift(embedded, "w", 2, 1)
    got1 = shift(after(send1, embedded_w), "m", 2, 1)
    every = gather_rest(jnp.concatenate([embedded, embedded_w], axis=0))

    image_grad, text_grad = pair_grads(m_arr, embedded, every)
    hidden = finish(own1, got1, 1, hidden)
    return jnp.transpose(hidden, (0, 2, 1)), image_grad, text_grad


def solution(mesh):
    split = Mesh(mesh.devices.reshape(8, 4, 2, 2, 2), ("z", "x", "w", "c", "m"))
    batch = ("z", "x", "w", "c")
    return jax.shard_map(
        on_device,
        mesh=split,
        in_specs=(
            P(batch, None, "m"),
            P(batch, None, "m"),
            P("m", batch),
            P(batch, None, "m"),
            P(None, None, "m"),
            P("m", None),
        ),
        out_specs=(P(batch, None, "m"), P(batch, "m"), P(batch, "m")),
        check_vma=False,
    )
```

```python
import functools
import math

import jax
import jax.numpy as jnp
import numpy as np
from jax import lax
from jax.experimental import pallas as pl
from jax.experimental.pallas import tpu as pltpu
from jax.sharding import Mesh, PartitionSpec as P

D = 1152
HALF = 576
HEAD_DIM = 72
SEQ = 729
ROWS = 768
QROWS = 736
QBLOCK = 368
TEXT = 64
COLS = 2304
QKV = 1792
WO_AT = 1664
WIN = 640
PIECE = 144
Z_STEPS = (0, 1, 2, 7)
MESSAGE = 4 * D

f32 = jnp.float32
bf16 = jnp.bfloat16
NT = (((1,), (1,)), ((), ()))
TN = (((0,), (0,)), ((), ()))
VMEM_LIMIT = 24 * 1024 * 1024


def dot(a, b, dims=(((1,), (0,)), ((), ()))):
    return lax.dot_general(a, b, dims, preferred_element_type=f32)


def call(body, outs, args, specs=None, out_specs=None, scratch=(), flops=0, bytes_accessed=0, name=None, aliases=None):
    whole = pl.BlockSpec(memory_space=pltpu.VMEM)
    return pl.pallas_call(
        body,
        out_shape=outs,
        in_specs=specs if specs is not None else [whole] * len(args),
        out_specs=out_specs if out_specs is not None else jax.tree.map(lambda _: whole, outs),
        scratch_shapes=list(scratch),
        compiler_params=pltpu.CompilerParams(vmem_limit_bytes=VMEM_LIMIT),
        cost_estimate=pl.CostEstimate(flops=int(flops), bytes_accessed=int(bytes_accessed), transcendentals=0),
        input_output_aliases=aliases or {},
        name=name,
    )(*args)


def shape(dims, kind):
    return jax.ShapeDtypeStruct(dims, kind)


VM = pl.BlockSpec(memory_space=pltpu.VMEM)
SM = pl.BlockSpec(memory_space=pltpu.SMEM)
ANY = pl.BlockSpec(memory_space=pl.ANY)


def shift(value, axis, size, step):
    return lax.ppermute(value, axis, [((i + step) % size, i) for i in range(size)])


def shift_wm(value):
    return lax.ppermute(value, ("w", "m"), [(3 - i, i) for i in range(4)])


def after(value, *others):
    return lax.optimization_barrier((value,) + others)[0]


def norm_kernel(idx_ref, xo_ref, xr_ref, out_ref, mean_ref, pad_ref, turned_ref):
    xo = xo_ref[0].astype(f32)
    xr = xr_ref[0].astype(f32)
    center = (jnp.sum(xo, axis=0, keepdims=True) + jnp.sum(xr, axis=0, keepdims=True)) * (1.0 / D)
    co = xo - center
    cr = xr - center
    spread = (jnp.sum(co * co, axis=0, keepdims=True) + jnp.sum(cr * cr, axis=0, keepdims=True)) * (1.0 / D)
    scale = lax.rsqrt(spread + 1e-06)
    pad_ref[:, pl.ds(640, 128)] = jnp.zeros((D, 128), bf16)
    pad_ref[pl.ds(0, HALF), pl.ds(0, SEQ)] = (co * scale).astype(bf16)
    pad_ref[pl.ds(HALF, HALF), pl.ds(0, SEQ)] = (cr * scale).astype(bf16)
    turned_ref[...] = jnp.transpose(pad_ref[...])
    for at in range(0, D, 256):
        size = min(256, D - at)
        rows = lax.broadcasted_iota(jnp.int32, (D, size), 0)
        pick = (rows == idx_ref[:, pl.ds(at, size)]).astype(f32).astype(bf16)
        out_ref[:, pl.ds(at, size)] = dot(turned_ref[...], pick).astype(bf16)
    ones = jnp.ones((8, SEQ), bf16)
    mean_ref[:, pl.ds(0, HALF)] = dot(ones, xo_ref[0], NT) * (1.0 / SEQ)
    mean_ref[:, pl.ds(HALF + 64, HALF)] = dot(ones, xr_ref[0], NT) * (1.0 / SEQ)


def norm_patches(idx, own, other, sample):
    sample_spec = pl.BlockSpec((1, HALF, SEQ), lambda i: (sample, 0, 0))
    other_spec = pl.BlockSpec((1, HALF, SEQ), lambda i: (0, 0, 0))
    return pl.pallas_call(
        norm_kernel,
        grid=(1,),
        out_shape=(shape((ROWS, D), bf16), shape((8, 1280), f32)),
        in_specs=[pl.BlockSpec((1, D), lambda i: (0, 0)), sample_spec, other_spec],
        out_specs=(pl.BlockSpec((ROWS, D), lambda i: (0, 0)), pl.BlockSpec((8, 1280), lambda i: (0, 0))),
        scratch_shapes=[pltpu.VMEM((D, ROWS), bf16), pltpu.VMEM((ROWS, D), bf16)],
        compiler_params=pltpu.CompilerParams(vmem_limit_bytes=VMEM_LIMIT),
        cost_estimate=pl.CostEstimate(flops=2 * ROWS * D * D, bytes_accessed=4 * ROWS * D, transcendentals=0),
        name="norm_patches",
    )(idx, own, other)


def order_kernel(idx_ref, *refs):
    pieces, (out_ref, mixed_ref, pick_ref, sems) = refs[:8], refs[8:]
    copies = []
    for n, piece in enumerate(pieces):
        rows = mixed_ref.at[pl.ds(PIECE * n, PIECE), :]
        copies.append(pltpu.make_async_copy(piece.at[:, pl.ds(WO_AT - D, WIN)], rows, sems.at[n]))
    for copy in copies:
        copy.start()
    for copy in copies:
        copy.wait()
    rows = lax.broadcasted_iota(jnp.int32, (D, D), 0)
    pick_ref[...] = (rows == idx_ref[...]).astype(f32).astype(bf16)
    for at in range(0, WIN, 256):
        size = min(256, WIN - at)
        out_ref[:, pl.ds(at, size)] = dot(pick_ref[...], mixed_ref[:, pl.ds(at, size)]).astype(bf16)


def order_out(idx, pieces):
    return call(
        order_kernel,
        shape((D, WIN), bf16),
        [idx] + pieces,
        specs=[VM] + [ANY] * 8,
        scratch=[pltpu.VMEM((D, WIN), bf16), pltpu.VMEM((D, D), bf16), pltpu.SemaphoreType.DMA((8,))],
        flops=2 * D * D * WIN,
        bytes_accessed=4 * D * WIN,
        name="order_out",
    )


def attend_kernel(x_ref, *refs):
    pieces, (att_ref, sum_ref, w_ref, qkv_ref, sems) = refs[:16], refs[16:]
    copies = []
    for n, piece in enumerate(pieces):
        rows = pl.ds(PIECE * (n % 8), PIECE)
        if n < 8:
            copies.append(pltpu.make_async_copy(piece, w_ref.at[rows, pl.ds(0, D)], sems.at[n]))
        else:
            part = piece.at[:, pl.ds(0, QKV - D)]
            copies.append(pltpu.make_async_copy(part, w_ref.at[rows, pl.ds(D, QKV - D)], sems.at[n]))
    for copy in copies:
        copy.start()
    att_ref[...] = jnp.zeros_like(att_ref)
    for copy in copies[:8]:
        copy.wait()

    q_scale = math.log2(math.e) * HEAD_DIM ** (-0.5)

    def project(n, carry):
        at = pl.multiple_of(n * 256, 256)
        lane = at + lax.broadcasted_iota(jnp.int32, (1, 256), 1)
        scale = jnp.where(lane < HALF, q_scale, 1.0).astype(f32)
        qkv_ref[:, pl.ds(at, 256)] = (dot(x_ref[...], w_ref[:, pl.ds(at, 256)]) * scale).astype(bf16)
        return carry

    lax.fori_loop(0, D // 256, project, 0)
    for copy in copies[8:]:
        copy.wait()
    lax.fori_loop(D // 256, QKV // 256, project, 0)

    lane = lax.broadcasted_iota(jnp.int32, (1, 256), 1)

    def between(low, high):
        return ((lane >= low) & (lane < high)).astype(f32)

    last = (lane == 255).astype(f32)
    key_row = lax.broadcasted_iota(jnp.int32, (ROWS, 1), 0)
    key_bias = jnp.where(key_row >= SEQ, -1e30, 0.0).astype(f32) * last

    def pair(p, carry):
        at = pl.multiple_of(p * 128, 128)
        q_at = 16 * p
        v_at = 64 + 16 * p
        k_win = qkv_ref[:, pl.ds(D + at, 256)] * (1.0 - last).astype(bf16) + key_bias.astype(bf16)
        v_win = qkv_ref[:, pl.ds(512 + at, 256)]
        values = []
        for h in range(2):
            low = v_at + HEAD_DIM * h
            ones = (lane == h).astype(f32).astype(bf16)
            values.append(v_win * between(low, low + HEAD_DIM).astype(bf16) + ones)
        units = [(row, h) for row in range(0, QROWS, QBLOCK) for h in range(2)]
        scores, weights, totals = {}, {}, {}

        def score(u):
            row, h = units[u]
            low = q_at + HEAD_DIM * h
            q_win = qkv_ref[pl.ds(row, QBLOCK), pl.ds(at, 256)]
            q = q_win * between(low, low + HEAD_DIM).astype(bf16) + last.astype(bf16)
            scores[u] = dot(q, k_win, NT)

        def weigh(u):
            s = scores.pop(u)
            weights[u] = jnp.exp2((s - jnp.max(s, axis=1, keepdims=True)).astype(bf16))

        def mix(u):
            row, h = units[u]
            totals[u] = dot(weights.pop(u), values[h])

        def store(u):
            row = units[u][0]
            total = totals.pop(u) + totals.pop(u + 1)
            inverse = jnp.where(lane < v_at + HEAD_DIM, 1.0 / total[:, 0:1], 1.0 / total[:, 1:2])
            mixed = (total * inverse * between(v_at, v_at + 2 * HEAD_DIM)).astype(bf16)
            att_ref[pl.ds(row, QBLOCK), pl.ds(at, 256)] = att_ref[pl.ds(row, QBLOCK), pl.ds(at, 256)] + mixed

        score(0)
        for u in range(len(units)):
            if u + 1 < len(units):
                score(u + 1)
            weigh(u)
            mix(u)
            if u % 2 == 1:
                store(u - 1)
        return carry

    lax.fori_loop(0, 4, pair, 0)
    valid = (lax.broadcasted_iota(jnp.int32, (8, QROWS), 1) < SEQ).astype(f32).astype(bf16)
    sum_ref[...] = dot(valid, att_ref[...])


def attend(x, pieces):
    return call(
        attend_kernel,
        (shape((QROWS, WIN), bf16), shape((8, WIN), f32)),
        [x] + pieces,
        specs=[VM] + [ANY] * 16,
        scratch=[
            pltpu.VMEM((D, QKV), bf16),
            pltpu.VMEM((ROWS, QKV), bf16),
            pltpu.SemaphoreType.DMA((16,)),
        ],
        flops=2 * ROWS * D * QKV + 8 * 4 * ROWS * ROWS * 256,
        bytes_accessed=2 * (D * QKV + ROWS * D + QROWS * WIN),
        name="attend",
    )


def project_kernel(m_ref, att_ref, w_ref, x_ref, own_ref, send_ref):
    m = m_ref[0]
    mine = w_ref[pl.ds(pl.multiple_of(m * HALF, HALF), HALF), :]
    theirs = w_ref[pl.ds(pl.multiple_of((1 - m) * HALF, HALF), HALF), :]
    send_ref[...] = dot(theirs, att_ref[...], NT)[:, :SEQ].astype(bf16)
    own_ref[...] = dot(mine, att_ref[...], NT)[:, :SEQ] + x_ref[0].astype(f32)


def project(m, att, w, x, sample):
    full = lambda *dims: pl.BlockSpec(dims, lambda i: (0,) * len(dims))
    return pl.pallas_call(
        project_kernel,
        grid=(1,),
        out_shape=(shape((HALF, SEQ), f32), shape((HALF, SEQ), bf16)),
        in_specs=[SM, full(QROWS, WIN), full(D, WIN), pl.BlockSpec((1, HALF, SEQ), lambda i: (sample, 0, 0))],
        out_specs=(full(HALF, SEQ), full(HALF, SEQ)),
        compiler_params=pltpu.CompilerParams(vmem_limit_bytes=VMEM_LIMIT),
        cost_estimate=pl.CostEstimate(
            flops=2 * D * WIN * QROWS, bytes_accessed=2 * (QROWS * WIN + D * WIN) + 8 * HALF * SEQ, transcendentals=0
        ),
        name="project",
    )(m, att, w, x)


def finish_kernel(own_ref, other_ref, *refs):
    out_ref = refs[-1]
    out_ref[0] = (own_ref[...] + other_ref[...].astype(f32)).astype(bf16)


def finish(own, other, sample, before=None):
    rows = 288
    spec = pl.BlockSpec((rows, SEQ), lambda i: (i, 0))
    args = [own, other] + ([before] if before is not None else [])
    return pl.pallas_call(
        finish_kernel,
        grid=(HALF // rows,),
        out_shape=shape((2, HALF, SEQ), bf16),
        in_specs=[spec, spec] + ([ANY] if before is not None else []),
        out_specs=pl.BlockSpec((1, rows, SEQ), lambda i: (sample, i, 0)),
        input_output_aliases={2: 0} if before is not None else {},
        compiler_params=pltpu.CompilerParams(vmem_limit_bytes=VMEM_LIMIT),
        cost_estimate=pl.CostEstimate(flops=HALF * SEQ, bytes_accessed=8 * HALF * SEQ, transcendentals=0),
        name="finish",
    )(*args)


def text_kernel(m_ref, co_ref, cr_ref, w_ref, wo_ref, part_ref, last_ref, x_ref):
    m = m_ref[0]
    own = co_ref[...].astype(f32)
    other = cr_ref[...].astype(f32)
    first = jnp.where(m == 0, own, other)
    second = jnp.where(m == 0, other, own)
    x_ref[:, pl.ds(0, HALF)] = first
    x_ref[:, pl.ds(HALF, HALF)] = second
    x = x_ref[...]
    center = jnp.sum(x, axis=1, keepdims=True) * (1.0 / D)
    centred = x - center
    spread = jnp.sum(centred * centred, axis=1, keepdims=True) * (1.0 / D)
    normed = (centred * lax.rsqrt(spread + 1e-06)).astype(bf16)
    q = dot(normed, w_ref[0], NT).astype(bf16).astype(f32)
    k = dot(normed, w_ref[1], NT).astype(bf16)
    v = dot(normed, w_ref[2], NT).astype(bf16)
    row = lax.broadcasted_iota(jnp.int32, (16, HALF), 0)
    lane = lax.broadcasted_iota(jnp.int32, (16, HALF), 1)
    low = (row % 8) * HEAD_DIM
    of_head = (lane >= low) & (lane < low + HEAD_DIM)
    q_last = jnp.where(row < 8, q[TEXT - 1 : TEXT], q[2 * TEXT - 1 : 2 * TEXT])
    q_head = jnp.where(of_head, q_last, 0.0).astype(bf16)
    s = dot(q_head, k, NT) * HEAD_DIM ** (-0.5)
    key = lax.broadcasted_iota(jnp.int32, (16, 2 * TEXT), 1)
    of = lax.broadcasted_iota(jnp.int32, (16, 2 * TEXT), 0)
    s = jnp.where((key < TEXT) == (of < 8), s, -1e30)
    e = jnp.exp(s - jnp.max(s, axis=1, keepdims=True))
    weight = (e / jnp.sum(e, axis=1, keepdims=True)).astype(bf16)
    o = jnp.where(of_head, dot(weight, v), 0.0)
    a = jnp.sum(jnp.where(row < 8, o, 0.0), axis=0, keepdims=True)
    b = jnp.sum(jnp.where(row < 8, 0.0, o), axis=0, keepdims=True)
    att = jnp.where(lax.broadcasted_iota(jnp.int32, (8, HALF), 0) == 2, a, b).astype(bf16)
    part_ref[...] = dot(att, wo_ref[...])
    at = lax.broadcasted_iota(jnp.int32, (8, D), 0)
    last_ref[...] = jnp.where(at == 2, x[TEXT - 1 : TEXT], x[2 * TEXT - 1 : 2 * TEXT])


def text_tower(m, own, other, w, wo):
    return call(
        text_kernel,
        (shape((8, D), f32), shape((8, D), f32)),
        [m, own, other, w, wo],
        specs=[SM, VM, VM, VM, VM],
        scratch=[pltpu.VMEM((2 * TEXT, D), f32)],
        flops=0,
        bytes_accessed=0,
        name="text_tower",
    )


def embed_kernel(mine_ref, other_ref, near_ref, far_ref, out_ref):
    for at, features in enumerate((mine_ref[...] + other_ref[...], near_ref[...] + far_ref[...])):
        total = jnp.sum(features * features, axis=1, keepdims=True)
        embedded = (features * lax.rsqrt(total + 1e-06)).astype(bf16)
        for which in range(4):
            out_ref[pl.ds(at, 1), pl.ds(D * which, D)] = embedded[which : which + 1]


def embed(parts):
    return call(embed_kernel, shape((2, MESSAGE), bf16), parts, bytes_accessed=200000, name="embed")


def pool_kernel(m_ref, a_ref, b_ref, ma_ref, mb_ref, w_ref, text_ref, last_ref, part_ref):
    row = lax.broadcasted_iota(jnp.int32, (8, WIN), 0)
    sums = jnp.where(row == 0, a_ref[...], b_ref[...]) * (1.0 / SEQ)
    high = sums.astype(bf16)
    rest = sums - high.astype(f32)
    mid = rest.astype(bf16)
    low = (rest - mid.astype(f32)).astype(bf16)
    w = w_ref[...]
    pooled = dot(high, w, NT) + (dot(mid, w, NT) + dot(low, w, NT))
    m = m_ref[0]
    at = lax.broadcasted_iota(jnp.int32, (8, HALF), 0)
    own = jnp.where(at == 0, ma_ref[:, pl.ds(0, HALF)], mb_ref[:, pl.ds(0, HALF)])
    other = jnp.where(at == 0, ma_ref[:, pl.ds(HALF + 64, HALF)], mb_ref[:, pl.ds(HALF + 64, HALF)])
    first = jnp.where(m == 0, 1.0, 0.0)
    for half, mean in ((0, own), (HALF, other)):
        part = jnp.where(at < 2, pooled[:, half : half + HALF], text_ref[:, pl.ds(half, HALF)])
        part_ref[:, pl.ds(half, HALF)] = part + first * jnp.where(at < 2, mean, last_ref[:, pl.ds(half, HALF)])


def pool(m, sum_a, sum_b, mean_a, mean_b, w, text_part, text_last):
    return call(
        pool_kernel,
        shape((8, D), f32),
        [m, sum_a, sum_b, mean_a, mean_b, w, text_part, text_last],
        specs=[SM] + [VM] * 7,
        flops=3 * 2 * 8 * WIN * D,
        bytes_accessed=2 * D * WIN,
        name="pool",
    )


def pair_kernel(m_ref, own_ref, *refs):
    pieces, (image_ref, text_ref, all_ref) = refs[:8], refs[8:]
    for n, piece in enumerate(pieces):
        all_ref[pl.ds(16 * n, 16), :] = piece[...]
    own = own_ref[...].astype(f32)[0:1]
    row = lax.broadcasted_iota(jnp.int32, (8, D), 0)
    at_row = lax.broadcasted_iota(jnp.int32, (8, 128), 0)
    at_col = lax.broadcasted_iota(jnp.int32, (8, 128), 1)
    for mine, others, out_ref in ((0, 2, image_ref), (2, 0, text_ref)):
        rows = jnp.where(row == 0, own[:, D * mine : D * mine + D], own[:, D * mine + D : D * mine + 2 * D]).astype(bf16)
        grad = None
        for which in range(2):
            each = all_ref[:, pl.ds(D * (others + which), D)]
            logit = 10.0 * dot(rows, each, NT) - 1.0
            label = jnp.where((at_row == which) & (at_col == 0), 1.0, -1.0)
            weight = (-10.0 * label / (1.0 + jnp.exp(label * logit))).astype(bf16)
            term = dot(weight, each)
            grad = term if grad is None else grad + term
        out_ref[...] = jnp.where(m_ref[0] == 0, grad[0:2, 0:HALF], grad[0:2, HALF:])


def pair_grads(m, own, pieces):
    return call(
        pair_kernel,
        (shape((2, HALF), f32), shape((2, HALF), f32)),
        [m, own] + pieces,
        specs=[SM] + [VM] * 9,
        scratch=[pltpu.VMEM((128, MESSAGE), bf16)],
        flops=4 * 2 * 8 * 256 * D,
        bytes_accessed=2 * 128 * MESSAGE,
        name="pair_grads",
    )


def gather_rest(pair):
    quad = jnp.concatenate([pair, shift(pair, "z", 8, 4)], axis=0)
    along_z = jnp.concatenate([quad] + [shift(quad, "z", 8, k) for k in (1, 2, 7)], axis=0)
    near = [along_z] + [shift(along_z, "x", 4, k) for k in (1, 3, 2)]
    return near + [shift(piece, "c", 2, 1) for piece in near]


def weight_slab(image_qkv, image_out):
    turned = jnp.transpose(image_out)
    return jnp.concatenate(
        [
            jnp.concatenate([image_qkv[:, 0], image_qkv[:, 2]], axis=1),
            jnp.concatenate([image_qkv[:, 1], turned], axis=1),
        ],
        axis=0,
    )


def gather_weights(slab, over_w, behind_pair, behind_quad):
    pair = after(jnp.concatenate([slab[:9], over_w[:9], slab[9:], over_w[9:]], axis=0), behind_pair)
    over_z = shift(pair, "z", 8, 4)
    quad = after(jnp.concatenate([pair[:18], over_z[:18], pair[18:], over_z[18:]], axis=0), behind_quad)
    others = [shift(quad, "z", 8, 1), shift(pair, "z", 8, 2), shift(pair, "z", 8, 6), shift(quad, "z", 8, 7)]
    halves = []
    for half in range(2):
        parts = [part[part.shape[0] // 2 * half : part.shape[0] // 2 * (half + 1)] for part in [quad] + others]
        halves.append(jnp.concatenate(parts, axis=0))
    return halves


def row_order(z, x, w, c):
    at = np.arange(D)
    r, rest = at % 9, at // 9
    wr, rest = rest % 2, rest // 2
    z4, rest = rest % 2, rest // 2
    zr, rest = np.array(Z_STEPS)[rest % 4] + 4 * z4, rest // 4
    xr, cr = rest % 4, rest // 4
    device = (((z + zr) % 8 * 4 + (x + xr) % 4) * 2 + (w + wr) % 2) * 2 + (c + cr) % 2
    return (device * 9 + r).astype(jnp.int32).reshape(1, D)


def on_device(patches, image_qkv, image_out, captions, text_qkv, text_out):
    z, x, w, c, m = (lax.axis_index(a) for a in ("z", "x", "w", "c", "m"))
    m_arr = jnp.reshape(m, (1,)).astype(jnp.int32)
    order = row_order(z, x, w, c)
    norm_order = (order + HALF * m) % D

    own = jnp.transpose(patches, (0, 2, 1))
    captions2 = captions.reshape(2 * TEXT, HALF)
    captions_other = shift(captions2, "m", 2, 1)
    slab = weight_slab(image_qkv, image_out)
    over_w = shift(slab, "w", 2, 1)
    other0 = shift(after(own[0:1], captions_other, over_w), "m", 2, 1)
    text_part, text_last = text_tower(
        m_arr, captions2, after(captions_other, over_w), jnp.transpose(text_qkv, (1, 2, 0)), text_out
    )

    qv, ko = gather_weights(slab, over_w, captions_other, text_part)

    next_qv, last_qv = shift(qv, "x", 4, 1), shift(qv, "x", 4, 3)
    next_ko, last_ko = shift(ko, "x", 4, 1), shift(ko, "x", 4, 3)
    other1 = shift(after(own[1:2], other0), "m", 2, 1)
    normed0, mean0 = norm_patches(norm_order, own, other0, 0)
    far_qv = shift(after(last_qv, normed0), "x", 4, 3)
    far_ko = shift(next_ko, "x", 4, 1)
    near_qv = [qv, next_qv, far_qv, last_qv]
    near_ko = [ko, next_ko, far_ko, last_ko]
    all_qv = near_qv + [shift(after(block, normed0), "c", 2, 1) for block in near_qv]
    all_ko = near_ko + [shift(after(block, normed0), "c", 2, 1) for block in near_ko]
    normed1, mean1 = norm_patches(norm_order, own, other1, 1)
    wo = order_out(order, all_ko)

    att0, sum0 = attend(after(normed0, normed1, wo), all_qv + all_ko)
    own0, send0 = project(m_arr, att0, wo, own, 0)
    got0 = shift(send0, "m", 2, 1)
    att1, sum1 = attend(after(normed1, send0), all_qv + all_ko)
    part = pool(m_arr, sum0, sum1, mean0, mean1, wo, text_part, text_last)
    own1, send1 = project(m_arr, after(att1, part), wo, own, 1)
    hidden = finish(own0, after(got0, part, send1), 0)
    parts = [part, shift(part, "m", 2, 1), shift(part, "w", 2, 1), shift_wm(part)]
    embedded = embed([after(parts[0], hidden)] + parts[1:])
    got1 = shift(after(send1, embedded), "m", 2, 1)
    every = gather_rest(embedded)

    image_grad, text_grad = pair_grads(m_arr, embedded, every)
    hidden = finish(own1, got1, 1, hidden)
    return jnp.transpose(hidden, (0, 2, 1)), image_grad, text_grad


def solution(mesh):
    split = Mesh(mesh.devices.reshape(8, 4, 2, 2, 2), ("z", "x", "w", "c", "m"))
    batch = ("z", "x", "w", "c")
    return jax.shard_map(
        on_device,
        mesh=split,
        in_specs=(
            P(batch, None, "m"),
            P(batch, None, "m"),
            P("m", batch),
            P(batch, None, "m"),
            P(None, None, "m"),
            P("m", None),
        ),
        out_specs=(P(batch, None, "m"), P(batch, "m"), P(batch, "m")),
        check_vma=False,
    )
```

```python
import functools
import math

import jax
import jax.numpy as jnp
import numpy as np
from jax import lax
from jax.experimental import pallas as pl
from jax.experimental.pallas import tpu as pltpu
from jax.sharding import Mesh, PartitionSpec as P

D = 1152
HALF = 576
HEAD_DIM = 72
SEQ = 729
ROWS = 768
QROWS = 736
QBLOCK = 368
TEXT = 64
COLS = 2304
QKV = 1792
WO_AT = 1664
WIN = 640
PIECE = 144
Z_STEPS = (0, 1, 2, 7)
MESSAGE = 4 * D

f32 = jnp.float32
bf16 = jnp.bfloat16
NT = (((1,), (1,)), ((), ()))
TN = (((0,), (0,)), ((), ()))
VMEM_LIMIT = 24 * 1024 * 1024


def dot(a, b, dims=(((1,), (0,)), ((), ()))):
    return lax.dot_general(a, b, dims, preferred_element_type=f32)


def call(body, outs, args, specs=None, out_specs=None, scratch=(), flops=0, bytes_accessed=0, name=None, aliases=None):
    whole = pl.BlockSpec(memory_space=pltpu.VMEM)
    return pl.pallas_call(
        body,
        out_shape=outs,
        in_specs=specs if specs is not None else [whole] * len(args),
        out_specs=out_specs if out_specs is not None else jax.tree.map(lambda _: whole, outs),
        scratch_shapes=list(scratch),
        compiler_params=pltpu.CompilerParams(vmem_limit_bytes=VMEM_LIMIT),
        cost_estimate=pl.CostEstimate(flops=int(flops), bytes_accessed=int(bytes_accessed), transcendentals=0),
        input_output_aliases=aliases or {},
        name=name,
    )(*args)


def shape(dims, kind):
    return jax.ShapeDtypeStruct(dims, kind)


VM = pl.BlockSpec(memory_space=pltpu.VMEM)
SM = pl.BlockSpec(memory_space=pltpu.SMEM)
ANY = pl.BlockSpec(memory_space=pl.ANY)


def shift(value, axis, size, step):
    return lax.ppermute(value, axis, [((i + step) % size, i) for i in range(size)])


def shift_wm(value):
    return lax.ppermute(value, ("w", "m"), [(3 - i, i) for i in range(4)])


def after(value, *others):
    return lax.optimization_barrier((value,) + others)[0]


def norm_kernel(idx_ref, xo_ref, xr_ref, out_ref, mean_ref, pad_ref, turned_ref):
    xo = xo_ref[0].astype(f32)
    xr = xr_ref[0].astype(f32)
    center = (jnp.sum(xo, axis=0, keepdims=True) + jnp.sum(xr, axis=0, keepdims=True)) * (1.0 / D)
    co = xo - center
    cr = xr - center
    spread = (jnp.sum(co * co, axis=0, keepdims=True) + jnp.sum(cr * cr, axis=0, keepdims=True)) * (1.0 / D)
    scale = lax.rsqrt(spread + 1e-06)
    pad_ref[:, pl.ds(640, 128)] = jnp.zeros((D, 128), bf16)
    pad_ref[pl.ds(0, HALF), pl.ds(0, SEQ)] = (co * scale).astype(bf16)
    pad_ref[pl.ds(HALF, HALF), pl.ds(0, SEQ)] = (cr * scale).astype(bf16)
    turned_ref[...] = jnp.transpose(pad_ref[...])
    for at in range(0, D, 256):
        size = min(256, D - at)
        rows = lax.broadcasted_iota(jnp.int32, (D, size), 0)
        pick = (rows == idx_ref[:, pl.ds(at, size)]).astype(f32).astype(bf16)
        out_ref[:, pl.ds(at, size)] = dot(turned_ref[...], pick).astype(bf16)
    ones = jnp.ones((8, SEQ), bf16)
    mean_ref[:, pl.ds(0, HALF)] = dot(ones, xo_ref[0], NT) * (1.0 / SEQ)
    mean_ref[:, pl.ds(HALF + 64, HALF)] = dot(ones, xr_ref[0], NT) * (1.0 / SEQ)


def norm_patches(idx, own, other, sample):
    sample_spec = pl.BlockSpec((1, HALF, SEQ), lambda i: (sample, 0, 0))
    other_spec = pl.BlockSpec((1, HALF, SEQ), lambda i: (0, 0, 0))
    return pl.pallas_call(
        norm_kernel,
        grid=(1,),
        out_shape=(shape((ROWS, D), bf16), shape((8, 1280), f32)),
        in_specs=[pl.BlockSpec((1, D), lambda i: (0, 0)), sample_spec, other_spec],
        out_specs=(pl.BlockSpec((ROWS, D), lambda i: (0, 0)), pl.BlockSpec((8, 1280), lambda i: (0, 0))),
        scratch_shapes=[pltpu.VMEM((D, ROWS), bf16), pltpu.VMEM((ROWS, D), bf16)],
        compiler_params=pltpu.CompilerParams(vmem_limit_bytes=VMEM_LIMIT),
        cost_estimate=pl.CostEstimate(flops=2 * ROWS * D * D, bytes_accessed=4 * ROWS * D, transcendentals=0),
        name="norm_patches",
    )(idx, own, other)


def stack_kernel(*refs):
    pieces, outs = refs[:-2], refs[-2:]
    for half, out in enumerate(outs):
        rows = []
        for piece in pieces:
            count = piece.shape[0] // 2
            rows.append(piece[...].astype(f32)[count * half : count * half + count])
        out[...] = jnp.concatenate(rows, axis=0).astype(bf16)


def stack(pieces):
    return call(
        stack_kernel,
        (shape((PIECE, D), bf16), shape((PIECE, D), bf16)),
        pieces,
        bytes_accessed=8 * PIECE * D,
        name="stack",
    )


def order_kernel(idx_ref, *refs):
    pieces, (out_ref, mixed_ref, pick_ref, sems) = refs[:8], refs[8:]
    copies = []
    for n, piece in enumerate(pieces):
        rows = mixed_ref.at[pl.ds(PIECE * n, PIECE), :]
        copies.append(pltpu.make_async_copy(piece.at[:, pl.ds(WO_AT - D, WIN)], rows, sems.at[n]))
    for copy in copies:
        copy.start()
    for copy in copies:
        copy.wait()
    rows = lax.broadcasted_iota(jnp.int32, (D, D), 0)
    pick_ref[...] = (rows == idx_ref[...]).astype(f32).astype(bf16)
    for at in range(0, WIN, 256):
        size = min(256, WIN - at)
        out_ref[:, pl.ds(at, size)] = dot(pick_ref[...], mixed_ref[:, pl.ds(at, size)]).astype(bf16)


def order_out(idx, pieces):
    return call(
        order_kernel,
        shape((D, WIN), bf16),
        [idx] + pieces,
        specs=[VM] + [ANY] * 8,
        scratch=[pltpu.VMEM((D, WIN), bf16), pltpu.VMEM((D, D), bf16), pltpu.SemaphoreType.DMA((8,))],
        flops=2 * D * D * WIN,
        bytes_accessed=4 * D * WIN,
        name="order_out",
    )


def attend_kernel(x_ref, *refs):
    pieces, (att_ref, sum_ref, w_ref, qkv_ref, sems) = refs[:16], refs[16:]
    copies = []
    for n, piece in enumerate(pieces):
        rows = pl.ds(PIECE * (n % 8), PIECE)
        if n < 8:
            copies.append(pltpu.make_async_copy(piece, w_ref.at[rows, pl.ds(0, D)], sems.at[n]))
        else:
            part = piece.at[:, pl.ds(0, QKV - D)]
            copies.append(pltpu.make_async_copy(part, w_ref.at[rows, pl.ds(D, QKV - D)], sems.at[n]))
    for copy in copies:
        copy.start()
    att_ref[...] = jnp.zeros_like(att_ref)
    for copy in copies[:8]:
        copy.wait()

    q_scale = math.log2(math.e) * HEAD_DIM ** (-0.5)

    def project(n, carry):
        at = pl.multiple_of(n * 256, 256)
        lane = at + lax.broadcasted_iota(jnp.int32, (1, 256), 1)
        scale = jnp.where(lane < HALF, q_scale, 1.0).astype(f32)
        qkv_ref[:, pl.ds(at, 256)] = (dot(x_ref[...], w_ref[:, pl.ds(at, 256)]) * scale).astype(bf16)
        return carry

    lax.fori_loop(0, D // 256, project, 0)
    for copy in copies[8:]:
        copy.wait()
    lax.fori_loop(D // 256, QKV // 256, project, 0)

    lane = lax.broadcasted_iota(jnp.int32, (1, 256), 1)

    def between(low, high):
        return ((lane >= low) & (lane < high)).astype(f32)

    last = (lane == 255).astype(f32)
    key_row = lax.broadcasted_iota(jnp.int32, (ROWS, 1), 0)
    key_bias = jnp.where(key_row >= SEQ, -1e30, 0.0).astype(f32) * last

    def pair(p, carry):
        at = pl.multiple_of(p * 128, 128)
        q_at = 16 * p
        v_at = 64 + 16 * p
        k_win = qkv_ref[:, pl.ds(D + at, 256)] * (1.0 - last).astype(bf16) + key_bias.astype(bf16)
        v_win = qkv_ref[:, pl.ds(512 + at, 256)]
        values = []
        for h in range(2):
            low = v_at + HEAD_DIM * h
            ones = (lane == h).astype(f32).astype(bf16)
            values.append(v_win * between(low, low + HEAD_DIM).astype(bf16) + ones)
        units = [(row, h) for row in range(0, QROWS, QBLOCK) for h in range(2)]
        scores, weights, totals = {}, {}, {}

        def score(u):
            row, h = units[u]
            low = q_at + HEAD_DIM * h
            q_win = qkv_ref[pl.ds(row, QBLOCK), pl.ds(at, 256)]
            q = q_win * between(low, low + HEAD_DIM).astype(bf16) + last.astype(bf16)
            scores[u] = dot(q, k_win, NT)

        def weigh(u):
            s = scores.pop(u)
            weights[u] = jnp.exp2((s - jnp.max(s, axis=1, keepdims=True)).astype(bf16))

        def mix(u):
            row, h = units[u]
            totals[u] = dot(weights.pop(u), values[h])

        def store(u):
            row = units[u][0]
            total = totals.pop(u) + totals.pop(u + 1)
            inverse = jnp.where(lane < v_at + HEAD_DIM, 1.0 / total[:, 0:1], 1.0 / total[:, 1:2])
            mixed = (total * inverse * between(v_at, v_at + 2 * HEAD_DIM)).astype(bf16)
            att_ref[pl.ds(row, QBLOCK), pl.ds(at, 256)] = att_ref[pl.ds(row, QBLOCK), pl.ds(at, 256)] + mixed

        score(0)
        for u in range(len(units)):
            if u + 1 < len(units):
                score(u + 1)
            weigh(u)
            mix(u)
            if u % 2 == 1:
                store(u - 1)
        return carry

    lax.fori_loop(0, 4, pair, 0)
    valid = (lax.broadcasted_iota(jnp.int32, (8, QROWS), 1) < SEQ).astype(f32).astype(bf16)
    sum_ref[...] = dot(valid, att_ref[...])


def attend(x, pieces):
    return call(
        attend_kernel,
        (shape((QROWS, WIN), bf16), shape((8, WIN), f32)),
        [x] + pieces,
        specs=[VM] + [ANY] * 16,
        scratch=[
            pltpu.VMEM((D, QKV), bf16),
            pltpu.VMEM((ROWS, QKV), bf16),
            pltpu.SemaphoreType.DMA((16,)),
        ],
        flops=2 * ROWS * D * QKV + 8 * 4 * ROWS * ROWS * 256,
        bytes_accessed=2 * (D * QKV + ROWS * D + QROWS * WIN),
        name="attend",
    )


def project_kernel(m_ref, att_ref, w_ref, x_ref, own_ref, send_ref):
    m = m_ref[0]
    mine = w_ref[pl.ds(pl.multiple_of(m * HALF, HALF), HALF), :]
    theirs = w_ref[pl.ds(pl.multiple_of((1 - m) * HALF, HALF), HALF), :]
    send_ref[...] = dot(theirs, att_ref[...], NT)[:, :SEQ].astype(bf16)
    own_ref[...] = dot(mine, att_ref[...], NT)[:, :SEQ] + x_ref[0].astype(f32)


def project(m, att, w, x, sample):
    full = lambda *dims: pl.BlockSpec(dims, lambda i: (0,) * len(dims))
    return pl.pallas_call(
        project_kernel,
        grid=(1,),
        out_shape=(shape((HALF, SEQ), f32), shape((HALF, SEQ), bf16)),
        in_specs=[SM, full(QROWS, WIN), full(D, WIN), pl.BlockSpec((1, HALF, SEQ), lambda i: (sample, 0, 0))],
        out_specs=(full(HALF, SEQ), full(HALF, SEQ)),
        compiler_params=pltpu.CompilerParams(vmem_limit_bytes=VMEM_LIMIT),
        cost_estimate=pl.CostEstimate(
            flops=2 * D * WIN * QROWS, bytes_accessed=2 * (QROWS * WIN + D * WIN) + 8 * HALF * SEQ, transcendentals=0
        ),
        name="project",
    )(m, att, w, x)


def finish_kernel(own_ref, other_ref, *refs):
    out_ref = refs[-1]
    out_ref[0] = (own_ref[...] + other_ref[...].astype(f32)).astype(bf16)


def finish(own, other, sample, before=None):
    rows = 288
    spec = pl.BlockSpec((rows, SEQ), lambda i: (i, 0))
    args = [own, other] + ([before] if before is not None else [])
    return pl.pallas_call(
        finish_kernel,
        grid=(HALF // rows,),
        out_shape=shape((2, HALF, SEQ), bf16),
        in_specs=[spec, spec] + ([ANY] if before is not None else []),
        out_specs=pl.BlockSpec((1, rows, SEQ), lambda i: (sample, i, 0)),
        input_output_aliases={2: 0} if before is not None else {},
        compiler_params=pltpu.CompilerParams(vmem_limit_bytes=VMEM_LIMIT),
        cost_estimate=pl.CostEstimate(flops=HALF * SEQ, bytes_accessed=8 * HALF * SEQ, transcendentals=0),
        name="finish",
    )(*args)


def text_kernel(m_ref, co_ref, cr_ref, w_ref, wo_ref, part_ref, last_ref, x_ref):
    m = m_ref[0]
    own = co_ref[...].astype(f32)
    other = cr_ref[...].astype(f32)
    first = jnp.where(m == 0, own, other)
    second = jnp.where(m == 0, other, own)
    x_ref[:, pl.ds(0, HALF)] = first
    x_ref[:, pl.ds(HALF, HALF)] = second
    x = x_ref[...]
    center = jnp.sum(x, axis=1, keepdims=True) * (1.0 / D)
    centred = x - center
    spread = jnp.sum(centred * centred, axis=1, keepdims=True) * (1.0 / D)
    normed = (centred * lax.rsqrt(spread + 1e-06)).astype(bf16)
    q = dot(normed, w_ref[0], NT).astype(bf16).astype(f32)
    k = dot(normed, w_ref[1], NT).astype(bf16)
    v = dot(normed, w_ref[2], NT).astype(bf16)
    row = lax.broadcasted_iota(jnp.int32, (16, HALF), 0)
    lane = lax.broadcasted_iota(jnp.int32, (16, HALF), 1)
    low = (row % 8) * HEAD_DIM
    of_head = (lane >= low) & (lane < low + HEAD_DIM)
    q_last = jnp.where(row < 8, q[TEXT - 1 : TEXT], q[2 * TEXT - 1 : 2 * TEXT])
    q_head = jnp.where(of_head, q_last, 0.0).astype(bf16)
    s = dot(q_head, k, NT) * HEAD_DIM ** (-0.5)
    key = lax.broadcasted_iota(jnp.int32, (16, 2 * TEXT), 1)
    of = lax.broadcasted_iota(jnp.int32, (16, 2 * TEXT), 0)
    s = jnp.where((key < TEXT) == (of < 8), s, -1e30)
    e = jnp.exp(s - jnp.max(s, axis=1, keepdims=True))
    weight = (e / jnp.sum(e, axis=1, keepdims=True)).astype(bf16)
    o = jnp.where(of_head, dot(weight, v), 0.0)
    a = jnp.sum(jnp.where(row < 8, o, 0.0), axis=0, keepdims=True)
    b = jnp.sum(jnp.where(row < 8, 0.0, o), axis=0, keepdims=True)
    att = jnp.where(lax.broadcasted_iota(jnp.int32, (8, HALF), 0) == 2, a, b).astype(bf16)
    part_ref[...] = dot(att, wo_ref[...])
    at = lax.broadcasted_iota(jnp.int32, (8, D), 0)
    last_ref[...] = jnp.where(at == 2, x[TEXT - 1 : TEXT], x[2 * TEXT - 1 : 2 * TEXT])


def text_tower(m, own, other, w, wo):
    return call(
        text_kernel,
        (shape((8, D), f32), shape((8, D), f32)),
        [m, own, other, w, wo],
        specs=[SM, VM, VM, VM, VM],
        scratch=[pltpu.VMEM((2 * TEXT, D), f32)],
        flops=0,
        bytes_accessed=0,
        name="text_tower",
    )


def embed_kernel(mine_ref, other_ref, near_ref, far_ref, out_ref):
    for at, features in enumerate((mine_ref[...] + other_ref[...], near_ref[...] + far_ref[...])):
        total = jnp.sum(features * features, axis=1, keepdims=True)
        embedded = (features * lax.rsqrt(total + 1e-06)).astype(bf16)
        for which in range(4):
            out_ref[pl.ds(at, 1), pl.ds(D * which, D)] = embedded[which : which + 1]


def embed(parts):
    return call(embed_kernel, shape((2, MESSAGE), bf16), parts, bytes_accessed=200000, name="embed")


def pool_kernel(m_ref, a_ref, b_ref, ma_ref, mb_ref, w_ref, text_ref, last_ref, part_ref):
    row = lax.broadcasted_iota(jnp.int32, (8, WIN), 0)
    sums = jnp.where(row == 0, a_ref[...], b_ref[...]) * (1.0 / SEQ)
    high = sums.astype(bf16)
    rest = sums - high.astype(f32)
    mid = rest.astype(bf16)
    low = (rest - mid.astype(f32)).astype(bf16)
    w = w_ref[...]
    pooled = dot(high, w, NT) + (dot(mid, w, NT) + dot(low, w, NT))
    m = m_ref[0]
    at = lax.broadcasted_iota(jnp.int32, (8, HALF), 0)
    own = jnp.where(at == 0, ma_ref[:, pl.ds(0, HALF)], mb_ref[:, pl.ds(0, HALF)])
    other = jnp.where(at == 0, ma_ref[:, pl.ds(HALF + 64, HALF)], mb_ref[:, pl.ds(HALF + 64, HALF)])
    first = jnp.where(m == 0, 1.0, 0.0)
    for half, mean in ((0, own), (HALF, other)):
        part = jnp.where(at < 2, pooled[:, half : half + HALF], text_ref[:, pl.ds(half, HALF)])
        part_ref[:, pl.ds(half, HALF)] = part + first * jnp.where(at < 2, mean, last_ref[:, pl.ds(half, HALF)])


def pool(m, sum_a, sum_b, mean_a, mean_b, w, text_part, text_last):
    return call(
        pool_kernel,
        shape((8, D), f32),
        [m, sum_a, sum_b, mean_a, mean_b, w, text_part, text_last],
        specs=[SM] + [VM] * 7,
        flops=3 * 2 * 8 * WIN * D,
        bytes_accessed=2 * D * WIN,
        name="pool",
    )


def pair_kernel(m_ref, own_ref, *refs):
    pieces, (image_ref, text_ref, all_ref) = refs[:8], refs[8:]
    for n, piece in enumerate(pieces):
        all_ref[pl.ds(16 * n, 16), :] = piece[...]
    own = own_ref[...].astype(f32)[0:1]
    row = lax.broadcasted_iota(jnp.int32, (8, D), 0)
    at_row = lax.broadcasted_iota(jnp.int32, (8, 128), 0)
    at_col = lax.broadcasted_iota(jnp.int32, (8, 128), 1)
    for mine, others, out_ref in ((0, 2, image_ref), (2, 0, text_ref)):
        rows = jnp.where(row == 0, own[:, D * mine : D * mine + D], own[:, D * mine + D : D * mine + 2 * D]).astype(bf16)
        grad = None
        for which in range(2):
            each = all_ref[:, pl.ds(D * (others + which), D)]
            logit = 10.0 * dot(rows, each, NT) - 1.0
            label = jnp.where((at_row == which) & (at_col == 0), 1.0, -1.0)
            weight = (-10.0 * label / (1.0 + jnp.exp(label * logit))).astype(bf16)
            term = dot(weight, each)
            grad = term if grad is None else grad + term
        out_ref[...] = jnp.where(m_ref[0] == 0, grad[0:2, 0:HALF], grad[0:2, HALF:])


def pair_grads(m, own, pieces):
    return call(
        pair_kernel,
        (shape((2, HALF), f32), shape((2, HALF), f32)),
        [m, own] + pieces,
        specs=[SM] + [VM] * 9,
        scratch=[pltpu.VMEM((128, MESSAGE), bf16)],
        flops=4 * 2 * 8 * 256 * D,
        bytes_accessed=2 * 128 * MESSAGE,
        name="pair_grads",
    )


def gather_rest(pair, behind, behind_last):
    quad = after(jnp.concatenate([pair, shift(pair, "z", 8, 4)], axis=0), behind)
    along_z = jnp.concatenate([quad] + [shift(quad, "z", 8, k) for k in (1, 2, 7)], axis=0)
    near = [along_z] + [shift(along_z, "x", 4, k) for k in (1, 3, 2)]
    near[3] = after(near[3], behind_last)
    return near + [shift(piece, "c", 2, 1) for piece in near]


def weight_slab(image_qkv, image_out):
    turned = jnp.transpose(image_out)
    return jnp.concatenate(
        [
            jnp.concatenate([image_qkv[:, 0], image_qkv[:, 2]], axis=1),
            jnp.concatenate([image_qkv[:, 1], turned], axis=1),
        ],
        axis=0,
    )


def gather_weights(slab, over_w, behind_pair, behind_quad):
    pair = after(jnp.concatenate([slab[:9], over_w[:9], slab[9:], over_w[9:]], axis=0), behind_pair)
    over_z = shift(pair, "z", 8, 4)
    quad = after(jnp.concatenate([pair[:18], over_z[:18], pair[18:], over_z[18:]], axis=0), behind_quad)
    others = [shift(quad, "z", 8, 1), shift(pair, "z", 8, 2), shift(pair, "z", 8, 6), shift(quad, "z", 8, 7)]
    return stack([quad] + others)


def row_order(z, x, w, c):
    at = np.arange(D)
    r, rest = at % 9, at // 9
    wr, rest = rest % 2, rest // 2
    z4, rest = rest % 2, rest // 2
    zr, rest = np.array(Z_STEPS)[rest % 4] + 4 * z4, rest // 4
    xr, cr = rest % 4, rest // 4
    device = (((z + zr) % 8 * 4 + (x + xr) % 4) * 2 + (w + wr) % 2) * 2 + (c + cr) % 2
    return (device * 9 + r).astype(jnp.int32).reshape(1, D)


def on_device(patches, image_qkv, image_out, captions, text_qkv, text_out):
    z, x, w, c, m = (lax.axis_index(a) for a in ("z", "x", "w", "c", "m"))
    m_arr = jnp.reshape(m, (1,)).astype(jnp.int32)
    order = row_order(z, x, w, c)
    norm_order = (order + HALF * m) % D

    own = jnp.transpose(patches, (0, 2, 1))
    captions2 = captions.reshape(2 * TEXT, HALF)
    captions_other = shift(captions2, "m", 2, 1)
    slab = weight_slab(image_qkv, image_out)
    over_w = shift(slab, "w", 2, 1)
    other0 = shift(after(own[0:1], captions_other, over_w), "m", 2, 1)
    text_part, text_last = text_tower(
        m_arr, captions2, after(captions_other, over_w), jnp.transpose(text_qkv, (1, 2, 0)), text_out
    )

    qv, ko = gather_weights(slab, over_w, captions_other, text_part)

    next_qv, last_qv = shift(qv, "x", 4, 1), shift(qv, "x", 4, 3)
    next_ko, last_ko = shift(ko, "x", 4, 1), shift(ko, "x", 4, 3)
    other1 = shift(after(own[1:2], over_w), "m", 2, 1)
    normed0, mean0 = norm_patches(norm_order, own, other0, 0)
    far_qv = shift(after(last_qv, normed0), "x", 4, 3)
    far_ko = shift(next_ko, "x", 4, 1)
    near_qv = [qv, next_qv, far_qv, last_qv]
    near_ko = [ko, next_ko, far_ko, last_ko]
    all_qv = near_qv + [shift(after(block, normed0), "c", 2, 1) for block in near_qv]
    all_ko = near_ko + [shift(after(block, normed0), "c", 2, 1) for block in near_ko]
    normed1, mean1 = norm_patches(norm_order, own, other1, 1)
    wo = order_out(order, all_ko)

    att0, sum0 = attend(after(normed0, normed1, wo), all_qv + all_ko)
    own0, send0 = project(m_arr, att0, wo, own, 0)
    got0 = shift(send0, "m", 2, 1)
    att1, sum1 = attend(after(normed1, send0), all_qv + all_ko)
    part = pool(m_arr, sum0, sum1, mean0, mean1, wo, text_part, text_last)
    own1, send1 = project(m_arr, after(att1, part), wo, own, 1)
    parts = [after(part, got0), shift(part, "m", 2, 1), shift(part, "w", 2, 1), shift_wm(part)]
    embedded = embed([after(parts[0], send1)] + parts[1:])
    got1 = shift(after(send1, embedded), "m", 2, 1)
    hidden = finish(own0, after(got0, embedded), 0)
    every = gather_rest(embedded, hidden, got1)

    image_grad, text_grad = pair_grads(m_arr, embedded, every)
    hidden = finish(own1, got1, 1, hidden)
    return jnp.transpose(hidden, (0, 2, 1)), image_grad, text_grad


def solution(mesh):
    split = Mesh(mesh.devices.reshape(8, 4, 2, 2, 2), ("z", "x", "w", "c", "m"))
    batch = ("z", "x", "w", "c")
    return jax.shard_map(
        on_device,
        mesh=split,
        in_specs=(
            P(batch, None, "m"),
            P(batch, None, "m"),
            P("m", batch),
            P(batch, None, "m"),
            P(None, None, "m"),
            P("m", None),
        ),
        out_specs=(P(batch, None, "m"), P(batch, "m"), P(batch, "m")),
        check_vma=False,
    )
```

```python
import functools
import math

import jax
import jax.numpy as jnp
import numpy as np
from jax import lax
from jax.experimental import pallas as pl
from jax.experimental.pallas import tpu as pltpu
from jax.sharding import Mesh, PartitionSpec as P

D = 1152
HALF = 576
HEAD_DIM = 72
SEQ = 729
ROWS = 768
QROWS = 736
QBLOCK = 368
TEXT = 64
COLS = 2304
QKV = 1792
WO_AT = 1664
WIN = 640
PIECE = 144
Z_STEPS = (0, 1, 2, 7)
MESSAGE = 4 * D

f32 = jnp.float32
bf16 = jnp.bfloat16
NT = (((1,), (1,)), ((), ()))
TN = (((0,), (0,)), ((), ()))
VMEM_LIMIT = 24 * 1024 * 1024


def dot(a, b, dims=(((1,), (0,)), ((), ()))):
    return lax.dot_general(a, b, dims, preferred_element_type=f32)


def call(body, outs, args, specs=None, out_specs=None, scratch=(), flops=0, bytes_accessed=0, name=None, aliases=None):
    whole = pl.BlockSpec(memory_space=pltpu.VMEM)
    return pl.pallas_call(
        body,
        out_shape=outs,
        in_specs=specs if specs is not None else [whole] * len(args),
        out_specs=out_specs if out_specs is not None else jax.tree.map(lambda _: whole, outs),
        scratch_shapes=list(scratch),
        compiler_params=pltpu.CompilerParams(vmem_limit_bytes=VMEM_LIMIT),
        cost_estimate=pl.CostEstimate(flops=int(flops), bytes_accessed=int(bytes_accessed), transcendentals=0),
        input_output_aliases=aliases or {},
        name=name,
    )(*args)


def shape(dims, kind):
    return jax.ShapeDtypeStruct(dims, kind)


VM = pl.BlockSpec(memory_space=pltpu.VMEM)
SM = pl.BlockSpec(memory_space=pltpu.SMEM)
ANY = pl.BlockSpec(memory_space=pl.ANY)


def shift(value, axis, size, step):
    return lax.ppermute(value, axis, [((i + step) % size, i) for i in range(size)])


def shift_wm(value):
    return lax.ppermute(value, ("w", "m"), [(3 - i, i) for i in range(4)])


def after(value, *others):
    return lax.optimization_barrier((value,) + others)[0]


def norm_kernel(idx_ref, xo_ref, xr_ref, out_ref, mean_ref, pad_ref, turned_ref):
    xo = xo_ref[0].astype(f32)
    xr = xr_ref[0].astype(f32)
    center = (jnp.sum(xo, axis=0, keepdims=True) + jnp.sum(xr, axis=0, keepdims=True)) * (1.0 / D)
    co = xo - center
    cr = xr - center
    spread = (jnp.sum(co * co, axis=0, keepdims=True) + jnp.sum(cr * cr, axis=0, keepdims=True)) * (1.0 / D)
    scale = lax.rsqrt(spread + 1e-06)
    pad_ref[:, pl.ds(640, 128)] = jnp.zeros((D, 128), bf16)
    pad_ref[pl.ds(0, HALF), pl.ds(0, SEQ)] = (co * scale).astype(bf16)
    pad_ref[pl.ds(HALF, HALF), pl.ds(0, SEQ)] = (cr * scale).astype(bf16)
    turned_ref[...] = jnp.transpose(pad_ref[...])
    for at in range(0, D, 256):
        size = min(256, D - at)
        rows = lax.broadcasted_iota(jnp.int32, (D, size), 0)
        pick = (rows == idx_ref[:, pl.ds(at, size)]).astype(f32).astype(bf16)
        out_ref[:, pl.ds(at, size)] = dot(turned_ref[...], pick).astype(bf16)
    ones = jnp.ones((8, SEQ), bf16)
    mean_ref[:, pl.ds(0, HALF)] = dot(ones, xo_ref[0], NT) * (1.0 / SEQ)
    mean_ref[:, pl.ds(HALF + 64, HALF)] = dot(ones, xr_ref[0], NT) * (1.0 / SEQ)


def norm_patches(idx, own, other, sample):
    sample_spec = pl.BlockSpec((1, HALF, SEQ), lambda i: (sample, 0, 0))
    other_spec = pl.BlockSpec((1, HALF, SEQ), lambda i: (0, 0, 0))
    return pl.pallas_call(
        norm_kernel,
        grid=(1,),
        out_shape=(shape((ROWS, D), bf16), shape((8, 1280), f32)),
        in_specs=[pl.BlockSpec((1, D), lambda i: (0, 0)), sample_spec, other_spec],
        out_specs=(pl.BlockSpec((ROWS, D), lambda i: (0, 0)), pl.BlockSpec((8, 1280), lambda i: (0, 0))),
        scratch_shapes=[pltpu.VMEM((D, ROWS), bf16), pltpu.VMEM((ROWS, D), bf16)],
        compiler_params=pltpu.CompilerParams(vmem_limit_bytes=VMEM_LIMIT),
        cost_estimate=pl.CostEstimate(flops=2 * ROWS * D * D, bytes_accessed=4 * ROWS * D, transcendentals=0),
        name="norm_patches",
    )(idx, own, other)


def stack_kernel(*refs):
    pieces, outs = refs[:-2], refs[-2:]
    for half, out in enumerate(outs):
        rows = []
        for piece in pieces:
            count = piece.shape[0] // 2
            rows.append(piece[...].astype(f32)[count * half : count * half + count])
        out[...] = jnp.concatenate(rows, axis=0).astype(bf16)


def stack(pieces):
    return call(
        stack_kernel,
        (shape((PIECE, D), bf16), shape((PIECE, D), bf16)),
        pieces,
        bytes_accessed=8 * PIECE * D,
        name="stack",
    )


def order_kernel(idx_ref, *refs):
    pieces, refs = refs[:4], refs[4:]
    out_ref, mixed_ref, pick_ref, sems = refs[-4:]
    copies = []
    for n, piece in enumerate(pieces):
        rows = mixed_ref.at[pl.ds(PIECE * n, PIECE), :]
        copies.append(pltpu.make_async_copy(piece.at[:, pl.ds(WO_AT - D, WIN)], rows, sems.at[n]))
    for copy in copies:
        copy.start()
    rows = lax.broadcasted_iota(jnp.int32, (D, HALF), 0)
    pick_ref[...] = (rows == idx_ref[...]).astype(f32).astype(bf16)
    for copy in copies:
        copy.wait()
    for at in range(0, WIN, 256):
        size = min(256, WIN - at)
        part = dot(pick_ref[...], mixed_ref[:, pl.ds(at, size)]).astype(bf16)
        out_ref[:, pl.ds(at, size)] = part if len(refs) == 4 else refs[0][:, pl.ds(at, size)] + part


def order_out(idx, pieces, before=()):
    return call(
        order_kernel,
        shape((D, WIN), bf16),
        [idx] + pieces + list(before),
        specs=[VM] + [ANY] * 4 + [VM] * len(before),
        scratch=[pltpu.VMEM((HALF, WIN), bf16), pltpu.VMEM((D, HALF), bf16), pltpu.SemaphoreType.DMA((4,))],
        flops=2 * D * HALF * WIN,
        bytes_accessed=4 * D * WIN,
        name="order_out",
    )


def attend_kernel(x_ref, *refs):
    pieces, (att_ref, sum_ref, w_ref, qkv_ref, sems) = refs[:16], refs[16:]
    copies = []
    for n, piece in enumerate(pieces):
        rows = pl.ds(PIECE * (n % 8), PIECE)
        if n < 8:
            copies.append(pltpu.make_async_copy(piece, w_ref.at[rows, pl.ds(0, D)], sems.at[n]))
        else:
            part = piece.at[:, pl.ds(0, QKV - D)]
            copies.append(pltpu.make_async_copy(part, w_ref.at[rows, pl.ds(D, QKV - D)], sems.at[n]))
    for copy in copies:
        copy.start()
    att_ref[...] = jnp.zeros_like(att_ref)
    for copy in copies[:8]:
        copy.wait()

    q_scale = math.log2(math.e) * HEAD_DIM ** (-0.5)

    def project(n, carry):
        at = pl.multiple_of(n * 256, 256)
        lane = at + lax.broadcasted_iota(jnp.int32, (1, 256), 1)
        scale = jnp.where(lane < HALF, q_scale, 1.0).astype(f32)
        qkv_ref[:, pl.ds(at, 256)] = (dot(x_ref[...], w_ref[:, pl.ds(at, 256)]) * scale).astype(bf16)
        return carry

    lax.fori_loop(0, D // 256, project, 0)
    for copy in copies[8:]:
        copy.wait()
    lax.fori_loop(D // 256, QKV // 256, project, 0)

    lane = lax.broadcasted_iota(jnp.int32, (1, 256), 1)

    def between(low, high):
        return ((lane >= low) & (lane < high)).astype(f32)

    last = (lane == 255).astype(f32)
    key_row = lax.broadcasted_iota(jnp.int32, (ROWS, 1), 0)
    key_bias = jnp.where(key_row >= SEQ, -1e30, 0.0).astype(f32) * last

    def pair(p, carry):
        at = pl.multiple_of(p * 128, 128)
        q_at = 16 * p
        v_at = 64 + 16 * p
        k_win = qkv_ref[:, pl.ds(D + at, 256)] * (1.0 - last).astype(bf16) + key_bias.astype(bf16)
        v_win = qkv_ref[:, pl.ds(512 + at, 256)]
        values = []
        for h in range(2):
            low = v_at + HEAD_DIM * h
            ones = (lane == h).astype(f32).astype(bf16)
            values.append(v_win * between(low, low + HEAD_DIM).astype(bf16) + ones)
        units = [(row, h) for row in range(0, QROWS, QBLOCK) for h in range(2)]
        scores, weights, totals = {}, {}, {}

        def score(u):
            row, h = units[u]
            low = q_at + HEAD_DIM * h
            q_win = qkv_ref[pl.ds(row, QBLOCK), pl.ds(at, 256)]
            q = q_win * between(low, low + HEAD_DIM).astype(bf16) + last.astype(bf16)
            scores[u] = dot(q, k_win, NT)

        def weigh(u):
            s = scores.pop(u)
            weights[u] = jnp.exp2((s - jnp.max(s, axis=1, keepdims=True)).astype(bf16))

        def mix(u):
            row, h = units[u]
            totals[u] = dot(weights.pop(u), values[h])

        def store(u):
            row = units[u][0]
            total = totals.pop(u) + totals.pop(u + 1)
            inverse = jnp.where(lane < v_at + HEAD_DIM, 1.0 / total[:, 0:1], 1.0 / total[:, 1:2])
            mixed = (total * inverse * between(v_at, v_at + 2 * HEAD_DIM)).astype(bf16)
            att_ref[pl.ds(row, QBLOCK), pl.ds(at, 256)] = att_ref[pl.ds(row, QBLOCK), pl.ds(at, 256)] + mixed

        score(0)
        for u in range(len(units)):
            if u + 1 < len(units):
                score(u + 1)
            weigh(u)
            mix(u)
            if u % 2 == 1:
                store(u - 1)
        return carry

    lax.fori_loop(0, 4, pair, 0)
    valid = (lax.broadcasted_iota(jnp.int32, (8, QROWS), 1) < SEQ).astype(f32).astype(bf16)
    sum_ref[...] = dot(valid, att_ref[...])


def attend(x, pieces):
    return call(
        attend_kernel,
        (shape((QROWS, WIN), bf16), shape((8, WIN), f32)),
        [x] + pieces,
        specs=[VM] + [ANY] * 16,
        scratch=[
            pltpu.VMEM((D, QKV), bf16),
            pltpu.VMEM((ROWS, QKV), bf16),
            pltpu.SemaphoreType.DMA((16,)),
        ],
        flops=2 * ROWS * D * QKV + 8 * 4 * ROWS * ROWS * 256,
        bytes_accessed=2 * (D * QKV + ROWS * D + QROWS * WIN),
        name="attend",
    )


def project_kernel(m_ref, att_ref, w_ref, x_ref, own_ref, send_ref):
    m = m_ref[0]
    mine = w_ref[pl.ds(pl.multiple_of(m * HALF, HALF), HALF), :]
    theirs = w_ref[pl.ds(pl.multiple_of((1 - m) * HALF, HALF), HALF), :]
    send_ref[...] = dot(theirs, att_ref[...], NT)[:, :SEQ].astype(bf16)
    own_ref[...] = dot(mine, att_ref[...], NT)[:, :SEQ] + x_ref[0].astype(f32)


def project(m, att, w, x, sample):
    full = lambda *dims: pl.BlockSpec(dims, lambda i: (0,) * len(dims))
    return pl.pallas_call(
        project_kernel,
        grid=(1,),
        out_shape=(shape((HALF, SEQ), f32), shape((HALF, SEQ), bf16)),
        in_specs=[SM, full(QROWS, WIN), full(D, WIN), pl.BlockSpec((1, HALF, SEQ), lambda i: (sample, 0, 0))],
        out_specs=(full(HALF, SEQ), full(HALF, SEQ)),
        compiler_params=pltpu.CompilerParams(vmem_limit_bytes=VMEM_LIMIT),
        cost_estimate=pl.CostEstimate(
            flops=2 * D * WIN * QROWS, bytes_accessed=2 * (QROWS * WIN + D * WIN) + 8 * HALF * SEQ, transcendentals=0
        ),
        name="project",
    )(m, att, w, x)


def finish_kernel(own_ref, other_ref, *refs):
    out_ref = refs[-1]
    out_ref[0] = (own_ref[...] + other_ref[...].astype(f32)).astype(bf16)


def finish(own, other, sample, before=None):
    rows = 288
    spec = pl.BlockSpec((rows, SEQ), lambda i: (i, 0))
    args = [own, other] + ([before] if before is not None else [])
    return pl.pallas_call(
        finish_kernel,
        grid=(HALF // rows,),
        out_shape=shape((2, HALF, SEQ), bf16),
        in_specs=[spec, spec] + ([ANY] if before is not None else []),
        out_specs=pl.BlockSpec((1, rows, SEQ), lambda i: (sample, i, 0)),
        input_output_aliases={2: 0} if before is not None else {},
        compiler_params=pltpu.CompilerParams(vmem_limit_bytes=VMEM_LIMIT),
        cost_estimate=pl.CostEstimate(flops=HALF * SEQ, bytes_accessed=8 * HALF * SEQ, transcendentals=0),
        name="finish",
    )(*args)


def text_kernel(m_ref, co_ref, cr_ref, w_ref, wo_ref, part_ref, last_ref, x_ref):
    m = m_ref[0]
    own = co_ref[...].astype(f32)
    other = cr_ref[...].astype(f32)
    first = jnp.where(m == 0, own, other)
    second = jnp.where(m == 0, other, own)
    x_ref[:, pl.ds(0, HALF)] = first
    x_ref[:, pl.ds(HALF, HALF)] = second
    x = x_ref[...]
    center = jnp.sum(x, axis=1, keepdims=True) * (1.0 / D)
    centred = x - center
    spread = jnp.sum(centred * centred, axis=1, keepdims=True) * (1.0 / D)
    normed = (centred * lax.rsqrt(spread + 1e-06)).astype(bf16)
    q = dot(normed, w_ref[0], NT).astype(bf16).astype(f32)
    k = dot(normed, w_ref[1], NT).astype(bf16)
    v = dot(normed, w_ref[2], NT).astype(bf16)
    row = lax.broadcasted_iota(jnp.int32, (16, HALF), 0)
    lane = lax.broadcasted_iota(jnp.int32, (16, HALF), 1)
    low = (row % 8) * HEAD_DIM
    of_head = (lane >= low) & (lane < low + HEAD_DIM)
    q_last = jnp.where(row < 8, q[TEXT - 1 : TEXT], q[2 * TEXT - 1 : 2 * TEXT])
    q_head = jnp.where(of_head, q_last, 0.0).astype(bf16)
    s = dot(q_head, k, NT) * HEAD_DIM ** (-0.5)
    key = lax.broadcasted_iota(jnp.int32, (16, 2 * TEXT), 1)
    of = lax.broadcasted_iota(jnp.int32, (16, 2 * TEXT), 0)
    s = jnp.where((key < TEXT) == (of < 8), s, -1e30)
    e = jnp.exp(s - jnp.max(s, axis=1, keepdims=True))
    weight = (e / jnp.sum(e, axis=1, keepdims=True)).astype(bf16)
    o = jnp.where(of_head, dot(weight, v), 0.0)
    a = jnp.sum(jnp.where(row < 8, o, 0.0), axis=0, keepdims=True)
    b = jnp.sum(jnp.where(row < 8, 0.0, o), axis=0, keepdims=True)
    att = jnp.where(lax.broadcasted_iota(jnp.int32, (8, HALF), 0) == 2, a, b).astype(bf16)
    part_ref[...] = dot(att, wo_ref[...])
    at = lax.broadcasted_iota(jnp.int32, (8, D), 0)
    last_ref[...] = jnp.where(at == 2, x[TEXT - 1 : TEXT], x[2 * TEXT - 1 : 2 * TEXT])


def text_tower(m, own, other, w, wo):
    return call(
        text_kernel,
        (shape((8, D), f32), shape((8, D), f32)),
        [m, own, other, w, wo],
        specs=[SM, VM, VM, VM, VM],
        scratch=[pltpu.VMEM((2 * TEXT, D), f32)],
        flops=0,
        bytes_accessed=0,
        name="text_tower",
    )


def embed_kernel(mine_ref, other_ref, near_ref, far_ref, out_ref):
    for at, features in enumerate((mine_ref[...] + other_ref[...], near_ref[...] + far_ref[...])):
        total = jnp.sum(features * features, axis=1, keepdims=True)
        embedded = (features * lax.rsqrt(total + 1e-06)).astype(bf16)
        for which in range(4):
            out_ref[pl.ds(at, 1), pl.ds(D * which, D)] = embedded[which : which + 1]


def embed(parts):
    return call(embed_kernel, shape((2, MESSAGE), bf16), parts, bytes_accessed=200000, name="embed")


def pool_kernel(m_ref, a_ref, b_ref, ma_ref, mb_ref, w_ref, text_ref, last_ref, part_ref):
    row = lax.broadcasted_iota(jnp.int32, (8, WIN), 0)
    sums = jnp.where(row == 0, a_ref[...], b_ref[...]) * (1.0 / SEQ)
    high = sums.astype(bf16)
    rest = sums - high.astype(f32)
    mid = rest.astype(bf16)
    low = (rest - mid.astype(f32)).astype(bf16)
    w = w_ref[...]
    pooled = dot(high, w, NT) + (dot(mid, w, NT) + dot(low, w, NT))
    m = m_ref[0]
    at = lax.broadcasted_iota(jnp.int32, (8, HALF), 0)
    own = jnp.where(at == 0, ma_ref[:, pl.ds(0, HALF)], mb_ref[:, pl.ds(0, HALF)])
    other = jnp.where(at == 0, ma_ref[:, pl.ds(HALF + 64, HALF)], mb_ref[:, pl.ds(HALF + 64, HALF)])
    first = jnp.where(m == 0, 1.0, 0.0)
    for half, mean in ((0, own), (HALF, other)):
        part = jnp.where(at < 2, pooled[:, half : half + HALF], text_ref[:, pl.ds(half, HALF)])
        part_ref[:, pl.ds(half, HALF)] = part + first * jnp.where(at < 2, mean, last_ref[:, pl.ds(half, HALF)])


def pool(m, sum_a, sum_b, mean_a, mean_b, w, text_part, text_last):
    return call(
        pool_kernel,
        shape((8, D), f32),
        [m, sum_a, sum_b, mean_a, mean_b, w, text_part, text_last],
        specs=[SM] + [VM] * 7,
        flops=3 * 2 * 8 * WIN * D,
        bytes_accessed=2 * D * WIN,
        name="pool",
    )


def pair_kernel(m_ref, own_ref, *refs):
    pieces, (image_ref, text_ref, all_ref) = refs[:8], refs[8:]
    for n, piece in enumerate(pieces):
        all_ref[pl.ds(16 * n, 16), :] = piece[...]
    own = own_ref[...].astype(f32)[0:1]
    row = lax.broadcasted_iota(jnp.int32, (8, D), 0)
    at_row = lax.broadcasted_iota(jnp.int32, (8, 128), 0)
    at_col = lax.broadcasted_iota(jnp.int32, (8, 128), 1)
    for mine, others, out_ref in ((0, 2, image_ref), (2, 0, text_ref)):
        rows = jnp.where(row == 0, own[:, D * mine : D * mine + D], own[:, D * mine + D : D * mine + 2 * D]).astype(bf16)
        grad = None
        for which in range(2):
            each = all_ref[:, pl.ds(D * (others + which), D)]
            logit = 10.0 * dot(rows, each, NT) - 1.0
            label = jnp.where((at_row == which) & (at_col == 0), 1.0, -1.0)
            weight = (-10.0 * label / (1.0 + jnp.exp(label * logit))).astype(bf16)
            term = dot(weight, each)
            grad = term if grad is None else grad + term
        out_ref[...] = jnp.where(m_ref[0] == 0, grad[0:2, 0:HALF], grad[0:2, HALF:])


def pair_grads(m, own, pieces):
    return call(
        pair_kernel,
        (shape((2, HALF), f32), shape((2, HALF), f32)),
        [m, own] + pieces,
        specs=[SM] + [VM] * 9,
        scratch=[pltpu.VMEM((128, MESSAGE), bf16)],
        flops=4 * 2 * 8 * 256 * D,
        bytes_accessed=2 * 128 * MESSAGE,
        name="pair_grads",
    )


def join_kernel(*refs):
    refs[-1][...] = jnp.concatenate([ref[...].astype(f32) for ref in refs[:-1]], axis=0).astype(bf16)


def join(pieces):
    rows = sum(piece.shape[0] for piece in pieces)
    return call(join_kernel, shape((rows, MESSAGE), bf16), pieces, bytes_accessed=4 * rows * MESSAGE, name="join")


def gather_rest(pair, behind, behind_last):
    others = [shift(pair, "z", 8, k) for k in (4, 3, 5, 2, 6, 1, 7)]
    along_z = join([after(pair, behind)] + others)
    near = [along_z] + [shift(along_z, "x", 4, k) for k in (1, 3, 2)]
    near[3] = after(near[3], behind_last)
    return near + [shift(piece, "c", 2, 1) for piece in near]


def weight_slab(image_qkv, image_out):
    turned = jnp.transpose(image_out)
    return jnp.concatenate(
        [
            jnp.concatenate([image_qkv[:, 0], image_qkv[:, 2]], axis=1),
            jnp.concatenate([image_qkv[:, 1], turned], axis=1),
        ],
        axis=0,
    )


def gather_weights(slab, over_w, behind_pair, *behind_last):
    pair = after(jnp.concatenate([slab[:9], over_w[:9], slab[9:], over_w[9:]], axis=0), behind_pair)
    over_z = shift(pair, "z", 8, 4)
    quad = after(jnp.concatenate([pair[:18], over_z[:18], pair[18:], over_z[18:]], axis=0))
    others = [shift(quad, "z", 8, 1), shift(pair, "z", 8, 2), shift(pair, "z", 8, 6), shift(quad, "z", 8, 7)]
    return stack([after(quad, *behind_last)] + others)


def row_order(z, x, w, c):
    at = np.arange(D)
    r, rest = at % 9, at // 9
    wr, rest = rest % 2, rest // 2
    z4, rest = rest % 2, rest // 2
    zr, rest = np.array(Z_STEPS)[rest % 4] + 4 * z4, rest // 4
    xr, cr = rest % 4, rest // 4
    device = (((z + zr) % 8 * 4 + (x + xr) % 4) * 2 + (w + wr) % 2) * 2 + (c + cr) % 2
    return (device * 9 + r).astype(jnp.int32).reshape(1, D)


def on_device(patches, image_qkv, image_out, captions, text_qkv, text_out):
    z, x, w, c, m = (lax.axis_index(a) for a in ("z", "x", "w", "c", "m"))
    m_arr = jnp.reshape(m, (1,)).astype(jnp.int32)
    order = row_order(z, x, w, c)
    norm_order = (order + HALF * m) % D

    own = jnp.transpose(patches, (0, 2, 1))
    captions2 = captions.reshape(2 * TEXT, HALF)
    captions_other = shift(captions2, "m", 2, 1)
    slab = weight_slab(image_qkv, image_out)
    over_w = shift(slab, "w", 2, 1)
    other0 = shift(after(own[0:1], captions_other, over_w), "m", 2, 1)
    text_part, text_last = text_tower(
        m_arr, captions2, after(captions_other, over_w), jnp.transpose(text_qkv, (1, 2, 0)), text_out
    )

    qv, ko = gather_weights(slab, over_w, captions_other, text_part)
    qv, ko = lax.optimization_barrier((qv, ko, other0))[:2]

    next_qv, last_qv = shift(qv, "x", 4, 1), shift(qv, "x", 4, 3)
    next_ko, last_ko = shift(ko, "x", 4, 1), shift(ko, "x", 4, 3)
    other1 = shift(after(own[1:2], over_w), "m", 2, 1)
    normed0, mean0 = norm_patches(norm_order, own, other0, 0)
    far_qv = shift(after(last_qv, normed0), "x", 4, 3)
    far_ko = shift(next_ko, "x", 4, 1)
    near_qv = [qv, next_qv, far_qv, last_qv]
    near_ko = [ko, next_ko, far_ko, last_ko]
    wo_near = order_out(order[:, :HALF], near_ko)
    all_qv = near_qv + [shift(after(block, normed0, wo_near), "c", 2, 1) for block in near_qv]
    all_ko = near_ko + [shift(after(block, normed0), "c", 2, 1) for block in near_ko]
    normed1, mean1 = norm_patches(norm_order, own, other1, 1)
    wo = order_out(order[:, HALF:], all_ko[4:], [wo_near])

    att0, sum0 = attend(after(normed0, normed1, wo), all_qv + all_ko)
    own0, send0 = project(m_arr, att0, wo, own, 0)
    got0 = shift(send0, "m", 2, 1)
    att1, sum1 = attend(after(normed1, send0), all_qv + all_ko)
    part = pool(m_arr, sum0, sum1, mean0, mean1, wo, text_part, text_last)
    own1, send1 = project(m_arr, after(att1, part), wo, own, 1)
    parts = [after(part, got0), shift(part, "m", 2, 1), shift(part, "w", 2, 1), shift_wm(part)]
    embedded = embed([after(parts[0], send1)] + parts[1:])
    got1 = shift(after(send1, embedded), "m", 2, 1)
    hidden = finish(own0, after(got0, embedded), 0)
    every = gather_rest(embedded, hidden, got1)

    image_grad, text_grad = pair_grads(m_arr, embedded, every)
    hidden = finish(own1, got1, 1, hidden)
    return jnp.transpose(hidden, (0, 2, 1)), image_grad, text_grad


def solution(mesh):
    split = Mesh(mesh.devices.reshape(8, 4, 2, 2, 2), ("z", "x", "w", "c", "m"))
    batch = ("z", "x", "w", "c")
    return jax.shard_map(
        on_device,
        mesh=split,
        in_specs=(
            P(batch, None, "m"),
            P(batch, None, "m"),
            P("m", batch),
            P(batch, None, "m"),
            P(None, None, "m"),
            P("m", None),
        ),
        out_specs=(P(batch, None, "m"), P(batch, "m"), P(batch, "m")),
        check_vma=False,
    )
```

```python
import functools
import math

import jax
import jax.numpy as jnp
import numpy as np
from jax import lax
from jax.experimental import pallas as pl
from jax.experimental.pallas import tpu as pltpu
from jax.sharding import Mesh, PartitionSpec as P

D = 1152
HALF = 576
HEAD_DIM = 72
SEQ = 729
ROWS = 768
QROWS = 736
QBLOCK = 368
TEXT = 64
COLS = 2304
QKV = 1792
WO_AT = 1664
WIN = 640
PIECE = 144
Z_STEPS = (0, 1, 2, 7)
MESSAGE = 4 * D

f32 = jnp.float32
bf16 = jnp.bfloat16
NT = (((1,), (1,)), ((), ()))
TN = (((0,), (0,)), ((), ()))
VMEM_LIMIT = 24 * 1024 * 1024


def dot(a, b, dims=(((1,), (0,)), ((), ()))):
    return lax.dot_general(a, b, dims, preferred_element_type=f32)


def call(body, outs, args, specs=None, out_specs=None, scratch=(), flops=0, bytes_accessed=0, name=None, aliases=None):
    whole = pl.BlockSpec(memory_space=pltpu.VMEM)
    return pl.pallas_call(
        body,
        out_shape=outs,
        in_specs=specs if specs is not None else [whole] * len(args),
        out_specs=out_specs if out_specs is not None else jax.tree.map(lambda _: whole, outs),
        scratch_shapes=list(scratch),
        compiler_params=pltpu.CompilerParams(vmem_limit_bytes=VMEM_LIMIT),
        cost_estimate=pl.CostEstimate(flops=int(flops), bytes_accessed=int(bytes_accessed), transcendentals=0),
        input_output_aliases=aliases or {},
        name=name,
    )(*args)


def shape(dims, kind):
    return jax.ShapeDtypeStruct(dims, kind)


VM = pl.BlockSpec(memory_space=pltpu.VMEM)
SM = pl.BlockSpec(memory_space=pltpu.SMEM)
ANY = pl.BlockSpec(memory_space=pl.ANY)


def shift(value, axis, size, step):
    return lax.ppermute(value, axis, [((i + step) % size, i) for i in range(size)])


def shift_wm(value):
    return lax.ppermute(value, ("w", "m"), [(3 - i, i) for i in range(4)])


def after(value, *others):
    return lax.optimization_barrier((value,) + others)[0]


def norm_kernel(idx_ref, xo_ref, xr_ref, out_ref, mean_ref, pad_ref, turned_ref):
    xo = xo_ref[0].astype(f32)
    xr = xr_ref[0].astype(f32)
    center = (jnp.sum(xo, axis=0, keepdims=True) + jnp.sum(xr, axis=0, keepdims=True)) * (1.0 / D)
    co = xo - center
    cr = xr - center
    spread = (jnp.sum(co * co, axis=0, keepdims=True) + jnp.sum(cr * cr, axis=0, keepdims=True)) * (1.0 / D)
    scale = lax.rsqrt(spread + 1e-06)
    pad_ref[:, pl.ds(640, 128)] = jnp.zeros((D, 128), bf16)
    pad_ref[pl.ds(0, HALF), pl.ds(0, SEQ)] = (co * scale).astype(bf16)
    pad_ref[pl.ds(HALF, HALF), pl.ds(0, SEQ)] = (cr * scale).astype(bf16)
    turned_ref[...] = jnp.transpose(pad_ref[...])
    for at in range(0, D, 256):
        size = min(256, D - at)
        rows = lax.broadcasted_iota(jnp.int32, (D, size), 0)
        pick = (rows == idx_ref[:, pl.ds(at, size)]).astype(f32).astype(bf16)
        out_ref[:, pl.ds(at, size)] = dot(turned_ref[...], pick).astype(bf16)
    ones = jnp.ones((8, SEQ), bf16)
    mean_ref[:, pl.ds(0, HALF)] = dot(ones, xo_ref[0], NT) * (1.0 / SEQ)
    mean_ref[:, pl.ds(HALF + 64, HALF)] = dot(ones, xr_ref[0], NT) * (1.0 / SEQ)


def norm_patches(idx, own, other, sample):
    sample_spec = pl.BlockSpec((1, HALF, SEQ), lambda i: (sample, 0, 0))
    return pl.pallas_call(
        norm_kernel,
        grid=(1,),
        out_shape=(shape((ROWS, D), bf16), shape((8, 1280), f32)),
        in_specs=[pl.BlockSpec((1, D), lambda i: (0, 0)), sample_spec, sample_spec],
        out_specs=(pl.BlockSpec((ROWS, D), lambda i: (0, 0)), pl.BlockSpec((8, 1280), lambda i: (0, 0))),
        scratch_shapes=[pltpu.VMEM((D, ROWS), bf16), pltpu.VMEM((ROWS, D), bf16)],
        compiler_params=pltpu.CompilerParams(vmem_limit_bytes=VMEM_LIMIT),
        cost_estimate=pl.CostEstimate(flops=2 * ROWS * D * D, bytes_accessed=4 * ROWS * D, transcendentals=0),
        name="norm_patches",
    )(idx, own, other)


def stack_kernel(*refs):
    pieces, outs = refs[:-2], refs[-2:]
    for half, out in enumerate(outs):
        rows = []
        for piece in pieces:
            count = piece.shape[0] // 2
            rows.append(piece[...].astype(f32)[count * half : count * half + count])
        out[...] = jnp.concatenate(rows, axis=0).astype(bf16)


def stack(pieces):
    return call(
        stack_kernel,
        (shape((PIECE, D), bf16), shape((PIECE, D), bf16)),
        pieces,
        bytes_accessed=8 * PIECE * D,
        name="stack",
    )


def order_kernel(idx_ref, *refs):
    pieces, (out_ref, mixed_ref, pick_ref, sems) = refs[:8], refs[8:]
    copies = []
    for n, piece in enumerate(pieces):
        rows = mixed_ref.at[pl.ds(PIECE * n, PIECE), :]
        copies.append(pltpu.make_async_copy(piece.at[:, pl.ds(WO_AT - D, WIN)], rows, sems.at[n]))
    for copy in copies:
        copy.start()
    for copy in copies:
        copy.wait()
    rows = lax.broadcasted_iota(jnp.int32, (D, D), 0)
    pick_ref[...] = (rows == idx_ref[...]).astype(f32).astype(bf16)
    for at in range(0, WIN, 256):
        size = min(256, WIN - at)
        out_ref[:, pl.ds(at, size)] = dot(pick_ref[...], mixed_ref[:, pl.ds(at, size)]).astype(bf16)


def order_out(idx, pieces):
    return call(
        order_kernel,
        shape((D, WIN), bf16),
        [idx] + pieces,
        specs=[VM] + [ANY] * 8,
        scratch=[pltpu.VMEM((D, WIN), bf16), pltpu.VMEM((D, D), bf16), pltpu.SemaphoreType.DMA((8,))],
        flops=2 * D * D * WIN,
        bytes_accessed=4 * D * WIN,
        name="order_out",
    )


def attend_kernel(x_ref, *refs):
    pieces, (att_ref, sum_ref, w_ref, qkv_ref, sems) = refs[:16], refs[16:]
    copies = []
    for n, piece in enumerate(pieces):
        rows = pl.ds(PIECE * (n % 8), PIECE)
        if n < 8:
            copies.append(pltpu.make_async_copy(piece, w_ref.at[rows, pl.ds(0, D)], sems.at[n]))
        else:
            part = piece.at[:, pl.ds(0, QKV - D)]
            copies.append(pltpu.make_async_copy(part, w_ref.at[rows, pl.ds(D, QKV - D)], sems.at[n]))
    for copy in copies:
        copy.start()
    att_ref[...] = jnp.zeros_like(att_ref)
    for copy in copies[:8]:
        copy.wait()

    q_scale = math.log2(math.e) * HEAD_DIM ** (-0.5)

    def project(n, carry):
        at = pl.multiple_of(n * 256, 256)
        lane = at + lax.broadcasted_iota(jnp.int32, (1, 256), 1)
        scale = jnp.where(lane < HALF, q_scale, 1.0).astype(f32)
        qkv_ref[:, pl.ds(at, 256)] = (dot(x_ref[...], w_ref[:, pl.ds(at, 256)]) * scale).astype(bf16)
        return carry

    lax.fori_loop(0, D // 256, project, 0)
    for copy in copies[8:]:
        copy.wait()
    lax.fori_loop(D // 256, QKV // 256, project, 0)

    lane = lax.broadcasted_iota(jnp.int32, (1, 256), 1)

    def between(low, high):
        return ((lane >= low) & (lane < high)).astype(f32)

    last = (lane == 255).astype(f32)
    key_row = lax.broadcasted_iota(jnp.int32, (ROWS, 1), 0)
    key_bias = jnp.where(key_row >= SEQ, -1e30, 0.0).astype(f32) * last

    def pair(p, carry):
        at = pl.multiple_of(p * 128, 128)
        q_at = 16 * p
        v_at = 64 + 16 * p
        k_win = qkv_ref[:, pl.ds(D + at, 256)] * (1.0 - last).astype(bf16) + key_bias.astype(bf16)
        v_win = qkv_ref[:, pl.ds(512 + at, 256)]
        values = []
        for h in range(2):
            low = v_at + HEAD_DIM * h
            ones = (lane == h).astype(f32).astype(bf16)
            values.append(v_win * between(low, low + HEAD_DIM).astype(bf16) + ones)
        units = [(row, h) for row in range(0, QROWS, QBLOCK) for h in range(2)]
        scores, weights, totals = {}, {}, {}

        def score(u):
            row, h = units[u]
            low = q_at + HEAD_DIM * h
            q_win = qkv_ref[pl.ds(row, QBLOCK), pl.ds(at, 256)]
            q = q_win * between(low, low + HEAD_DIM).astype(bf16) + last.astype(bf16)
            scores[u] = dot(q, k_win, NT)

        def weigh(u):
            s = scores.pop(u)
            weights[u] = jnp.exp2((s - jnp.max(s, axis=1, keepdims=True)).astype(bf16))

        def mix(u):
            row, h = units[u]
            totals[u] = dot(weights.pop(u), values[h])

        def store(u):
            row = units[u][0]
            total = totals.pop(u) + totals.pop(u + 1)
            inverse = jnp.where(lane < v_at + HEAD_DIM, 1.0 / total[:, 0:1], 1.0 / total[:, 1:2])
            mixed = (total * inverse * between(v_at, v_at + 2 * HEAD_DIM)).astype(bf16)
            att_ref[pl.ds(row, QBLOCK), pl.ds(at, 256)] = att_ref[pl.ds(row, QBLOCK), pl.ds(at, 256)] + mixed

        score(0)
        for u in range(len(units)):
            if u + 1 < len(units):
                score(u + 1)
            weigh(u)
            mix(u)
            if u % 2 == 1:
                store(u - 1)
        return carry

    lax.fori_loop(0, 4, pair, 0)
    valid = (lax.broadcasted_iota(jnp.int32, (8, QROWS), 1) < SEQ).astype(f32).astype(bf16)
    sum_ref[...] = dot(valid, att_ref[...])


def attend(x, pieces):
    return call(
        attend_kernel,
        (shape((QROWS, WIN), bf16), shape((8, WIN), f32)),
        [x] + pieces,
        specs=[VM] + [ANY] * 16,
        scratch=[
            pltpu.VMEM((D, QKV), bf16),
            pltpu.VMEM((ROWS, QKV), bf16),
            pltpu.SemaphoreType.DMA((16,)),
        ],
        flops=2 * ROWS * D * QKV + 8 * 4 * ROWS * ROWS * 256,
        bytes_accessed=2 * (D * QKV + ROWS * D + QROWS * WIN),
        name="attend",
    )


def project_kernel(m_ref, att_ref, w_ref, x_ref, own_ref, send_ref):
    m = m_ref[0]
    mine = w_ref[pl.ds(pl.multiple_of(m * HALF, HALF), HALF), :]
    theirs = w_ref[pl.ds(pl.multiple_of((1 - m) * HALF, HALF), HALF), :]
    send_ref[...] = dot(theirs, att_ref[...], NT)[:, :SEQ].astype(bf16)
    own_ref[...] = dot(mine, att_ref[...], NT)[:, :SEQ] + x_ref[0].astype(f32)


def project(m, att, w, x, sample):
    full = lambda *dims: pl.BlockSpec(dims, lambda i: (0,) * len(dims))
    return pl.pallas_call(
        project_kernel,
        grid=(1,),
        out_shape=(shape((HALF, SEQ), f32), shape((HALF, SEQ), bf16)),
        in_specs=[SM, full(QROWS, WIN), full(D, WIN), pl.BlockSpec((1, HALF, SEQ), lambda i: (sample, 0, 0))],
        out_specs=(full(HALF, SEQ), full(HALF, SEQ)),
        compiler_params=pltpu.CompilerParams(vmem_limit_bytes=VMEM_LIMIT),
        cost_estimate=pl.CostEstimate(
            flops=2 * D * WIN * QROWS, bytes_accessed=2 * (QROWS * WIN + D * WIN) + 8 * HALF * SEQ, transcendentals=0
        ),
        name="project",
    )(m, att, w, x)


def finish_kernel(own_ref, other_ref, *refs):
    out_ref = refs[-1]
    out_ref[0] = (own_ref[...] + other_ref[...].astype(f32)).astype(bf16)


def finish(own, other, sample, before=None):
    rows = 288
    spec = pl.BlockSpec((rows, SEQ), lambda i: (i, 0))
    args = [own, other] + ([before] if before is not None else [])
    return pl.pallas_call(
        finish_kernel,
        grid=(HALF // rows,),
        out_shape=shape((2, HALF, SEQ), bf16),
        in_specs=[spec, spec] + ([ANY] if before is not None else []),
        out_specs=pl.BlockSpec((1, rows, SEQ), lambda i: (sample, i, 0)),
        input_output_aliases={2: 0} if before is not None else {},
        compiler_params=pltpu.CompilerParams(vmem_limit_bytes=VMEM_LIMIT),
        cost_estimate=pl.CostEstimate(flops=HALF * SEQ, bytes_accessed=8 * HALF * SEQ, transcendentals=0),
        name="finish",
    )(*args)


def text_kernel(m_ref, co_ref, cr_ref, w_ref, wo_ref, part_ref, last_ref, x_ref):
    m = m_ref[0]
    own = co_ref[...].astype(f32)
    other = cr_ref[...].astype(f32)
    first = jnp.where(m == 0, own, other)
    second = jnp.where(m == 0, other, own)
    x_ref[:, pl.ds(0, HALF)] = first
    x_ref[:, pl.ds(HALF, HALF)] = second
    x = x_ref[...]
    center = jnp.sum(x, axis=1, keepdims=True) * (1.0 / D)
    centred = x - center
    spread = jnp.sum(centred * centred, axis=1, keepdims=True) * (1.0 / D)
    normed = (centred * lax.rsqrt(spread + 1e-06)).astype(bf16)
    q = dot(normed, w_ref[0], NT).astype(bf16).astype(f32)
    k = dot(normed, w_ref[1], NT).astype(bf16)
    v = dot(normed, w_ref[2], NT).astype(bf16)
    row = lax.broadcasted_iota(jnp.int32, (16, HALF), 0)
    lane = lax.broadcasted_iota(jnp.int32, (16, HALF), 1)
    low = (row % 8) * HEAD_DIM
    of_head = (lane >= low) & (lane < low + HEAD_DIM)
    q_last = jnp.where(row < 8, q[TEXT - 1 : TEXT], q[2 * TEXT - 1 : 2 * TEXT])
    q_head = jnp.where(of_head, q_last, 0.0).astype(bf16)
    s = dot(q_head, k, NT) * HEAD_DIM ** (-0.5)
    key = lax.broadcasted_iota(jnp.int32, (16, 2 * TEXT), 1)
    of = lax.broadcasted_iota(jnp.int32, (16, 2 * TEXT), 0)
    s = jnp.where((key < TEXT) == (of < 8), s, -1e30)
    e = jnp.exp(s - jnp.max(s, axis=1, keepdims=True))
    weight = (e / jnp.sum(e, axis=1, keepdims=True)).astype(bf16)
    o = jnp.where(of_head, dot(weight, v), 0.0)
    a = jnp.sum(jnp.where(row < 8, o, 0.0), axis=0, keepdims=True)
    b = jnp.sum(jnp.where(row < 8, 0.0, o), axis=0, keepdims=True)
    att = jnp.where(lax.broadcasted_iota(jnp.int32, (8, HALF), 0) == 2, a, b).astype(bf16)
    part_ref[...] = dot(att, wo_ref[...])
    at = lax.broadcasted_iota(jnp.int32, (8, D), 0)
    last_ref[...] = jnp.where(at == 2, x[TEXT - 1 : TEXT], x[2 * TEXT - 1 : 2 * TEXT])


def text_tower(m, own, other, w, wo):
    return call(
        text_kernel,
        (shape((8, D), f32), shape((8, D), f32)),
        [m, own, other, w, wo],
        specs=[SM, VM, VM, VM, VM],
        scratch=[pltpu.VMEM((2 * TEXT, D), f32)],
        flops=0,
        bytes_accessed=0,
        name="text_tower",
    )


def embed_kernel(mine_ref, other_ref, near_ref, far_ref, out_ref):
    for at, features in enumerate((mine_ref[...] + other_ref[...], near_ref[...] + far_ref[...])):
        total = jnp.sum(features * features, axis=1, keepdims=True)
        embedded = (features * lax.rsqrt(total + 1e-06)).astype(bf16)
        for which in range(4):
            out_ref[pl.ds(at, 1), pl.ds(D * which, D)] = embedded[which : which + 1]


def embed(parts):
    return call(embed_kernel, shape((2, MESSAGE), bf16), parts, bytes_accessed=200000, name="embed")


def pool_kernel(m_ref, a_ref, b_ref, ma_ref, mb_ref, w_ref, text_ref, last_ref, part_ref):
    row = lax.broadcasted_iota(jnp.int32, (8, WIN), 0)
    sums = jnp.where(row == 0, a_ref[...], b_ref[...]) * (1.0 / SEQ)
    high = sums.astype(bf16)
    rest = sums - high.astype(f32)
    mid = rest.astype(bf16)
    low = (rest - mid.astype(f32)).astype(bf16)
    w = w_ref[...]
    pooled = dot(high, w, NT) + (dot(mid, w, NT) + dot(low, w, NT))
    m = m_ref[0]
    at = lax.broadcasted_iota(jnp.int32, (8, HALF), 0)
    own = jnp.where(at == 0, ma_ref[:, pl.ds(0, HALF)], mb_ref[:, pl.ds(0, HALF)])
    other = jnp.where(at == 0, ma_ref[:, pl.ds(HALF + 64, HALF)], mb_ref[:, pl.ds(HALF + 64, HALF)])
    first = jnp.where(m == 0, 1.0, 0.0)
    for half, mean in ((0, own), (HALF, other)):
        part = jnp.where(at < 2, pooled[:, half : half + HALF], text_ref[:, pl.ds(half, HALF)])
        part_ref[:, pl.ds(half, HALF)] = part + first * jnp.where(at < 2, mean, last_ref[:, pl.ds(half, HALF)])


def pool(m, sum_a, sum_b, mean_a, mean_b, w, text_part, text_last):
    return call(
        pool_kernel,
        shape((8, D), f32),
        [m, sum_a, sum_b, mean_a, mean_b, w, text_part, text_last],
        specs=[SM] + [VM] * 7,
        flops=3 * 2 * 8 * WIN * D,
        bytes_accessed=2 * D * WIN,
        name="pool",
    )


def pair_kernel(m_ref, own_ref, *refs):
    pieces, (image_ref, text_ref, all_ref) = refs[:8], refs[8:]
    for n, piece in enumerate(pieces):
        all_ref[pl.ds(16 * n, 16), :] = piece[...]
    own = own_ref[...].astype(f32)[0:1]
    row = lax.broadcasted_iota(jnp.int32, (8, D), 0)
    at_row = lax.broadcasted_iota(jnp.int32, (8, 128), 0)
    at_col = lax.broadcasted_iota(jnp.int32, (8, 128), 1)
    for mine, others, out_ref in ((0, 2, image_ref), (2, 0, text_ref)):
        rows = jnp.where(row == 0, own[:, D * mine : D * mine + D], own[:, D * mine + D : D * mine + 2 * D]).astype(bf16)
        grad = None
        for which in range(2):
            each = all_ref[:, pl.ds(D * (others + which), D)]
            logit = 10.0 * dot(rows, each, NT) - 1.0
            label = jnp.where((at_row == which) & (at_col == 0), 1.0, -1.0)
            weight = (-10.0 * label / (1.0 + jnp.exp(label * logit))).astype(bf16)
            term = dot(weight, each)
            grad = term if grad is None else grad + term
        out_ref[...] = jnp.where(m_ref[0] == 0, grad[0:2, 0:HALF], grad[0:2, HALF:])


def pair_grads(m, own, pieces):
    return call(
        pair_kernel,
        (shape((2, HALF), f32), shape((2, HALF), f32)),
        [m, own] + pieces,
        specs=[SM] + [VM] * 9,
        scratch=[pltpu.VMEM((128, MESSAGE), bf16)],
        flops=4 * 2 * 8 * 256 * D,
        bytes_accessed=2 * 128 * MESSAGE,
        name="pair_grads",
    )


def gather_rest(pair, behind, behind_last):
    quad = after(jnp.concatenate([pair, shift(pair, "z", 8, 4)], axis=0), behind)
    along_z = jnp.concatenate([quad] + [shift(quad, "z", 8, k) for k in (1, 2, 7)], axis=0)
    near = [along_z] + [shift(along_z, "x", 4, k) for k in (1, 3, 2)]
    near[3] = after(near[3], behind_last)
    return near + [shift(piece, "c", 2, 1) for piece in near]


def weight_slab(image_qkv, image_out):
    turned = jnp.transpose(image_out)
    return jnp.concatenate(
        [
            jnp.concatenate([image_qkv[:, 0], image_qkv[:, 2]], axis=1),
            jnp.concatenate([image_qkv[:, 1], turned], axis=1),
        ],
        axis=0,
    )


def gather_weights(slab, over_w, behind_pair, behind_quad):
    pair = after(jnp.concatenate([slab[:9], over_w[:9], slab[9:], over_w[9:]], axis=0), behind_pair)
    over_z = shift(pair, "z", 8, 4)
    quad = after(jnp.concatenate([pair[:18], over_z[:18], pair[18:], over_z[18:]], axis=0), behind_quad)
    others = [shift(quad, "z", 8, 1), shift(pair, "z", 8, 2), shift(pair, "z", 8, 6), shift(quad, "z", 8, 7)]
    return stack([quad] + others)


def row_order(z, x, w, c):
    at = np.arange(D)
    r, rest = at % 9, at // 9
    wr, rest = rest % 2, rest // 2
    z4, rest = rest % 2, rest // 2
    zr, rest = np.array(Z_STEPS)[rest % 4] + 4 * z4, rest // 4
    xr, cr = rest % 4, rest // 4
    device = (((z + zr) % 8 * 4 + (x + xr) % 4) * 2 + (w + wr) % 2) * 2 + (c + cr) % 2
    return (device * 9 + r).astype(jnp.int32).reshape(1, D)


def on_device(patches, image_qkv, image_out, captions, text_qkv, text_out):
    z, x, w, c, m = (lax.axis_index(a) for a in ("z", "x", "w", "c", "m"))
    m_arr = jnp.reshape(m, (1,)).astype(jnp.int32)
    order = row_order(z, x, w, c)
    norm_order = (order + HALF * m) % D

    own = jnp.transpose(patches, (0, 2, 1))
    captions2 = captions.reshape(2 * TEXT, HALF)
    captions_other = shift(captions2, "m", 2, 1)
    slab = weight_slab(image_qkv, image_out)
    over_w = shift(slab, "w", 2, 1)
    other = shift(after(own, over_w), "m", 2, 1)
    text_part, text_last = text_tower(
        m_arr, captions2, after(captions_other, over_w), jnp.transpose(text_qkv, (1, 2, 0)), text_out
    )

    qv, ko = gather_weights(slab, over_w, captions_other, text_part)

    next_qv, last_qv = shift(qv, "x", 4, 1), shift(qv, "x", 4, 3)
    next_ko, last_ko = shift(ko, "x", 4, 1), shift(ko, "x", 4, 3)
    normed0, mean0 = norm_patches(norm_order, own, other, 0)
    normed1, mean1 = norm_patches(norm_order, own, other, 1)
    far_qv = shift(last_qv, "x", 4, 3)
    far_ko = shift(next_ko, "x", 4, 1)
    near_qv = [qv, next_qv, far_qv, last_qv]
    near_ko = [ko, next_ko, far_ko, last_ko]
    all_qv = near_qv + [shift(after(block, normed0, normed1), "c", 2, 1) for block in near_qv]
    all_ko = near_ko + [shift(after(block, normed0, normed1), "c", 2, 1) for block in near_ko]
    wo = order_out(order, all_ko)

    att0, sum0 = attend(after(normed0, normed1, wo), all_qv + all_ko)
    own0, send0 = project(m_arr, att0, wo, own, 0)
    got0 = shift(send0, "m", 2, 1)
    att1, sum1 = attend(after(normed1, send0), all_qv + all_ko)
    part = pool(m_arr, sum0, sum1, mean0, mean1, wo, text_part, text_last)
    own1, send1 = project(m_arr, after(att1, part), wo, own, 1)
    parts = [after(part, got0), shift(part, "m", 2, 1), shift(part, "w", 2, 1), shift_wm(part)]
    embedded = embed([after(parts[0], send1)] + parts[1:])
    got1 = shift(after(send1, embedded), "m", 2, 1)
    hidden = finish(own0, after(got0, embedded), 0)
    every = gather_rest(embedded, hidden, got1)

    image_grad, text_grad = pair_grads(m_arr, embedded, every)
    hidden = finish(own1, got1, 1, hidden)
    return jnp.transpose(hidden, (0, 2, 1)), image_grad, text_grad


def solution(mesh):
    split = Mesh(mesh.devices.reshape(8, 4, 2, 2, 2), ("z", "x", "w", "c", "m"))
    batch = ("z", "x", "w", "c")
    return jax.shard_map(
        on_device,
        mesh=split,
        in_specs=(
            P(batch, None, "m"),
            P(batch, None, "m"),
            P("m", batch),
            P(batch, None, "m"),
            P(None, None, "m"),
            P("m", None),
        ),
        out_specs=(P(batch, None, "m"), P(batch, "m"), P(batch, "m")),
        check_vma=False,
    )
```

```python
import functools
import math

import jax
import jax.numpy as jnp
import numpy as np
from jax import lax
from jax.experimental import pallas as pl
from jax.experimental.pallas import tpu as pltpu
from jax.sharding import Mesh, PartitionSpec as P

D = 1152
HALF = 576
HEAD_DIM = 72
SEQ = 729
ROWS = 768
QROWS = 736
QBLOCK = 368
TEXT = 64
COLS = 2304
QKV = 1792
WO_AT = 1664
WIN = 640
PIECE = 144
Z_STEPS = (0, 1, 2, 7)
MESSAGE = 4 * D

f32 = jnp.float32
bf16 = jnp.bfloat16
NT = (((1,), (1,)), ((), ()))
TN = (((0,), (0,)), ((), ()))
VMEM_LIMIT = 24 * 1024 * 1024


def dot(a, b, dims=(((1,), (0,)), ((), ()))):
    return lax.dot_general(a, b, dims, preferred_element_type=f32)


def call(body, outs, args, specs=None, out_specs=None, scratch=(), flops=0, bytes_accessed=0, name=None, limit=VMEM_LIMIT):
    whole = pl.BlockSpec(memory_space=pltpu.VMEM)
    return pl.pallas_call(
        body,
        out_shape=outs,
        in_specs=specs if specs is not None else [whole] * len(args),
        out_specs=out_specs if out_specs is not None else jax.tree.map(lambda _: whole, outs),
        scratch_shapes=list(scratch),
        compiler_params=pltpu.CompilerParams(vmem_limit_bytes=limit),
        cost_estimate=pl.CostEstimate(flops=int(flops), bytes_accessed=int(bytes_accessed), transcendentals=0),
        name=name,
    )(*args)


def shape(dims, kind):
    return jax.ShapeDtypeStruct(dims, kind)


VM = pl.BlockSpec(memory_space=pltpu.VMEM)
SM = pl.BlockSpec(memory_space=pltpu.SMEM)
ANY = pl.BlockSpec(memory_space=pl.ANY)
HBM = pl.BlockSpec(memory_space=pltpu.HBM)


def shift(value, axis, size, step):
    return lax.ppermute(value, axis, [((i + step) % size, i) for i in range(size)])


def shift_wm(value):
    return lax.ppermute(value, ("w", "m"), [(3 - i, i) for i in range(4)])


def after(value, *others):
    return lax.optimization_barrier((value,) + others)[0]


def norm_kernel(idx_ref, xo_ref, xr_ref, out0_ref, out1_ref, mean0_ref, mean1_ref, pad_ref, turned_ref):
    pad_ref[:, pl.ds(640, 128)] = jnp.zeros((D, 128), bf16)
    ones = jnp.ones((8, SEQ), bf16)
    for image, mean_ref in enumerate((mean0_ref, mean1_ref)):
        xo = xo_ref[image].astype(f32)
        xr = xr_ref[image].astype(f32)
        center = (jnp.sum(xo, axis=0, keepdims=True) + jnp.sum(xr, axis=0, keepdims=True)) * (1.0 / D)
        co = xo - center
        cr = xr - center
        spread = (jnp.sum(co * co, axis=0, keepdims=True) + jnp.sum(cr * cr, axis=0, keepdims=True)) * (1.0 / D)
        scale = lax.rsqrt(spread + 1e-06)
        pad_ref[pl.ds(0, HALF), pl.ds(0, SEQ)] = (co * scale).astype(bf16)
        pad_ref[pl.ds(HALF, HALF), pl.ds(0, SEQ)] = (cr * scale).astype(bf16)
        turned_ref[pl.ds(ROWS * image, ROWS), :] = jnp.transpose(pad_ref[...])
        mean_ref[:, pl.ds(0, HALF)] = dot(ones, xo_ref[image], NT) * (1.0 / SEQ)
        mean_ref[:, pl.ds(HALF + 64, HALF)] = dot(ones, xr_ref[image], NT) * (1.0 / SEQ)
    for at in range(0, D, 256):
        size = min(256, D - at)
        rows = lax.broadcasted_iota(jnp.int32, (D, size), 0)
        pick = (rows == idx_ref[:, pl.ds(at, size)]).astype(f32).astype(bf16)
        both = dot(turned_ref[...], pick).astype(bf16)
        out0_ref[:, pl.ds(at, size)] = both[:ROWS]
        out1_ref[:, pl.ds(at, size)] = both[ROWS:]


def norm_patches(idx, own, other):
    return call(
        norm_kernel,
        (shape((ROWS, D), bf16), shape((ROWS, D), bf16), shape((8, 1280), f32), shape((8, 1280), f32)),
        [idx, own, other],
        scratch=[pltpu.VMEM((D, ROWS), bf16), pltpu.VMEM((2 * ROWS, D), bf16)],
        flops=4 * ROWS * D * D,
        bytes_accessed=8 * ROWS * D,
        name="norm_patches",
    )


def stack_kernel(*refs):
    pieces, outs = refs[:-2], refs[-2:]
    for half, out in enumerate(outs):
        rows = []
        for piece in pieces:
            count = piece.shape[0] // 2
            rows.append(piece[...].astype(f32)[count * half : count * half + count])
        out[...] = jnp.concatenate(rows, axis=0).astype(bf16)


def stack(pieces):
    return call(
        stack_kernel,
        (shape((PIECE, D), bf16), shape((PIECE, D), bf16)),
        pieces,
        bytes_accessed=8 * PIECE * D,
        name="stack",
    )


def order_kernel(idx_ref, *refs):
    pieces, (out_ref, mixed_ref, pick_ref, sems) = refs[:8], refs[8:]
    copies = []
    for n, piece in enumerate(pieces):
        rows = mixed_ref.at[pl.ds(PIECE * n, PIECE), :]
        copies.append(pltpu.make_async_copy(piece.at[:, pl.ds(WO_AT - D, WIN)], rows, sems.at[n]))
    for copy in copies:
        copy.start()
    for copy in copies:
        copy.wait()
    rows = lax.broadcasted_iota(jnp.int32, (D, D), 0)
    pick_ref[...] = (rows == idx_ref[...]).astype(f32).astype(bf16)
    for at in range(0, WIN, 256):
        size = min(256, WIN - at)
        out_ref[:, pl.ds(at, size)] = dot(pick_ref[...], mixed_ref[:, pl.ds(at, size)]).astype(bf16)


def order_out(idx, pieces):
    return call(
        order_kernel,
        shape((D, WIN), bf16),
        [idx] + pieces,
        specs=[VM] + [ANY] * 8,
        scratch=[pltpu.VMEM((D, WIN), bf16), pltpu.VMEM((D, D), bf16), pltpu.SemaphoreType.DMA((8,))],
        flops=2 * D * D * WIN,
        bytes_accessed=4 * D * WIN,
        name="order_out",
    )


def attend_kernel(x_ref, *refs):
    pieces, (att_ref, sum_ref, w_ref, qkv_ref, sems) = refs[:16], refs[16:]
    copies = []
    for n, piece in enumerate(pieces):
        rows = pl.ds(PIECE * (n % 8), PIECE)
        if n < 8:
            copies.append(pltpu.make_async_copy(piece, w_ref.at[rows, pl.ds(0, D)], sems.at[n]))
        else:
            part = piece.at[:, pl.ds(0, QKV - D)]
            copies.append(pltpu.make_async_copy(part, w_ref.at[rows, pl.ds(D, QKV - D)], sems.at[n]))
    for copy in copies:
        copy.start()
    att_ref[...] = jnp.zeros_like(att_ref)
    for copy in copies[:8]:
        copy.wait()

    q_scale = math.log2(math.e) * HEAD_DIM ** (-0.5)

    def project(n, carry):
        at = pl.multiple_of(n * 256, 256)
        lane = at + lax.broadcasted_iota(jnp.int32, (1, 256), 1)
        scale = jnp.where(lane < HALF, q_scale, 1.0).astype(f32)
        qkv_ref[:, pl.ds(at, 256)] = (dot(x_ref[...], w_ref[:, pl.ds(at, 256)]) * scale).astype(bf16)
        return carry

    lax.fori_loop(0, D // 256, project, 0)
    for copy in copies[8:]:
        copy.wait()
    lax.fori_loop(D // 256, QKV // 256, project, 0)

    lane = lax.broadcasted_iota(jnp.int32, (1, 256), 1)

    def between(low, high):
        return ((lane >= low) & (lane < high)).astype(f32)

    last = (lane == 255).astype(f32)
    key_row = lax.broadcasted_iota(jnp.int32, (ROWS, 1), 0)
    key_bias = jnp.where(key_row >= SEQ, -1e30, 0.0).astype(f32) * last

    def pair(p, carry):
        at = pl.multiple_of(p * 128, 128)
        q_at = 16 * p
        v_at = 64 + 16 * p
        k_win = qkv_ref[:, pl.ds(D + at, 256)] * (1.0 - last).astype(bf16) + key_bias.astype(bf16)
        v_win = qkv_ref[:, pl.ds(512 + at, 256)]
        values = []
        for h in range(2):
            low = v_at + HEAD_DIM * h
            ones = (lane == h).astype(f32).astype(bf16)
            values.append(v_win * between(low, low + HEAD_DIM).astype(bf16) + ones)
        units = [(row, h) for row in range(0, QROWS, QBLOCK) for h in range(2)]
        scores, weights, totals = {}, {}, {}

        def score(u):
            row, h = units[u]
            low = q_at + HEAD_DIM * h
            q_win = qkv_ref[pl.ds(row, QBLOCK), pl.ds(at, 256)]
            q = q_win * between(low, low + HEAD_DIM).astype(bf16) + last.astype(bf16)
            scores[u] = dot(q, k_win, NT)

        def weigh(u):
            s = scores.pop(u)
            weights[u] = jnp.exp2((s - jnp.max(s, axis=1, keepdims=True)).astype(bf16))

        def mix(u):
            row, h = units[u]
            totals[u] = dot(weights.pop(u), values[h])

        def store(u):
            row = units[u][0]
            total = totals.pop(u) + totals.pop(u + 1)
            inverse = jnp.where(lane < v_at + HEAD_DIM, 1.0 / total[:, 0:1], 1.0 / total[:, 1:2])
            mixed = (total * inverse * between(v_at, v_at + 2 * HEAD_DIM)).astype(bf16)
            att_ref[pl.ds(row, QBLOCK), pl.ds(at, 256)] = att_ref[pl.ds(row, QBLOCK), pl.ds(at, 256)] + mixed

        score(0)
        for u in range(len(units)):
            if u + 1 < len(units):
                score(u + 1)
            weigh(u)
            mix(u)
            if u % 2 == 1:
                store(u - 1)
        return carry

    lax.fori_loop(0, 4, pair, 0)
    valid = (lax.broadcasted_iota(jnp.int32, (8, QROWS), 1) < SEQ).astype(f32).astype(bf16)
    sum_ref[...] = dot(valid, att_ref[...])


def attend(x, pieces):
    return call(
        attend_kernel,
        (shape((QROWS, WIN), bf16), shape((8, WIN), f32)),
        [x] + pieces,
        specs=[VM] + [ANY] * 16,
        scratch=[
            pltpu.VMEM((D, QKV), bf16),
            pltpu.VMEM((ROWS, QKV), bf16),
            pltpu.SemaphoreType.DMA((16,)),
        ],
        flops=2 * ROWS * D * QKV + 8 * 4 * ROWS * ROWS * 256,
        bytes_accessed=2 * (D * QKV + ROWS * D + QROWS * WIN),
        name="attend",
    )


def project_kernel(m_ref, att_ref, w_ref, x_ref, own_ref, send_ref):
    m = m_ref[0]
    mine = w_ref[pl.ds(pl.multiple_of(m * HALF, HALF), HALF), :]
    theirs = w_ref[pl.ds(pl.multiple_of((1 - m) * HALF, HALF), HALF), :]
    send_ref[...] = dot(theirs, att_ref[...], NT)[:, :SEQ].astype(bf16)
    own_ref[...] = dot(mine, att_ref[...], NT)[:, :SEQ] + x_ref[0].astype(f32)


def project(m, att, w, x, sample):
    full = lambda *dims: pl.BlockSpec(dims, lambda i: (0,) * len(dims))
    return pl.pallas_call(
        project_kernel,
        grid=(1,),
        out_shape=(shape((HALF, SEQ), f32), shape((HALF, SEQ), bf16)),
        in_specs=[SM, full(QROWS, WIN), full(D, WIN), pl.BlockSpec((1, HALF, SEQ), lambda i: (sample, 0, 0))],
        out_specs=(full(HALF, SEQ), full(HALF, SEQ)),
        compiler_params=pltpu.CompilerParams(vmem_limit_bytes=VMEM_LIMIT),
        cost_estimate=pl.CostEstimate(
            flops=2 * D * WIN * QROWS, bytes_accessed=2 * (QROWS * WIN + D * WIN) + 8 * HALF * SEQ, transcendentals=0
        ),
        name="project",
    )(m, att, w, x)


def finish_kernel(own_ref, other_ref, *refs):
    out_ref = refs[-1]
    out_ref[0] = (own_ref[...] + other_ref[...].astype(f32)).astype(bf16)


def finish(own, other, sample, before=None):
    rows = 288
    spec = pl.BlockSpec((rows, SEQ), lambda i: (i, 0))
    args = [own, other] + ([before] if before is not None else [])
    return pl.pallas_call(
        finish_kernel,
        grid=(HALF // rows,),
        out_shape=shape((2, HALF, SEQ), bf16),
        in_specs=[spec, spec] + ([ANY] if before is not None else []),
        out_specs=pl.BlockSpec((1, rows, SEQ), lambda i: (sample, i, 0)),
        input_output_aliases={2: 0} if before is not None else {},
        compiler_params=pltpu.CompilerParams(vmem_limit_bytes=VMEM_LIMIT),
        cost_estimate=pl.CostEstimate(flops=HALF * SEQ, bytes_accessed=8 * HALF * SEQ, transcendentals=0),
        name="finish",
    )(*args)


def text_kernel(m_ref, *refs):
    hbm, (part_ref, last_ref, x_ref, co_ref, cr_ref, w_ref, wo_ref, sems) = refs[:4], refs[4:]
    copies = [
        pltpu.make_async_copy(source, ref, sems.at[n])
        for n, (source, ref) in enumerate(zip(hbm, (co_ref, cr_ref, w_ref, wo_ref)))
    ]
    for copy in copies:
        copy.start()
    m = m_ref[0]
    for copy in copies[:2]:
        copy.wait()
    own = co_ref[...].astype(f32)
    other = cr_ref[...].astype(f32)
    first = jnp.where(m == 0, own, other)
    second = jnp.where(m == 0, other, own)
    x_ref[:, pl.ds(0, HALF)] = first
    x_ref[:, pl.ds(HALF, HALF)] = second
    x = x_ref[...]
    center = jnp.sum(x, axis=1, keepdims=True) * (1.0 / D)
    centred = x - center
    spread = jnp.sum(centred * centred, axis=1, keepdims=True) * (1.0 / D)
    normed = (centred * lax.rsqrt(spread + 1e-06)).astype(bf16)
    copies[2].wait()
    q = dot(normed, w_ref[0], NT).astype(bf16).astype(f32)
    k = dot(normed, w_ref[1], NT).astype(bf16)
    v = dot(normed, w_ref[2], NT).astype(bf16)
    row = lax.broadcasted_iota(jnp.int32, (16, HALF), 0)
    lane = lax.broadcasted_iota(jnp.int32, (16, HALF), 1)
    low = (row % 8) * HEAD_DIM
    of_head = (lane >= low) & (lane < low + HEAD_DIM)
    q_last = jnp.where(row < 8, q[TEXT - 1 : TEXT], q[2 * TEXT - 1 : 2 * TEXT])
    q_head = jnp.where(of_head, q_last, 0.0).astype(bf16)
    s = dot(q_head, k, NT) * HEAD_DIM ** (-0.5)
    key = lax.broadcasted_iota(jnp.int32, (16, 2 * TEXT), 1)
    of = lax.broadcasted_iota(jnp.int32, (16, 2 * TEXT), 0)
    s = jnp.where((key < TEXT) == (of < 8), s, -1e30)
    e = jnp.exp(s - jnp.max(s, axis=1, keepdims=True))
    weight = (e / jnp.sum(e, axis=1, keepdims=True)).astype(bf16)
    o = jnp.where(of_head, dot(weight, v), 0.0)
    a = jnp.sum(jnp.where(row < 8, o, 0.0), axis=0, keepdims=True)
    b = jnp.sum(jnp.where(row < 8, 0.0, o), axis=0, keepdims=True)
    att = jnp.where(lax.broadcasted_iota(jnp.int32, (8, HALF), 0) == 2, a, b).astype(bf16)
    copies[3].wait()
    part_ref[...] = dot(att, wo_ref[...])
    at = lax.broadcasted_iota(jnp.int32, (8, D), 0)
    last_ref[...] = jnp.where(at == 2, x[TEXT - 1 : TEXT], x[2 * TEXT - 1 : 2 * TEXT])


def text_tower(m, own, other, w, wo):
    return call(
        text_kernel,
        (shape((8, D), f32), shape((8, D), f32)),
        [m, own, other, w, wo],
        specs=[SM, ANY, ANY, HBM, HBM],
        scratch=[
            pltpu.VMEM((2 * TEXT, D), f32),
            pltpu.VMEM((2 * TEXT, HALF), bf16),
            pltpu.VMEM((2 * TEXT, HALF), bf16),
            pltpu.VMEM((3, HALF, D), bf16),
            pltpu.VMEM((HALF, D), bf16),
            pltpu.SemaphoreType.DMA((4,)),
        ],
        flops=0,
        bytes_accessed=0,
        name="text_tower",
        limit=60 * 1024 * 1024,
    )


def embed_kernel(mine_ref, other_ref, near_ref, far_ref, out_ref):
    for at, features in enumerate((mine_ref[...] + other_ref[...], near_ref[...] + far_ref[...])):
        total = jnp.sum(features * features, axis=1, keepdims=True)
        embedded = (features * lax.rsqrt(total + 1e-06)).astype(bf16)
        for which in range(4):
            out_ref[pl.ds(at, 1), pl.ds(D * which, D)] = embedded[which : which + 1]


def embed(parts):
    return call(embed_kernel, shape((2, MESSAGE), bf16), parts, bytes_accessed=200000, name="embed")


def pool_kernel(m_ref, a_ref, b_ref, ma_ref, mb_ref, w_ref, text_ref, last_ref, part_ref):
    row = lax.broadcasted_iota(jnp.int32, (8, WIN), 0)
    sums = jnp.where(row == 0, a_ref[...], b_ref[...]) * (1.0 / SEQ)
    high = sums.astype(bf16)
    rest = sums - high.astype(f32)
    mid = rest.astype(bf16)
    low = (rest - mid.astype(f32)).astype(bf16)
    w = w_ref[...]
    pooled = dot(high, w, NT) + (dot(mid, w, NT) + dot(low, w, NT))
    m = m_ref[0]
    at = lax.broadcasted_iota(jnp.int32, (8, HALF), 0)
    own = jnp.where(at == 0, ma_ref[:, pl.ds(0, HALF)], mb_ref[:, pl.ds(0, HALF)])
    other = jnp.where(at == 0, ma_ref[:, pl.ds(HALF + 64, HALF)], mb_ref[:, pl.ds(HALF + 64, HALF)])
    first = jnp.where(m == 0, 1.0, 0.0)
    for half, mean in ((0, own), (HALF, other)):
        part = jnp.where(at < 2, pooled[:, half : half + HALF], text_ref[:, pl.ds(half, HALF)])
        part_ref[:, pl.ds(half, HALF)] = part + first * jnp.where(at < 2, mean, last_ref[:, pl.ds(half, HALF)])


def pool(m, sum_a, sum_b, mean_a, mean_b, w, text_part, text_last):
    return call(
        pool_kernel,
        shape((8, D), f32),
        [m, sum_a, sum_b, mean_a, mean_b, w, text_part, text_last],
        specs=[SM] + [VM] * 7,
        flops=3 * 2 * 8 * WIN * D,
        bytes_accessed=2 * D * WIN,
        name="pool",
    )


def pair_kernel(m_ref, own_ref, *refs):
    pieces, (image_ref, text_ref, all_ref) = refs[:8], refs[8:]
    for n, piece in enumerate(pieces):
        all_ref[pl.ds(16 * n, 16), :] = piece[...]
    own = own_ref[...].astype(f32)[0:1]
    row = lax.broadcasted_iota(jnp.int32, (8, D), 0)
    at_row = lax.broadcasted_iota(jnp.int32, (8, 128), 0)
    at_col = lax.broadcasted_iota(jnp.int32, (8, 128), 1)
    for mine, others, out_ref in ((0, 2, image_ref), (2, 0, text_ref)):
        rows = jnp.where(row == 0, own[:, D * mine : D * mine + D], own[:, D * mine + D : D * mine + 2 * D]).astype(bf16)
        grad = None
        for which in range(2):
            each = all_ref[:, pl.ds(D * (others + which), D)]
            logit = 10.0 * dot(rows, each, NT) - 1.0
            label = jnp.where((at_row == which) & (at_col == 0), 1.0, -1.0)
            weight = (-10.0 * label / (1.0 + jnp.exp(label * logit))).astype(bf16)
            term = dot(weight, each)
            grad = term if grad is None else grad + term
        out_ref[...] = jnp.where(m_ref[0] == 0, grad[0:2, 0:HALF], grad[0:2, HALF:])


def pair_grads(m, own, pieces):
    return call(
        pair_kernel,
        (shape((2, HALF), f32), shape((2, HALF), f32)),
        [m, own] + pieces,
        specs=[SM] + [VM] * 9,
        scratch=[pltpu.VMEM((128, MESSAGE), bf16)],
        flops=4 * 2 * 8 * 256 * D,
        bytes_accessed=2 * 128 * MESSAGE,
        name="pair_grads",
    )


def gather_rest(pair, behind, behind_last):
    quad = after(jnp.concatenate([pair, shift(pair, "z", 8, 4)], axis=0), behind)
    along_z = jnp.concatenate([quad] + [shift(quad, "z", 8, k) for k in (1, 2, 7)], axis=0)
    near = [along_z] + [shift(along_z, "x", 4, k) for k in (1, 3, 2)]
    near[3] = after(near[3], behind_last)
    return near + [shift(piece, "c", 2, 1) for piece in near]


def weight_slab(image_qkv, image_out):
    turned = jnp.transpose(image_out)
    return jnp.concatenate(
        [
            jnp.concatenate([image_qkv[:, 0], image_qkv[:, 2]], axis=1),
            jnp.concatenate([image_qkv[:, 1], turned], axis=1),
        ],
        axis=0,
    )


def gather_weights(slab, over_w, behind_pair, behind_quad):
    pair = after(jnp.concatenate([slab[:9], over_w[:9], slab[9:], over_w[9:]], axis=0), behind_pair)
    over_z = shift(pair, "z", 8, 4)
    quad = after(jnp.concatenate([pair[:18], over_z[:18], pair[18:], over_z[18:]], axis=0), behind_quad)
    others = [shift(quad, "z", 8, 1), shift(pair, "z", 8, 2), shift(pair, "z", 8, 6), shift(quad, "z", 8, 7)]
    return stack([quad] + others)


def row_order(z, x, w, c):
    at = np.arange(D)
    r, rest = at % 9, at // 9
    wr, rest = rest % 2, rest // 2
    z4, rest = rest % 2, rest // 2
    zr, rest = np.array(Z_STEPS)[rest % 4] + 4 * z4, rest // 4
    xr, cr = rest % 4, rest // 4
    device = (((z + zr) % 8 * 4 + (x + xr) % 4) * 2 + (w + wr) % 2) * 2 + (c + cr) % 2
    return (device * 9 + r).astype(jnp.int32).reshape(1, D)


def on_device(patches, image_qkv, image_out, captions, text_qkv, text_out):
    z, x, w, c, m = (lax.axis_index(a) for a in ("z", "x", "w", "c", "m"))
    m_arr = jnp.reshape(m, (1,)).astype(jnp.int32)
    order = row_order(z, x, w, c)
    norm_order = (order + HALF * m) % D

    own = jnp.transpose(patches, (0, 2, 1))
    captions2 = captions.reshape(2 * TEXT, HALF)
    captions_other = shift(captions2, "m", 2, 1)
    slab = weight_slab(image_qkv, image_out)
    over_w = shift(slab, "w", 2, 1)
    other = shift(after(own, over_w), "m", 2, 1)
    text_part, text_last = text_tower(
        m_arr, captions2, after(captions_other, over_w), jnp.transpose(text_qkv, (1, 2, 0)), text_out
    )

    qv, ko = gather_weights(slab, over_w, captions_other, text_part)

    next_qv, last_qv = shift(qv, "x", 4, 1), shift(qv, "x", 4, 3)
    next_ko, last_ko = shift(ko, "x", 4, 1), shift(ko, "x", 4, 3)
    normed0, normed1, mean0, mean1 = norm_patches(norm_order, own, other)
    far_qv = shift(last_qv, "x", 4, 3)
    far_ko = shift(next_ko, "x", 4, 1)
    near_qv = [qv, next_qv, far_qv, last_qv]
    near_ko = [ko, next_ko, far_ko, last_ko]
    all_qv = near_qv + [shift(after(block, normed0, normed1), "c", 2, 1) for block in near_qv]
    all_ko = near_ko + [shift(after(block, normed0, normed1), "c", 2, 1) for block in near_ko]
    wo = order_out(order, all_ko)

    att0, sum0 = attend(after(normed0, normed1, wo), all_qv + all_ko)
    own0, send0 = project(m_arr, att0, wo, own, 0)
    got0 = shift(send0, "m", 2, 1)
    att1, sum1 = attend(after(normed1, send0), all_qv + all_ko)
    part = pool(m_arr, sum0, sum1, mean0, mean1, wo, text_part, text_last)
    own1, send1 = project(m_arr, after(att1, part), wo, own, 1)
    parts = [after(part, got0), shift(part, "m", 2, 1), shift(part, "w", 2, 1), shift_wm(part)]
    embedded = embed([after(parts[0], send1)] + parts[1:])
    got1 = shift(after(send1, embedded), "m", 2, 1)
    hidden = finish(own0, after(got0, embedded), 0)
    every = gather_rest(embedded, hidden, got1)

    image_grad, text_grad = pair_grads(m_arr, embedded, every)
    hidden = finish(own1, got1, 1, hidden)
    return jnp.transpose(hidden, (0, 2, 1)), image_grad, text_grad


def solution(mesh):
    split = Mesh(mesh.devices.reshape(8, 4, 2, 2, 2), ("z", "x", "w", "c", "m"))
    batch = ("z", "x", "w", "c")
    return jax.shard_map(
        on_device,
        mesh=split,
        in_specs=(
            P(batch, None, "m"),
            P(batch, None, "m"),
            P("m", batch),
            P(batch, None, "m"),
            P(None, None, "m"),
            P("m", None),
        ),
        out_specs=(P(batch, None, "m"), P(batch, "m"), P(batch, "m")),
        check_vma=False,
    )
```

```python
import functools
import math

import jax
import jax.numpy as jnp
import numpy as np
from jax import lax
from jax.experimental import pallas as pl
from jax.experimental.pallas import tpu as pltpu
from jax.sharding import Mesh, PartitionSpec as P

D = 1152
HALF = 576
HEAD_DIM = 72
SEQ = 729
ROWS = 768
QROWS = 736
QBLOCK = 368
TEXT = 64
COLS = 2304
QKV = 1792
WO_AT = 1664
WIN = 640
PIECE = 144
Z_STEPS = (0, 1, 2, 7)
MESSAGE = 4 * D

f32 = jnp.float32
bf16 = jnp.bfloat16
NT = (((1,), (1,)), ((), ()))
TN = (((0,), (0,)), ((), ()))
VMEM_LIMIT = 24 * 1024 * 1024


def dot(a, b, dims=(((1,), (0,)), ((), ()))):
    return lax.dot_general(a, b, dims, preferred_element_type=f32)


def call(body, outs, args, specs=None, out_specs=None, scratch=(), flops=0, bytes_accessed=0, name=None):
    whole = pl.BlockSpec(memory_space=pltpu.VMEM)
    return pl.pallas_call(
        body,
        out_shape=outs,
        in_specs=specs if specs is not None else [whole] * len(args),
        out_specs=out_specs if out_specs is not None else jax.tree.map(lambda _: whole, outs),
        scratch_shapes=list(scratch),
        compiler_params=pltpu.CompilerParams(vmem_limit_bytes=VMEM_LIMIT),
        cost_estimate=pl.CostEstimate(flops=int(flops), bytes_accessed=int(bytes_accessed), transcendentals=0),
        name=name,
    )(*args)


def shape(dims, kind):
    return jax.ShapeDtypeStruct(dims, kind)


VM = pl.BlockSpec(memory_space=pltpu.VMEM)
SM = pl.BlockSpec(memory_space=pltpu.SMEM)
ANY = pl.BlockSpec(memory_space=pl.ANY)


def shift(value, axis, size, step):
    return lax.ppermute(value, axis, [((i + step) % size, i) for i in range(size)])


def shift_wm(value):
    return lax.ppermute(value, ("w", "m"), [(3 - i, i) for i in range(4)])


def after(value, *others):
    return lax.optimization_barrier((value,) + others)[0]


def norm_kernel(idx_ref, xo_ref, xr_ref, out0_ref, out1_ref, mean0_ref, mean1_ref, pad_ref, turned_ref):
    pad_ref[:, pl.ds(640, 128)] = jnp.zeros((D, 128), bf16)
    ones = jnp.ones((8, SEQ), bf16)
    for image, mean_ref in enumerate((mean0_ref, mean1_ref)):
        xo = xo_ref[image].astype(f32)
        xr = xr_ref[image].astype(f32)
        center = (jnp.sum(xo, axis=0, keepdims=True) + jnp.sum(xr, axis=0, keepdims=True)) * (1.0 / D)
        co = xo - center
        cr = xr - center
        spread = (jnp.sum(co * co, axis=0, keepdims=True) + jnp.sum(cr * cr, axis=0, keepdims=True)) * (1.0 / D)
        scale = lax.rsqrt(spread + 1e-06)
        pad_ref[pl.ds(0, HALF), pl.ds(0, SEQ)] = (co * scale).astype(bf16)
        pad_ref[pl.ds(HALF, HALF), pl.ds(0, SEQ)] = (cr * scale).astype(bf16)
        turned_ref[pl.ds(ROWS * image, ROWS), :] = jnp.transpose(pad_ref[...])
        mean_ref[:, pl.ds(0, HALF)] = dot(ones, xo_ref[image], NT) * (1.0 / SEQ)
        mean_ref[:, pl.ds(HALF + 64, HALF)] = dot(ones, xr_ref[image], NT) * (1.0 / SEQ)
    for at in range(0, D, 256):
        size = min(256, D - at)
        rows = lax.broadcasted_iota(jnp.int32, (D, size), 0)
        pick = (rows == idx_ref[:, pl.ds(at, size)]).astype(f32).astype(bf16)
        both = dot(turned_ref[...], pick).astype(bf16)
        out0_ref[:, pl.ds(at, size)] = both[:ROWS]
        out1_ref[:, pl.ds(at, size)] = both[ROWS:]


def norm_patches(idx, own, other):
    return call(
        norm_kernel,
        (shape((ROWS, D), bf16), shape((ROWS, D), bf16), shape((8, 1280), f32), shape((8, 1280), f32)),
        [idx, own, other],
        scratch=[pltpu.VMEM((D, ROWS), bf16), pltpu.VMEM((2 * ROWS, D), bf16)],
        flops=4 * ROWS * D * D,
        bytes_accessed=8 * ROWS * D,
        name="norm_patches",
    )


def stack_kernel(*refs):
    pieces, outs = refs[:-2], refs[-2:]
    for half, out in enumerate(outs):
        rows = []
        for piece in pieces:
            count = piece.shape[0] // 2
            rows.append(piece[...].astype(f32)[count * half : count * half + count])
        out[...] = jnp.concatenate(rows, axis=0).astype(bf16)


def stack(pieces):
    return call(
        stack_kernel,
        (shape((PIECE, D), bf16), shape((PIECE, D), bf16)),
        pieces,
        bytes_accessed=8 * PIECE * D,
        name="stack",
    )


def order_kernel(idx_ref, *refs):
    pieces, (out_ref, mixed_ref, pick_ref, sems) = refs[:8], refs[8:]
    copies = []
    for n, piece in enumerate(pieces):
        rows = mixed_ref.at[pl.ds(PIECE * n, PIECE), :]
        copies.append(pltpu.make_async_copy(piece.at[:, pl.ds(WO_AT - D, WIN)], rows, sems.at[n]))
    for copy in copies:
        copy.start()
    for copy in copies:
        copy.wait()
    rows = lax.broadcasted_iota(jnp.int32, (D, D), 0)
    pick_ref[...] = (rows == idx_ref[...]).astype(f32).astype(bf16)
    for at in range(0, WIN, 256):
        size = min(256, WIN - at)
        out_ref[:, pl.ds(at, size)] = dot(pick_ref[...], mixed_ref[:, pl.ds(at, size)]).astype(bf16)


def order_out(idx, pieces):
    return call(
        order_kernel,
        shape((D, WIN), bf16),
        [idx] + pieces,
        specs=[VM] + [ANY] * 8,
        scratch=[pltpu.VMEM((D, WIN), bf16), pltpu.VMEM((D, D), bf16), pltpu.SemaphoreType.DMA((8,))],
        flops=2 * D * D * WIN,
        bytes_accessed=4 * D * WIN,
        name="order_out",
    )


def attend_kernel(x_ref, *refs):
    pieces, (att_ref, sum_ref, w_ref, qkv_ref, sems) = refs[:16], refs[16:]
    copies = []
    for n, piece in enumerate(pieces):
        rows = pl.ds(PIECE * (n % 8), PIECE)
        if n < 8:
            copies.append(pltpu.make_async_copy(piece, w_ref.at[rows, pl.ds(0, D)], sems.at[n]))
        else:
            part = piece.at[:, pl.ds(0, QKV - D)]
            copies.append(pltpu.make_async_copy(part, w_ref.at[rows, pl.ds(D, QKV - D)], sems.at[n]))
    for copy in copies:
        copy.start()
    att_ref[...] = jnp.zeros_like(att_ref)
    for copy in copies[:8]:
        copy.wait()

    q_scale = math.log2(math.e) * HEAD_DIM ** (-0.5)

    def project(n, carry):
        at = pl.multiple_of(n * 256, 256)
        lane = at + lax.broadcasted_iota(jnp.int32, (1, 256), 1)
        scale = jnp.where(lane < HALF, q_scale, 1.0).astype(f32)
        qkv_ref[:, pl.ds(at, 256)] = (dot(x_ref[...], w_ref[:, pl.ds(at, 256)]) * scale).astype(bf16)
        return carry

    lax.fori_loop(0, D // 256, project, 0)
    for copy in copies[8:]:
        copy.wait()
    lax.fori_loop(D // 256, QKV // 256, project, 0)

    lane = lax.broadcasted_iota(jnp.int32, (1, 256), 1)

    def between(low, high):
        return ((lane >= low) & (lane < high)).astype(f32)

    last = (lane == 255).astype(f32)
    key_row = lax.broadcasted_iota(jnp.int32, (ROWS, 1), 0)
    key_bias = jnp.where(key_row >= SEQ, -1e30, 0.0).astype(f32) * last

    def pair(p, carry):
        at = pl.multiple_of(p * 128, 128)
        q_at = 16 * p
        v_at = 64 + 16 * p
        k_win = qkv_ref[:, pl.ds(D + at, 256)] * (1.0 - last).astype(bf16) + key_bias.astype(bf16)
        v_win = qkv_ref[:, pl.ds(512 + at, 256)]
        values = []
        for h in range(2):
            low = v_at + HEAD_DIM * h
            ones = (lane == h).astype(f32).astype(bf16)
            values.append(v_win * between(low, low + HEAD_DIM).astype(bf16) + ones)
        units = [(row, h) for row in range(0, QROWS, QBLOCK) for h in range(2)]
        scores, weights, totals = {}, {}, {}

        def score(u):
            row, h = units[u]
            low = q_at + HEAD_DIM * h
            q_win = qkv_ref[pl.ds(row, QBLOCK), pl.ds(at, 256)]
            q = q_win * between(low, low + HEAD_DIM).astype(bf16) + last.astype(bf16)
            scores[u] = dot(q, k_win, NT)

        def weigh(u):
            s = scores.pop(u)
            weights[u] = jnp.exp2((s - jnp.max(s, axis=1, keepdims=True)).astype(bf16))

        def mix(u):
            row, h = units[u]
            totals[u] = dot(weights.pop(u), values[h])

        def store(u):
            row = units[u][0]
            total = totals.pop(u) + totals.pop(u + 1)
            inverse = jnp.where(lane < v_at + HEAD_DIM, 1.0 / total[:, 0:1], 1.0 / total[:, 1:2])
            mixed = (total * inverse * between(v_at, v_at + 2 * HEAD_DIM)).astype(bf16)
            att_ref[pl.ds(row, QBLOCK), pl.ds(at, 256)] = att_ref[pl.ds(row, QBLOCK), pl.ds(at, 256)] + mixed

        score(0)
        for u in range(len(units)):
            if u + 1 < len(units):
                score(u + 1)
            weigh(u)
            mix(u)
            if u % 2 == 1:
                store(u - 1)
        return carry

    lax.fori_loop(0, 4, pair, 0)
    valid = (lax.broadcasted_iota(jnp.int32, (8, QROWS), 1) < SEQ).astype(f32).astype(bf16)
    sum_ref[...] = dot(valid, att_ref[...])


def attend(x, pieces):
    return call(
        attend_kernel,
        (shape((QROWS, WIN), bf16), shape((8, WIN), f32)),
        [x] + pieces,
        specs=[VM] + [ANY] * 16,
        scratch=[
            pltpu.VMEM((D, QKV), bf16),
            pltpu.VMEM((ROWS, QKV), bf16),
            pltpu.SemaphoreType.DMA((16,)),
        ],
        flops=2 * ROWS * D * QKV + 8 * 4 * ROWS * ROWS * 256,
        bytes_accessed=2 * (D * QKV + ROWS * D + QROWS * WIN),
        name="attend",
    )


def project_kernel(m_ref, att_ref, w_ref, x_ref, own_ref, send_ref):
    m = m_ref[0]
    mine = w_ref[pl.ds(pl.multiple_of(m * HALF, HALF), HALF), :]
    theirs = w_ref[pl.ds(pl.multiple_of((1 - m) * HALF, HALF), HALF), :]
    send_ref[...] = dot(theirs, att_ref[...], NT)[:, :SEQ].astype(bf16)
    own_ref[...] = dot(mine, att_ref[...], NT)[:, :SEQ] + x_ref[0].astype(f32)


def project(m, att, w, x, sample):
    full = lambda *dims: pl.BlockSpec(dims, lambda i: (0,) * len(dims))
    return pl.pallas_call(
        project_kernel,
        grid=(1,),
        out_shape=(shape((HALF, SEQ), f32), shape((HALF, SEQ), bf16)),
        in_specs=[SM, full(QROWS, WIN), full(D, WIN), pl.BlockSpec((1, HALF, SEQ), lambda i: (sample, 0, 0))],
        out_specs=(full(HALF, SEQ), full(HALF, SEQ)),
        compiler_params=pltpu.CompilerParams(vmem_limit_bytes=VMEM_LIMIT),
        cost_estimate=pl.CostEstimate(
            flops=2 * D * WIN * QROWS, bytes_accessed=2 * (QROWS * WIN + D * WIN) + 8 * HALF * SEQ, transcendentals=0
        ),
        name="project",
    )(m, att, w, x)


def finish_kernel(own_ref, other_ref, *refs):
    out_ref = refs[-1]
    out_ref[0] = (own_ref[...] + other_ref[...].astype(f32)).astype(bf16)


def finish(own, other, sample, before=None):
    rows = 288
    spec = pl.BlockSpec((rows, SEQ), lambda i: (i, 0))
    args = [own, other] + ([before] if before is not None else [])
    return pl.pallas_call(
        finish_kernel,
        grid=(HALF // rows,),
        out_shape=shape((2, HALF, SEQ), bf16),
        in_specs=[spec, spec] + ([ANY] if before is not None else []),
        out_specs=pl.BlockSpec((1, rows, SEQ), lambda i: (sample, i, 0)),
        input_output_aliases={2: 0} if before is not None else {},
        compiler_params=pltpu.CompilerParams(vmem_limit_bytes=VMEM_LIMIT),
        cost_estimate=pl.CostEstimate(flops=HALF * SEQ, bytes_accessed=8 * HALF * SEQ, transcendentals=0),
        name="finish",
    )(*args)


def text_kernel(m_ref, co_ref, cr_ref, w_ref, wo_ref, part_ref, last_ref, x_ref):
    m = m_ref[0]
    own = co_ref[...].astype(f32)
    other = cr_ref[...].astype(f32)
    first = jnp.where(m == 0, own, other)
    second = jnp.where(m == 0, other, own)
    x_ref[:, pl.ds(0, HALF)] = first
    x_ref[:, pl.ds(HALF, HALF)] = second
    x = x_ref[...]
    center = jnp.sum(x, axis=1, keepdims=True) * (1.0 / D)
    centred = x - center
    spread = jnp.sum(centred * centred, axis=1, keepdims=True) * (1.0 / D)
    normed = (centred * lax.rsqrt(spread + 1e-06)).astype(bf16)
    q = dot(normed, w_ref[0], NT).astype(bf16).astype(f32)
    k = dot(normed, w_ref[1], NT).astype(bf16)
    v = dot(normed, w_ref[2], NT).astype(bf16)
    row = lax.broadcasted_iota(jnp.int32, (16, HALF), 0)
    lane = lax.broadcasted_iota(jnp.int32, (16, HALF), 1)
    low = (row % 8) * HEAD_DIM
    of_head = (lane >= low) & (lane < low + HEAD_DIM)
    q_last = jnp.where(row < 8, q[TEXT - 1 : TEXT], q[2 * TEXT - 1 : 2 * TEXT])
    q_head = jnp.where(of_head, q_last, 0.0).astype(bf16)
    s = dot(q_head, k, NT) * HEAD_DIM ** (-0.5)
    key = lax.broadcasted_iota(jnp.int32, (16, 2 * TEXT), 1)
    of = lax.broadcasted_iota(jnp.int32, (16, 2 * TEXT), 0)
    s = jnp.where((key < TEXT) == (of < 8), s, -1e30)
    e = jnp.exp(s - jnp.max(s, axis=1, keepdims=True))
    weight = (e / jnp.sum(e, axis=1, keepdims=True)).astype(bf16)
    o = jnp.where(of_head, dot(weight, v), 0.0)
    a = jnp.sum(jnp.where(row < 8, o, 0.0), axis=0, keepdims=True)
    b = jnp.sum(jnp.where(row < 8, 0.0, o), axis=0, keepdims=True)
    att = jnp.where(lax.broadcasted_iota(jnp.int32, (8, HALF), 0) == 2, a, b).astype(bf16)
    part_ref[...] = dot(att, wo_ref[...])
    at = lax.broadcasted_iota(jnp.int32, (8, D), 0)
    last_ref[...] = jnp.where(at == 2, x[TEXT - 1 : TEXT], x[2 * TEXT - 1 : 2 * TEXT])


def text_tower(m, own, other, w, wo):
    return call(
        text_kernel,
        (shape((8, D), f32), shape((8, D), f32)),
        [m, own, other, w, wo],
        specs=[SM, VM, VM, VM, VM],
        scratch=[pltpu.VMEM((2 * TEXT, D), f32)],
        flops=0,
        bytes_accessed=0,
        name="text_tower",
    )


def embed_kernel(mine_ref, other_ref, near_ref, far_ref, out_ref):
    for at, features in enumerate((mine_ref[...] + other_ref[...], near_ref[...] + far_ref[...])):
        total = jnp.sum(features * features, axis=1, keepdims=True)
        embedded = (features * lax.rsqrt(total + 1e-06)).astype(bf16)
        for which in range(4):
            out_ref[pl.ds(at, 1), pl.ds(D * which, D)] = embedded[which : which + 1]


def embed(parts):
    return call(embed_kernel, shape((2, MESSAGE), bf16), parts, bytes_accessed=200000, name="embed")


def pool_kernel(m_ref, a_ref, b_ref, ma_ref, mb_ref, w_ref, text_ref, last_ref, part_ref):
    row = lax.broadcasted_iota(jnp.int32, (8, WIN), 0)
    sums = jnp.where(row == 0, a_ref[...], b_ref[...]) * (1.0 / SEQ)
    high = sums.astype(bf16)
    rest = sums - high.astype(f32)
    mid = rest.astype(bf16)
    low = (rest - mid.astype(f32)).astype(bf16)
    w = w_ref[...]
    pooled = dot(high, w, NT) + (dot(mid, w, NT) + dot(low, w, NT))
    m = m_ref[0]
    at = lax.broadcasted_iota(jnp.int32, (8, HALF), 0)
    own = jnp.where(at == 0, ma_ref[:, pl.ds(0, HALF)], mb_ref[:, pl.ds(0, HALF)])
    other = jnp.where(at == 0, ma_ref[:, pl.ds(HALF + 64, HALF)], mb_ref[:, pl.ds(HALF + 64, HALF)])
    first = jnp.where(m == 0, 1.0, 0.0)
    for half, mean in ((0, own), (HALF, other)):
        part = jnp.where(at < 2, pooled[:, half : half + HALF], text_ref[:, pl.ds(half, HALF)])
        part_ref[:, pl.ds(half, HALF)] = part + first * jnp.where(at < 2, mean, last_ref[:, pl.ds(half, HALF)])


def pool(m, sum_a, sum_b, mean_a, mean_b, w, text_part, text_last):
    return call(
        pool_kernel,
        shape((8, D), f32),
        [m, sum_a, sum_b, mean_a, mean_b, w, text_part, text_last],
        specs=[SM] + [VM] * 7,
        flops=3 * 2 * 8 * WIN * D,
        bytes_accessed=2 * D * WIN,
        name="pool",
    )


def pair_kernel(m_ref, own_ref, *refs):
    pieces, (image_ref, text_ref, all_ref) = refs[:8], refs[8:]
    for n, piece in enumerate(pieces):
        all_ref[pl.ds(16 * n, 16), :] = piece[...]
    own = own_ref[...].astype(f32)[0:1]
    row = lax.broadcasted_iota(jnp.int32, (8, D), 0)
    at_row = lax.broadcasted_iota(jnp.int32, (8, 128), 0)
    at_col = lax.broadcasted_iota(jnp.int32, (8, 128), 1)
    for mine, others, out_ref in ((0, 2, image_ref), (2, 0, text_ref)):
        rows = jnp.where(row == 0, own[:, D * mine : D * mine + D], own[:, D * mine + D : D * mine + 2 * D]).astype(bf16)
        grad = None
        for which in range(2):
            each = all_ref[:, pl.ds(D * (others + which), D)]
            logit = 10.0 * dot(rows, each, NT) - 1.0
            label = jnp.where((at_row == which) & (at_col == 0), 1.0, -1.0)
            weight = (-10.0 * label / (1.0 + jnp.exp(label * logit))).astype(bf16)
            term = dot(weight, each)
            grad = term if grad is None else grad + term
        out_ref[...] = jnp.where(m_ref[0] == 0, grad[0:2, 0:HALF], grad[0:2, HALF:])


def pair_grads(m, own, pieces):
    return call(
        pair_kernel,
        (shape((2, HALF), f32), shape((2, HALF), f32)),
        [m, own] + pieces,
        specs=[SM] + [VM] * 9,
        scratch=[pltpu.VMEM((128, MESSAGE), bf16)],
        flops=4 * 2 * 8 * 256 * D,
        bytes_accessed=2 * 128 * MESSAGE,
        name="pair_grads",
    )


def gather_rest(pair, behind, behind_last):
    quad = after(jnp.concatenate([pair, shift(pair, "z", 8, 4)], axis=0), behind)
    along_z = jnp.concatenate([quad] + [shift(quad, "z", 8, k) for k in (1, 2, 7)], axis=0)
    near = [along_z] + [shift(along_z, "x", 4, k) for k in (1, 3, 2)]
    near[3] = after(near[3], behind_last)
    return near + [shift(piece, "c", 2, 1) for piece in near]


def weight_slab(image_qkv, image_out):
    turned = jnp.transpose(image_out)
    return jnp.concatenate(
        [
            jnp.concatenate([image_qkv[:, 0], image_qkv[:, 2]], axis=1),
            jnp.concatenate([image_qkv[:, 1], turned], axis=1),
        ],
        axis=0,
    )


def gather_weights(slab, over_w, behind_pair, behind_quad):
    pair = after(jnp.concatenate([slab[:9], over_w[:9], slab[9:], over_w[9:]], axis=0), behind_pair)
    over_z = shift(pair, "z", 8, 4)
    quad = after(jnp.concatenate([pair[:18], over_z[:18], pair[18:], over_z[18:]], axis=0), behind_quad)
    others = [shift(quad, "z", 8, 1), shift(pair, "z", 8, 2), shift(pair, "z", 8, 6), shift(quad, "z", 8, 7)]
    return stack([quad] + others)


def row_order(z, x, w, c):
    at = np.arange(D)
    r, rest = at % 9, at // 9
    wr, rest = rest % 2, rest // 2
    z4, rest = rest % 2, rest // 2
    zr, rest = np.array(Z_STEPS)[rest % 4] + 4 * z4, rest // 4
    xr, cr = rest % 4, rest // 4
    device = (((z + zr) % 8 * 4 + (x + xr) % 4) * 2 + (w + wr) % 2) * 2 + (c + cr) % 2
    return (device * 9 + r).astype(jnp.int32).reshape(1, D)


def on_device(patches, image_qkv, image_out, captions, text_qkv, text_out):
    z, x, w, c, m = (lax.axis_index(a) for a in ("z", "x", "w", "c", "m"))
    m_arr = jnp.reshape(m, (1,)).astype(jnp.int32)
    order = row_order(z, x, w, c)
    norm_order = (order + HALF * m) % D

    own = jnp.transpose(patches, (0, 2, 1))
    captions2 = captions.reshape(2 * TEXT, HALF)
    captions_other = shift(captions2, "m", 2, 1)
    slab = weight_slab(image_qkv, image_out)
    over_w = shift(slab, "w", 2, 1)
    other = shift(after(own, over_w), "m", 2, 1)
    text_part, text_last = text_tower(
        m_arr, captions2, after(captions_other, over_w), jnp.transpose(text_qkv, (1, 2, 0)), text_out
    )

    qv, ko = gather_weights(slab, over_w, captions_other, text_part)

    next_qv, last_qv = shift(qv, "x", 4, 1), shift(qv, "x", 4, 3)
    next_ko, last_ko = shift(ko, "x", 4, 1), shift(ko, "x", 4, 3)
    normed0, normed1, mean0, mean1 = norm_patches(norm_order, own, other)
    far_qv = shift(last_qv, "x", 4, 3)
    far_ko = shift(next_ko, "x", 4, 1)
    near_qv = [qv, next_qv, far_qv, last_qv]
    near_ko = [ko, next_ko, far_ko, last_ko]
    all_qv = near_qv + [shift(after(block, normed0, normed1), "c", 2, 1) for block in near_qv]
    all_ko = near_ko + [shift(after(block, normed0, normed1), "c", 2, 1) for block in near_ko]
    wo = order_out(order, all_ko)

    att0, sum0 = attend(after(normed0, normed1, wo), all_qv + all_ko)
    own0, send0 = project(m_arr, att0, wo, own, 0)
    got0 = shift(send0, "m", 2, 1)
    att1, sum1 = attend(after(normed1, send0), all_qv + all_ko)
    part = pool(m_arr, sum0, sum1, mean0, mean1, wo, text_part, text_last)
    own1, send1 = project(m_arr, after(att1, part), wo, own, 1)
    parts = [after(part, got0), shift(part, "m", 2, 1), shift(part, "w", 2, 1), shift_wm(part)]
    embedded = embed([after(parts[0], send1)] + parts[1:])
    got1 = shift(after(send1, embedded), "m", 2, 1)
    hidden = finish(own0, after(got0, embedded), 0)
    every = gather_rest(embedded, hidden, got1)

    image_grad, text_grad = pair_grads(m_arr, embedded, every)
    hidden = finish(own1, got1, 1, hidden)
    return jnp.transpose(hidden, (0, 2, 1)), image_grad, text_grad


def solution(mesh):
    split = Mesh(mesh.devices.reshape(8, 4, 2, 2, 2), ("z", "x", "w", "c", "m"))
    batch = ("z", "x", "w", "c")
    return jax.shard_map(
        on_device,
        mesh=split,
        in_specs=(
            P(batch, None, "m"),
            P(batch, None, "m"),
            P("m", batch),
            P(batch, None, "m"),
            P(None, None, "m"),
            P("m", None),
        ),
        out_specs=(P(batch, None, "m"), P(batch, "m"), P(batch, "m")),
        check_vma=False,
    )
```
